1024 devices in a mesh: dom: 256 (over x, z, core), grp: 4 (over y).
Axes of the slice: x: 4, y: 4, z: 32, core: 2. Of those that a mesh axis runs over, the one named last changes fastest.
Arguments:
- residual: float32 [256, 4, 12, 4096], P('dom', None, 'grp'), may hold values from -6 to 6
- orders: int32 [256, 4, 12], P('dom', None, 'grp'), may hold values from 7 to 15
- factors: float32 [256, 4, 12, 4], P('dom', None, 'grp'), may hold values from 0.3 to 3
- widths: int32 [4], replicated, may hold values from 1 to 3, 8 in all
Outputs:
- correction: float32 [256, 4, 12, 4096], P('dom', None, 'grp')
The draws below stay inside these ranges and needn't reach their ends.
Inputs may be any that keep to these rules, and one draw needn't show every extreme that they name: Each strip is 1 to 3 layers wide, the widths sum to 8, and at least one strip, and at most two, is exactly 3 wide.
All inputs are finite; a program needn't handle non-finite values.
Results may differ from the reference program's by a relative error of at most 0.0003.
Values sent between devices are 32-bit elements; how exact they have to be, the bound alone decides.
A program may use at most 64 MiB of HBM per device.

```python
import functools
import math
import jax
import jax.numpy as jnp
import numpy as np
from jax import lax

PTS = 16
NY = 4
ZB = 2
ZMAX = 3
NX = 256
NZ = 8
NZS = 12
N_GRP = 4


def place_ends(entries, own_key, smallest, top_value):
    extent = entries.shape
    place = [jax.random.randint(jax.random.fold_in(own_key, axis), (), 0, extent[axis]) for axis in range(len(extent))]
    entries = entries.at[tuple(place)].set(smallest)
    longest = extent.index(max(extent))
    place[longest] = (place[longest] + 1) % extent[longest]
    return entries.at[tuple(place)].set(top_value)


def level_of(own_key, dims, cuts, smallest, largest):
    gain, own = 1.0, jax.random.fold_in(own_key, 6)
    for position, blocks in cuts:
        heights = jnp.exp(jax.random.uniform(jax.random.fold_in(own, position), (blocks,), jnp.float32, smallest / len(cuts), largest / len(cuts)))
        gain = gain * jnp.repeat(heights, dims[position] // blocks).reshape([-1 if axis == position else 1 for axis in range(len(dims))])
    return gain


def split_up(count, total, limit, slope):
    portions = [(1 << 20) // math.isqrt(grade ** slope) + 1 for grade in range(2, count + 1)]
    rest, given = total - limit - (count - 1), [1] * (count - 1)
    while rest > 0:
        movable = [i for i in range(count - 1) if given[i] < limit]
        pool, budget = sum([portions[i] for i in movable]), rest
        for i in movable:
            addition = min(limit - given[i], max(1, budget * portions[i] // pool), rest)
            given[i] = given[i] + addition
            rest = rest - addition
    return np.array([limit] + given)


def ragged(stream_key, count, total, reach, lean):
    if count == 2:
        one = jax.random.randint(stream_key, (), max(1, total - reach), min(reach, total - 1) + 1)
        return jnp.stack([one, total - one])
    sizes = jnp.asarray(split_up(count, total, reach, lean), jnp.int32)
    pairs = (count - 1) // 2
    source_of, sink = sizes[1:1 + 2 * pairs:2], sizes[2:2 + 2 * pairs:2]
    slack = jnp.minimum(source_of - 1, reach - sink)
    moved = jax.random.randint(jax.random.fold_in(stream_key, 1), (pairs,), 0, 1 << 20) % (slack + 1)
    sizes = sizes.at[1:1 + 2 * pairs:2].set(source_of - moved).at[2:2 + 2 * pairs:2].set(sink + moved)
    return sizes[jax.random.permutation(jax.random.fold_in(stream_key, 2), count)]


def gaussian(rng, dims, width, reach, cuts=(), held_as=jnp.bfloat16):
    gain = level_of(rng, dims, cuts, -0.22, 0.18) if cuts else 1.0
    entries = jax.random.normal(rng, dims, jnp.float32) * width * gain
    return jnp.minimum(jnp.maximum(entries, -reach), reach).astype(held_as)


def setup_inputs(seed: int = 0) -> dict:
    splits = jax.random.split(jax.random.key(seed), 5)
    residual = gaussian(splits[0], (NX, NY, NZS, PTS ** 3), 1.0, 6.0, ((0, 256), (2, 4)), jnp.float32)
    orders = place_ends(jax.random.randint(splits[1], (NX, NY, NZS), 7, 16), jax.random.fold_in(splits[1], 1), 7, 15).astype(jnp.int32)
    factors = jnp.clip(jnp.exp(math.log(3.0) - 2.3025851 * jax.random.uniform(splits[2], (NX, NY, NZS, 4), jnp.float32) ** level_of(splits[2], (NX, NY, NZS, 4), ((0, 256), (2, 4)), -0.2, 0.2)), 0.3, 3.0)
    widths = ragged(splits[3], N_GRP, ZB * N_GRP, ZMAX, 2).astype(jnp.int32)
    return dict(residual=residual, orders=orders, factors=factors, widths=widths)


precise = lax.Precision.HIGHEST
mass_weight = 0.5
penalty = 0.5
cheb_high = 4.0
cheb_low = 0.15


def cheb_nodes(degree):
    return -np.cos(np.pi * np.arange(degree + 1) / degree)


def bary_weights(npoints):
    weights = (-1.0) ** np.arange(npoints)
    weights[0] = 0.5 * weights[0]
    weights[-1] = 0.5 * weights[-1]
    return weights


def lagrange_table(source, target):
    weights = bary_weights(source.shape[0])
    spacing = target[:, None] - source[None, :]
    coincide = np.abs(spacing) < 1e-12
    fractions = weights[None, :] / np.where(coincide, 1.0, spacing)
    lookup = fractions / fractions.sum(axis=1, keepdims=True)
    return np.where(coincide.any(axis=1, keepdims=True), np.where(coincide, 1.0, 0.0), lookup)


def quad_weights(degree):
    weights = np.full(degree + 1, np.pi / degree)
    weights[0] = 0.5 * weights[0]
    weights[-1] = 0.5 * weights[-1]
    return weights


def derivative(degree):
    points = cheb_nodes(degree)
    weights = bary_weights(degree + 1)
    spacing = points[:, None] - points[None, :] + np.eye(degree + 1)
    lookup = (weights[None, :] / weights[:, None]) / spacing
    lookup = lookup * (1.0 - np.eye(degree + 1))
    return lookup - np.eye(degree + 1) * lookup.sum(axis=1)[:, None]


def level_degree(degree, level_index):
    return [degree, degree // 2, 1][level_index]


def level_tables(level_index):
    points = [16, 8, 2][level_index]
    common = cheb_nodes(points - 1)
    common_w = quad_weights(points - 1)
    stiffness, quad_w, last_pick, interpolate, face_diag, living, prolong_pick = [], [], [], [], [], [], []
    for degree in range(7, 16):
        local = level_degree(degree, level_index)
        deriv_mat = derivative(local)
        quad_wts = quad_weights(local)
        stiff_pad = np.zeros((points, points))
        stiff_pad[:local + 1, :local + 1] = deriv_mat.T @ (quad_wts[:, None] * deriv_mat)
        quad_pad = np.zeros(points)
        quad_pad[:local + 1] = quad_wts
        last_vec = np.zeros(points)
        last_vec[local] = 1.0
        interp_pad = np.zeros((points, points))
        interp_pad[:, :local + 1] = lagrange_table(cheb_nodes(local), common)
        stiffness.append(stiff_pad)
        quad_w.append(quad_pad)
        last_pick.append(last_vec)
        interpolate.append(interp_pad)
        face_diag.append((common_w[:, None] * interp_pad ** 2).sum(axis=0))
        living.append(np.where(np.arange(points) <= local, 1.0, 0.0))
        if level_index < 2:
            next_points = [16, 8, 2][level_index + 1]
            coarse = level_degree(degree, level_index + 1)
            prolong_pad = np.zeros((points, next_points))
            prolong_pad[:local + 1, :coarse + 1] = lagrange_table(cheb_nodes(coarse), cheb_nodes(local))
            prolong_pick.append(prolong_pad)
    lookup = {"stiffness": stiffness, "quad_w": quad_w, "last_pick": last_pick, "interpolate": interpolate,
              "face_diag": face_diag, "living": living}
    if level_index < 2:
        lookup["prolong_pick"] = prolong_pick
    lookup = {entry: np.stack(lookup[entry]).astype(np.float32) for entry in lookup}
    factor_tau = penalty * (points - 1) ** 2
    lookup["tau"] = factor_tau
    lookup["pair"] = (factor_tau * np.outer(common_w, common_w)).astype(np.float32)
    first_vec = np.zeros(points)
    first_vec[0] = 1.0
    lookup["first_pick"] = first_vec.astype(np.float32)
    return lookup


def along_i(vector):
    return vector[:, :, None, None]


def along_j(vector):
    return vector[:, None, :, None]


def along_k(vector):
    return vector[:, None, None, :]


def setup_level(lookup, onehot, factors, element_mask):
    def select_rows(entry):
        return jnp.einsum('ec,c...->e...', onehot, jnp.asarray(lookup[entry]), precision=precise)

    names = ["stiffness", "quad_w", "last_pick", "interpolate", "face_diag", "living"]
    if "prolong_pick" in lookup:
        names.append("prolong_pick")
    setup = {entry: select_rows(entry) for entry in names}
    setup["pair"] = jnp.asarray(lookup["pair"])
    setup["first_pick"] = jnp.asarray(lookup["first_pick"])
    setup["factors"] = factors
    quad_w = setup["quad_w"]
    stiff_diag = jnp.diagonal(setup["stiffness"], axis1=1, axis2=2)
    coeff = [factors[:, column, None, None, None] for column in range(4)]
    ends = setup["first_pick"][None, :] + setup["last_pick"]
    face_diag = setup["face_diag"]
    diagonal = (coeff[0] * along_i(stiff_diag) * along_j(quad_w) * along_k(quad_w)
                + coeff[1] * along_i(quad_w) * along_j(stiff_diag) * along_k(quad_w)
                + coeff[2] * along_i(quad_w) * along_j(quad_w) * along_k(stiff_diag)
                + coeff[3] * mass_weight * along_i(quad_w) * along_j(quad_w) * along_k(quad_w)
                + lookup["tau"] * (along_i(ends) * along_j(face_diag) * along_k(face_diag)
                                   + along_i(face_diag) * along_j(ends) * along_k(face_diag)
                                   + along_i(face_diag) * along_j(face_diag) * along_k(ends)))
    living = setup["living"]
    node_live = along_i(living) * along_j(living) * along_k(living) * element_mask[:, None, None, None]
    setup["node_live"] = node_live
    setup["dinv"] = node_live / (diagonal + 1.0 - node_live)
    return setup


def build_levels(orders_flat, factors_flat, element_mask):
    onehot = (orders_flat[:, None] == jnp.arange(7, 16)[None, :]).astype(jnp.float32)
    return [setup_level(level_tables(level_index), onehot, factors_flat, element_mask) for level_index in range(3)]


def volume(values, setup):
    quad_w = setup["quad_w"]
    factors = setup["factors"]
    coeff = [factors[:, column, None, None, None] for column in range(4)]
    along_x = jnp.einsum('eai,eijk->eajk', setup["stiffness"], values, precision=precise)
    along_y = jnp.einsum('eaj,eijk->eiak', setup["stiffness"], values, precision=precise)
    along_z = jnp.einsum('eak,eijk->eija', setup["stiffness"], values, precision=precise)
    return (coeff[0] * along_x * along_j(quad_w) * along_k(quad_w)
            + coeff[1] * along_i(quad_w) * along_y * along_k(quad_w)
            + coeff[2] * along_i(quad_w) * along_j(quad_w) * along_z
            + coeff[3] * mass_weight * along_i(quad_w) * along_j(quad_w) * along_k(quad_w) * values)


def traces(values, setup):
    last_pick = setup["last_pick"]
    interpolate = setup["interpolate"]
    raw_faces = [values[:, 0], jnp.einsum('ei,eijk->ejk', last_pick, values, precision=precise),
                 values[:, :, 0], jnp.einsum('ej,eijk->eik', last_pick, values, precision=precise),
                 values[:, :, :, 0], jnp.einsum('ek,eijk->eij', last_pick, values, precision=precise)]
    common_faces = []
    for face in raw_faces:
        halfway = jnp.einsum('ebj,ejk->ebk', interpolate, face, precision=precise)
        common_faces.append(jnp.einsum('eck,ebk->ebc', interpolate, halfway, precision=precise))
    return common_faces


def face_apply(setup, own_traces, nearby):
    interpolate = setup["interpolate"]
    returned = []
    for own_trace, near_trace in zip(own_traces, nearby):
        jump_term = setup["pair"][None] * (own_trace - near_trace)
        halfway = jnp.einsum('ebc,eck->ebk', jump_term, interpolate, precision=precise)
        returned.append(jnp.einsum('ebj,ebk->ejk', interpolate, halfway, precision=precise))
    first_pick = setup["first_pick"]
    last_pick = setup["last_pick"]
    return (first_pick[None, :, None, None] * returned[0][:, None] + along_i(last_pick) * returned[1][:, None]
            + first_pick[None, None, :, None] * returned[2][:, :, None] + along_j(last_pick) * returned[3][:, :, None]
            + first_pick[None, None, None, :] * returned[4][:, :, :, None] + along_k(last_pick) * returned[5][:, :, :, None])


def smooth(rhs, setup, operate):
    centre = 0.5 * (cheb_high + cheb_low)
    radius = 0.5 * (cheb_high - cheb_low)
    rho_first = radius / centre
    rho_next = 1.0 / (2.0 * centre / radius - rho_first)
    update = setup["dinv"] * rhs / centre
    iterate = update
    remainder = rhs - operate(iterate)
    update = rho_next * rho_first * update + (2.0 * rho_next / radius) * setup["dinv"] * remainder
    return iterate + update


def restrict(pick, values):
    values = jnp.einsum('eia,eijk->eajk', pick, values, precision=precise)
    values = jnp.einsum('ejb,eajk->eabk', pick, values, precision=precise)
    return jnp.einsum('ekc,eabk->eabc', pick, values, precision=precise)


def prolong(pick, values):
    values = jnp.einsum('eia,eabc->eibc', pick, values, precision=precise)
    values = jnp.einsum('ejb,eibc->eijc', pick, values, precision=precise)
    return jnp.einsum('ekc,eijc->eijk', pick, values, precision=precise)


def vcycle(fine_rhs, levels, operate):
    fine_op = functools.partial(operate, 0)
    middle_op = functools.partial(operate, 1)
    coarse_op = functools.partial(operate, 2)
    fine_x = smooth(fine_rhs, levels[0], fine_op)
    middle_rhs = restrict(levels[0]["prolong_pick"], fine_rhs - fine_op(fine_x))
    middle_x = smooth(middle_rhs, levels[1], middle_op)
    coarse_rhs = restrict(levels[1]["prolong_pick"], middle_rhs - middle_op(middle_x))
    coarse_x = smooth(coarse_rhs, levels[2], coarse_op)
    coarse_x = coarse_x + smooth(coarse_rhs - coarse_op(coarse_x), levels[2], coarse_op)
    middle_x = middle_x + prolong(levels[1]["prolong_pick"], coarse_x)
    middle_x = middle_x + smooth(middle_rhs - middle_op(middle_x), levels[1], middle_op)
    fine_x = fine_x + prolong(levels[0]["prolong_pick"], middle_x)
    return fine_x + smooth(fine_rhs - fine_op(fine_x), levels[0], fine_op)


def neighbours(own_traces, grid_shape):
    points = own_traces[0].shape[1]
    grid = [trace.reshape(grid_shape + (points, points)) for trace in own_traces]
    zero_row = jnp.zeros_like(grid[0][:, :1])
    nearby = [jnp.roll(grid[1], 1, axis=0), jnp.roll(grid[0], -1, axis=0),
              jnp.concatenate([zero_row, grid[3][:, :-1]], axis=1),
              jnp.concatenate([grid[2][:, 1:], zero_row], axis=1),
              jnp.roll(grid[5], 1, axis=2), jnp.roll(grid[4], -1, axis=2)]
    return [entry.reshape(-1, points, points) for entry in nearby]


def reference(residual, orders, factors, widths):
    offsets = (jnp.cumsum(widths) - widths).astype(jnp.int32)
    layer_ids = jnp.arange(NZ).astype(jnp.int32)
    owner_group = (jnp.sum((offsets[None, :] <= layer_ids[:, None]).astype(jnp.int32), axis=1) - 1).astype(jnp.int32)
    owner_offset = jnp.sum(jnp.where(jnp.arange(N_GRP)[None, :] == owner_group[:, None], offsets[None, :], 0), axis=1)
    slot_ids = (owner_group * ZMAX + layer_ids - owner_offset).astype(jnp.int32)
    compact_rhs = jnp.take(residual, slot_ids, axis=2)
    compact_orders = jnp.take(orders, slot_ids, axis=2)
    compact_factors = jnp.take(factors, slot_ids, axis=2)
    element_total = NX * NY * NZ
    element_mask = jnp.ones((element_total,), jnp.float32)
    levels = build_levels(compact_orders.reshape(-1), compact_factors.reshape(-1, 4), element_mask)
    grid_shape = (NX, NY, NZ)

    def operate(level_index, values):
        setup = levels[level_index]
        own_traces = traces(values, setup)
        nearby = neighbours(own_traces, grid_shape)
        return volume(values, setup) + face_apply(setup, own_traces, nearby)

    fine_rhs = compact_rhs.reshape(-1, 16, 16, 16) * levels[0]["node_live"]
    result = vcycle(fine_rhs, levels, operate).reshape(NX, NY, NZ, -1)
    slot_all = jnp.arange(NZS).astype(jnp.int32)
    group_of = (slot_all // ZMAX).astype(jnp.int32)
    local_of = (slot_all % ZMAX).astype(jnp.int32)
    width_of = jnp.take(widths, group_of)
    alive = (local_of < width_of).astype(jnp.float32)
    back_ids = jnp.clip(jnp.take(offsets, group_of) + local_of, 0, NZ - 1).astype(jnp.int32)
    return jnp.take(result, back_ids, axis=2) * alive[None, None, :, None]
```

```python
import functools

import jax
import jax.numpy as jnp
import ml_dtypes
import numpy as np
from jax import lax
from jax.experimental import pallas as pl
from jax.experimental.pallas import tpu as pltpu
from jax.sharding import PartitionSpec as P

MESH = pl.DeviceIdType.MESH
SLOTS = 16
mass_weight = 0.5
penalty = 0.5
cheb_high = 4.0
cheb_low = 0.15


def cheb_nodes(degree):
    return -np.cos(np.pi * np.arange(degree + 1) / degree)


def bary_weights(npoints):
    weights = (-1.0) ** np.arange(npoints)
    weights[0] = 0.5 * weights[0]
    weights[-1] = 0.5 * weights[-1]
    return weights


def lagrange_table(source, target):
    weights = bary_weights(source.shape[0])
    spacing = target[:, None] - source[None, :]
    coincide = np.abs(spacing) < 1e-12
    fractions = weights[None, :] / np.where(coincide, 1.0, spacing)
    lookup = fractions / fractions.sum(axis=1, keepdims=True)
    return np.where(coincide.any(axis=1, keepdims=True), np.where(coincide, 1.0, 0.0), lookup)


def quad_weights(degree):
    weights = np.full(degree + 1, np.pi / degree)
    weights[0] = 0.5 * weights[0]
    weights[-1] = 0.5 * weights[-1]
    return weights


def derivative(degree):
    points = cheb_nodes(degree)
    weights = bary_weights(degree + 1)
    spacing = points[:, None] - points[None, :] + np.eye(degree + 1)
    lookup = weights[None, :] / weights[:, None] / spacing
    lookup = lookup * (1.0 - np.eye(degree + 1))
    return lookup - np.eye(degree + 1) * lookup.sum(axis=1)[:, None]


def level_degree(degree, level_index):
    return [degree, degree // 2, 1][level_index]


def split3(table):
    high = table.astype(ml_dtypes.bfloat16)
    rest = table - high.astype(np.float64)
    middle = rest.astype(ml_dtypes.bfloat16)
    low = (rest - middle.astype(np.float64)).astype(ml_dtypes.bfloat16)
    return high, middle, low


def packed(tables):
    rows = np.concatenate([entry.reshape(9, -1) for entry in tables], axis=1).T
    return np.concatenate(list(split3(rows)) + [np.zeros((rows.shape[0], 5), ml_dtypes.bfloat16)], axis=1)


def order_tables(level_index):
    points = [16, 8, 2][level_index]
    common = cheb_nodes(points - 1)
    common_w = quad_weights(points - 1)
    names = ("scaled", "stiff_diag", "quad_w", "interpolate", "face_diag", "living", "prolong")
    table = {name: [] for name in names}
    for degree in range(7, 16):
        local = level_degree(degree, level_index)
        quad = quad_weights(local)
        deriv = derivative(local)
        stiff = deriv.T @ (quad[:, None] * deriv)
        scaled = np.zeros((points, points))
        scaled[: local + 1, : local + 1] = stiff / quad[:, None]
        padded = lambda vector: np.concatenate([vector, np.zeros(points - local - 1)])
        interp = np.zeros((points, points))
        interp[:, : local + 1] = lagrange_table(cheb_nodes(local), common)
        table["scaled"].append(scaled)
        table["stiff_diag"].append(padded(np.diagonal(stiff)))
        table["quad_w"].append(padded(quad))
        table["interpolate"].append(interp)
        table["face_diag"].append((common_w[:, None] * interp**2).sum(axis=0))
        table["living"].append(padded(np.ones(local + 1)))
        if level_index < 2:
            coarse = level_degree(degree, level_index + 1)
            lift = np.zeros((points, [16, 8, 2][level_index + 1]))
            lift[: local + 1, : coarse + 1] = lagrange_table(cheb_nodes(coarse), cheb_nodes(local))
            table["prolong"].append(lift)
    table = {name: np.stack(table[name]) for name in names if table[name]}
    tau = penalty * (points - 1) ** 2
    table["pair"] = tau * np.outer(common_w, common_w)
    table["tau"] = tau
    return table


def flip(table):
    return np.swapaxes(table, 1, 2)


def constants():
    fine, middle, coarse = [order_tables(level_index) for level_index in range(3)]
    vectors = ("quad_w", "face_diag", "living", "stiff_diag")
    matrices = lambda t: [flip(t["scaled"]), t["scaled"], flip(t["interpolate"]), t["interpolate"]]
    c0 = packed(matrices(fine) + [fine[name] for name in vectors])
    c1 = packed(
        matrices(middle)
        + [middle[name] for name in vectors]
        + [fine["prolong"], flip(fine["prolong"]), flip(middle["prolong"])]
    )
    pairs = [np.repeat(t["pair"], SLOTS, axis=1).astype(np.float32) for t in (fine, middle)]
    return c0, c1, pairs[0], pairs[1], (fine["tau"], middle["tau"]), coarse


def split(values):
    high = values.astype(jnp.bfloat16)
    return high, (values - high.astype(jnp.float32)).astype(jnp.bfloat16)


def dot(left, right):
    return jnp.dot(left, right, preferred_element_type=jnp.float32)


def dot3(values, high, low):
    first, second = split(values)
    return dot(first, high[...]) + dot(second, high[...]) + dot(first, low[...])


def roll(values, shift, axis=-1):
    axis = axis % values.ndim
    return pltpu.roll(values, shift % values.shape[axis], axis)


def lanes_iota(lanes):
    return lax.broadcasted_iota(jnp.int32, (1, lanes), 1)


def rows_iota(rows, lanes):
    return lax.broadcasted_iota(jnp.int32, (rows, lanes), 0)


class Level:
    pass


def resolve(table, place):
    own = lax.broadcasted_iota(jnp.int32, table.shape[1:], 0) == place
    return jnp.sum(jnp.where(own[None], table[...], 0.0), axis=1)


def spread(keep, rows, count, target, low=None):
    keep[: rows.shape[0], : rows.shape[1]] = rows
    lanes = rows.shape[1]
    same = rows_iota(SLOTS, lanes) == (lanes_iota(lanes) & (SLOTS - 1))
    for p in range(count):
        block = jnp.where(same, keep[p : p + 1, :lanes], 0.0)
        high = block.astype(jnp.bfloat16)
        target[p * SLOTS : (p + 1) * SLOTS, :] = high
        if low is not None:
            low[p * SLOTS : (p + 1) * SLOTS, :] = (block - high.astype(jnp.float32)).astype(jnp.bfloat16)


def kernel(taus, coarse, *refs):
    names = iter(refs)
    take = lambda count: [next(names) for _ in range(count)]
    widths_ref, orders_ref, factors_ref, c0_ref, c1_ref, pair0_ref, pair1_ref, res_ref = take(8)
    (out_ref,) = take(1)
    levels = []
    for index in range(2):
        lv = Level()
        lv.n = [16, 8][index]
        lv.lanes = lv.n * SLOTS
        (lv.T, lv.TT, lv.TI, lv.TIT) = take(4)
        (lv.RS, lv.RSl, lv.RI, lv.RIl, lv.RIT, lv.RITl, lv.PP, lv.PPT) = take(8)
        (lv.IL, lv.DINV, lv.WWW, lv.R, lv.X, lv.V, lv.OUT) = take(7)
        (lv.H, lv.Q, lv.G, lv.RZ, lv.U, lv.Y, lv.SB, lv.RB) = take(8)
        lv.pair = [pair0_ref, pair1_ref][index]
        levels.append(lv)
    TP, TPT, PT1, RP, RPl, RPT, RPTl, RP1, RP1l, RPT1, RPT1l, A8, C8, SB2, RB2, KEEP, XIN = take(17)
    send_sem, recv_sem = take(2)

    dom, grp = lax.axis_index("dom"), lax.axis_index("grp")
    n_dom, n_grp = lax.axis_size("dom"), lax.axis_size("grp")
    targets = [
        {"dom": lax.rem(dom + n_dom - 1, n_dom)},
        {"dom": lax.rem(dom + 1, n_dom)},
        {"grp": lax.rem(grp + n_grp - 1, n_grp)},
        {"grp": lax.rem(grp + 1, n_grp)},
    ]
    barrier = pltpu.get_barrier_semaphore()
    for target in targets:
        pl.semaphore_signal(barrier, inc=1, device_id=target, device_id_type=MESH)

    lane = lanes_iota(16 * SLOTS)
    slot = lane & (SLOTS - 1)
    layer = slot & 3
    row = slot >> 2
    width = jnp.int32(0)
    for g in range(4):
        width = jnp.where(grp == g, widths_ref[g], width)
    order = jnp.full(lane.shape, 7, jnp.int32)
    factor = [jnp.full(lane.shape, 1.0, jnp.float32) for _ in range(4)]
    for r in range(4):
        for t in range(3):
            here = slot == r * 4 + t
            order = jnp.where(here, orders_ref[0, r, t], order)
            for c in range(4):
                factor[c] = jnp.where(here, factors_ref[0, r, t, c], factor[c])
    alive = layer < width
    mask = jnp.where(alive, 1.0, 0.0)
    at_first = layer == 0
    at_last = layer == width - 1
    line = rows_iota(32, 16 * SLOTS)
    line = jnp.where(line < 9, line, jnp.where(line < 18, line - 9, jnp.where(line < 27, line - 18, -1)))
    onehot = jnp.where(line == order - 7, 1.0, 0.0).astype(jnp.bfloat16)

    for index, lv in enumerate(levels):
        n, lanes = lv.n, lv.lanes
        lv.place = lane[:, :lanes] >> 4
        lv.last = [order, order >> 1][index][:, :lanes]
        lv.f = [entry[:, :lanes] for entry in factor]
        lv.cm = lv.f[3] * mass_weight
        lv.at_first, lv.at_last = at_first[:, :lanes], at_last[:, :lanes]
        lv.row = row[:, :lanes]
        lv.last_range = [range(7, 16), range(3, 8)][index]
        hot = onehot[:, :lanes]
        source = [c0_ref, c1_ref][index]
        at = 0
        for ref in (lv.T, lv.TT, lv.TI, lv.TIT):
            ref[...] = dot(source[at : at + n * n, :], hot).reshape(n, n, lanes)
            at += n * n
        vectors = dot(source[at : at + 4 * n, :], hot)
        at += 4 * n
        quad, face, live, stiff = [vectors[i * n : (i + 1) * n] for i in range(4)]
        if index == 1:
            TP[...] = dot(source[at : at + 128, :], hot).reshape(16, 8, lanes)
            TPT[...] = dot(source[at + 128 : at + 256, :], hot).reshape(8, 16, lanes)
            PT1[...] = dot(source[at + 256 : at + 272, :], hot).reshape(2, 8, lanes)
        spread(KEEP, resolve(lv.T, lv.place) * lv.f[0], n, lv.RS, lv.RSl)
        inter = resolve(lv.TI, lv.place)
        lv.IL[...] = inter
        spread(KEEP, inter, n, lv.RI, lv.RIl)
        spread(KEEP, resolve(lv.TIT, lv.place), n, lv.RIT, lv.RITl)
        points = rows_iota(n, lanes)
        lv.FM = jnp.where(points == 0, 1.0, 0.0)
        lv.LM = jnp.where(points == lv.last, 1.0, 0.0)
        same = rows_iota(SLOTS, lanes) == (lane[:, :lanes] & (SLOTS - 1))
        one = lambda cond: jnp.where(cond, 1.0, 0.0).astype(jnp.bfloat16)
        for p in range(n):
            rows = slice(p * SLOTS, (p + 1) * SLOTS)
            lv.PP[rows, :lanes] = one(same) if p == 0 else jnp.zeros((SLOTS, lanes), jnp.bfloat16)
            lv.PP[rows, lanes:] = one(same & (lv.last == p))
            lv.PPT[rows, :] = one(same & (lv.place == 0))
            lv.PPT[lanes + p * SLOTS : lanes + (p + 1) * SLOTS, :] = one(same & (lv.place == lv.last))
        pick = lambda table: jnp.sum(jnp.where(points == lv.place, table, 0.0), axis=0, keepdims=True)
        w_i, face_i, live_i, stiff_i = pick(quad), pick(face), pick(live) * mask[:, :lanes], pick(stiff)
        ends = lv.FM + lv.LM
        ends_i = pick(ends)
        f0, f1, f2, _ = lv.f
        for j in range(n):
            one_row = lambda table: table[j : j + 1, :]
            w_j, face_j, live_j, stiff_j, ends_j = [one_row(t) for t in (quad, face, live, stiff, ends)]
            www = (w_i * w_j) * quad
            diagonal = (
                (f0 * stiff_i * w_j) * quad
                + (f1 * w_i * stiff_j) * quad
                + (f2 * w_i * w_j) * stiff
                + lv.cm * www
                + taus[index] * ((ends_j * face_i + face_j * ends_i) * face + (face_j * face_i) * ends)
            )
            node_live = (live_j * live_i) * live
            lv.WWW[j] = www
            lv.DINV[j] = node_live / (diagonal + 1.0 - node_live)
            if index == 0:
                lv.X[j] = node_live
        lv.w_lane = w_i

    fine, middle = levels
    spread(KEEP, resolve(TP, middle.place), 16, RP, RPl)
    wide = jnp.concatenate([TPT[...], TPT[...]], axis=2)
    spread(KEEP, resolve(wide, fine.place), 8, RPT, RPTl)
    place1 = middle.place
    spread(KEEP, jnp.where(place1 == 0, PT1[0], jnp.where(place1 == 1, PT1[1], 0.0)), 8, RP1, RP1l)
    RPT1[...] = jnp.zeros(RPT1.shape, jnp.bfloat16)
    RPT1l[...] = jnp.zeros(RPT1l.shape, jnp.bfloat16)
    spread(KEEP, resolve(PT1, place1), 2, RPT1, RPT1l)

    XIN[...] = jnp.zeros(XIN.shape, jnp.float32)
    for i in range(16):
        for r in range(4):
            XIN[i * SLOTS + r * 4 : i * SLOTS + r * 4 + 3, :] = res_ref[0, r, :, i * 256 : (i + 1) * 256]
    fine.R[...] = jnp.transpose(XIN[...]).reshape(16, 16, 256) * fine.X[...]

    pl.semaphore_wait(barrier, 4)
    pending = []

    def send(number, direction, value, source, landing):
        source[...] = value
        where = number * 4 + direction
        copy = pltpu.make_async_remote_copy(
            src_ref=source,
            dst_ref=landing,
            send_sem=send_sem.at[where],
            recv_sem=recv_sem.at[where],
            device_id=targets[direction],
            device_id_type=MESH,
        )
        copy.start()
        pending.append(copy)
        return copy

    def towards_first(value, last):
        value = jnp.where(last, value, 0.0)
        return value + roll(value, -1) + roll(value, -2)

    def towards_last(value):
        return jnp.where(width == 1, value, jnp.where(width == 2, roll(value, 1), roll(value, 2)))

    def contract(table, source, first, count):
        total = None
        for k in range(table.shape[0]):
            term = table[k][None] * source[first : first + count, k : k + 1, :]
            total = term if total is None else total + term
        return total

    def apply_level(lv, slot_of, number, consume):
        n, lanes = lv.n, lv.lanes
        flat = lv.V[...].reshape(n * n, lanes)
        high, low = split(flat)
        lv.U[...] = (dot(high, lv.PP[...]) + dot(low, lv.PP[...])).reshape(n, n, 2 * lanes)
        y0, z0 = lv.V[0], lv.V[:, 0, :]
        y1, z1 = jnp.zeros_like(y0), jnp.zeros_like(z0)
        for p in lv.last_range:
            here = lv.last == p
            y1 = jnp.where(here, lv.V[p], y1)
            z1 = jnp.where(here, lv.V[:, p, :], z1)
        turned = dot3(jnp.concatenate([z0, z1, y0, y1], axis=0), lv.RI, lv.RIl)
        lv.H[2:6] = turned.reshape(4, n, lanes)
        for f in range(2):
            total = None
            for j in range(n):
                term = lv.IL[j : j + 1, :] * lv.U[j, :, f * lanes : (f + 1) * lanes]
                total = term if total is None else total + term
            lv.H[f] = total
        lv.Q[...] = contract(lv.TI, lv.H, 0, 6)
        outgoing = [lv.Q[0], lv.Q[1], lv.Q[2], towards_first(lv.Q[3], lv.at_last)]
        copies = [
            send(number, d, outgoing[d], lv.SB.at[slot_of, d], lv.RB.at[slot_of, d]) for d in range(4)
        ]
        lv.G[4] = lv.pair[...] * (lv.Q[4] - jnp.where(lv.row > 0, roll(lv.Q[5], 4), 0.0))
        lv.G[5] = lv.pair[...] * (lv.Q[5] - jnp.where(lv.row < 3, roll(lv.Q[4], -4), 0.0))
        back = contract(lv.TIT, lv.G, 4, 2).reshape(2 * n, lanes)
        back = dot3(back, lv.RIT, lv.RITl)
        y_back = [back[:n], back[n:]]
        lv.OUT[...] = (
            dot(high, lv.RS[...]) + dot(low, lv.RS[...]) + dot(high, lv.RSl[...])
        ).reshape(n, n, lanes)
        size = 4 if n == 16 else 8
        for a in range(0, n, size):
            block = slice(a, a + size)
            along_j, along_k = None, None
            for j in range(n):
                term = lv.TT[block, j : j + 1, :] * lv.V[j][None]
                along_j = term if along_j is None else along_j + term
            for k in range(n):
                term = lv.T[k][None] * lv.V[block, k : k + 1, :]
                along_k = term if along_k is None else along_k + term
            lv.OUT[block] = lv.WWW[block] * (
                lv.OUT[block] + lv.f[1] * along_j + lv.f[2] * along_k + lv.cm * lv.V[block]
            )
        lv.OUT[0] = lv.OUT[0] + y_back[0]
        for p in lv.last_range:
            lv.OUT[p] = lv.OUT[p] + jnp.where(lv.last == p, y_back[1], 0.0)
        for copy in copies:
            copy.wait_recv()
        pair = lv.pair[...]
        landed = lambda d: lv.RB[slot_of, d]
        lv.G[0] = pair * (lv.Q[0] - landed(1))
        lv.G[1] = pair * (lv.Q[1] - landed(0))
        lv.G[2] = pair * (lv.Q[2] - jnp.where(lv.at_first, landed(3), roll(lv.Q[3], 1)))
        lv.G[3] = pair * (lv.Q[3] - jnp.where(lv.at_last, towards_last(landed(2)), roll(lv.Q[2], -1)))
        back = contract(lv.TIT, lv.G, 0, 4)
        for f in range(2):
            for j in range(n):
                lv.Y[j, :, f * lanes : (f + 1) * lanes] = lv.IL[j : j + 1, :] * back[f]
        lv.RZ[...] = dot3(back[2:4].reshape(2 * n, lanes), lv.RIT, lv.RITl).reshape(2, n, lanes)
        first, second = split(lv.Y[...].reshape(n * n, 2 * lanes))
        x_back = (dot(first, lv.PPT[...]) + dot(second, lv.PPT[...])).reshape(n, n, lanes)
        for j in range(n):
            z_back = lv.FM * lv.RZ[0, j : j + 1, :] + lv.LM * lv.RZ[1, j : j + 1, :]
            consume(j, lv.OUT[j] + x_back[j] + z_back)

    centre = 0.5 * (cheb_high + cheb_low)
    radius = 0.5 * (cheb_high - cheb_low)
    rho_first = radius / centre
    rho_next = 1.0 / (2.0 * centre / radius - rho_first)
    keep_d = 1.0 + rho_next * rho_first
    take_e = 2.0 * rho_next / radius

    def first_step(lv):
        lv.V[...] = lv.DINV[...] * lv.R[...] * (1.0 / centre)

    def end_pre(lv):
        def consume(j, applied):
            lv.V[j] = keep_d * lv.V[j] + take_e * lv.DINV[j] * (lv.R[j] - applied)

        return consume

    def remainder(lv):
        def consume(j, applied):
            lv.OUT[j] = lv.R[j] - applied

        return consume

    def begin_post(lv):
        def consume(j, applied):
            rest = lv.R[j] - applied
            lv.R[j] = rest
            lv.X[j] = lv.V[j]
            lv.V[j] = lv.DINV[j] * rest * (1.0 / centre)

        return consume

    def end_post(lv):
        def consume(j, applied):
            lv.V[j] = lv.X[j] + keep_d * lv.V[j] + take_e * lv.DINV[j] * (lv.R[j] - applied)

        return consume

    first_step(fine)
    apply_level(fine, 0, 0, end_pre(fine))
    apply_level(fine, 1, 1, remainder(fine))

    lanes_down = dot3(fine.OUT[...].reshape(256, 256), RP, RPl).reshape(16, 16, 128)
    total = None
    for j in range(16):
        term = TPT[:, j : j + 1, :] * lanes_down[j][None]
        total = term if total is None else total + term
    A8[...] = total
    middle.R[...] = contract(TP, A8, 0, 8)
    first_step(middle)
    apply_level(middle, 0, 2, end_pre(middle))
    apply_level(middle, 1, 3, remainder(middle))

    parts = []
    for a in range(2):
        total = None
        for j in range(8):
            term = PT1[a, j : j + 1, :] * middle.OUT[j]
            total = term if total is None else total + term
        for b in range(2):
            parts.append(jnp.sum(PT1[b] * total, axis=0, keepdims=True))
    coarse_r = dot3(jnp.concatenate(parts + [jnp.zeros((4, 128), jnp.float32)], axis=0), RP1, RP1l)

    lane1 = lane[:, :128]
    place2 = lane1 >> 4
    line2 = rows_iota(8, 128)
    low_i = place2 == 0
    low_j = line2 < 2
    low_k = (line2 & 1) == 0
    f0, f1, f2, f3 = middle.f
    s00, s01 = float(coarse["scaled"][0, 0, 0]), float(coarse["scaled"][0, 0, 1])
    w0 = float(coarse["quad_w"][0, 0])
    www = w0**3
    pair2 = float(coarse["pair"][0, 0])
    centre_coeff = www * (s00 * (f0 + f1 + f2) + mass_weight * f3) + 3.0 * pair2
    live2 = jnp.where((place2 < 2) & (line2 < 4), mask[:, :128], 0.0)
    dinv2 = live2 / (centre_coeff + 1.0 - live2)
    inside = live2 > 0.0

    def coarse_apply(v, slot_of, number):
        flip_k = jnp.where(low_k, roll(v, -1, 0), roll(v, 1, 0))
        outgoing = [v, v, flip_k, towards_first(flip_k, middle.at_last)]
        copies = [send(number, d, outgoing[d], SB2.at[slot_of, d], RB2.at[slot_of, d]) for d in range(4)]
        flip_i = jnp.where(low_i, roll(v, -16), roll(v, 16))
        flip_j = jnp.where(low_j, roll(v, -2, 0), roll(v, 2, 0))
        near_y = jnp.where(
            low_j,
            jnp.where(middle.row > 0, roll(flip_j, 4), 0.0),
            jnp.where(middle.row < 3, roll(flip_j, -4), 0.0),
        )
        total = centre_coeff * v + (www * s01) * (f0 * flip_i + f1 * flip_j + f2 * flip_k) - pair2 * near_y
        near_low, near_high = roll(flip_k, 1), roll(flip_k, -1)
        for copy in copies:
            copy.wait_recv()
        landed = lambda d: RB2[slot_of, d]
        near_x = jnp.where(low_i, roll(landed(1), -16), roll(landed(0), 16))
        near_z = jnp.where(
            low_k,
            jnp.where(middle.at_first, landed(3), near_low),
            jnp.where(middle.at_last, towards_last(landed(2)), near_high),
        )
        return jnp.where(inside, total - pair2 * (near_x + near_z), 0.0)

    d = dinv2 * coarse_r * (1.0 / centre)
    x = keep_d * d + take_e * dinv2 * (coarse_r - coarse_apply(d, 0, 4))
    rest = coarse_r - coarse_apply(x, 1, 5)
    d = dinv2 * rest * (1.0 / centre)
    x = x + keep_d * d + take_e * dinv2 * (rest - coarse_apply(d, 2, 6))

    lifted = dot3(x, RPT1, RPT1l)
    columns = []
    for a in range(2):
        columns.append(PT1[0] * lifted[2 * a : 2 * a + 1, :] + PT1[1] * lifted[2 * a + 1 : 2 * a + 2, :])
    for j in range(8):
        middle.V[j] = middle.V[j] + PT1[0, j : j + 1, :] * columns[0] + PT1[1, j : j + 1, :] * columns[1]
    apply_level(middle, 2, 7, begin_post(middle))
    apply_level(middle, 3, 8, end_post(middle))

    C8[...] = contract(TPT, middle.V, 0, 8)
    for j0 in (0, 8):
        total = None
        for a in range(8):
            term = TP[j0 : j0 + 8, a : a + 1, :] * C8[a][None]
            total = term if total is None else total + term
        fine.U[j0 : j0 + 8, :, :128] = total
    lifted = dot3(fine.U[:, :, :128].reshape(256, 128), RPT, RPTl)
    fine.V[...] = fine.V[...] + lifted.reshape(16, 16, 256)
    apply_level(fine, 2, 9, begin_post(fine))
    apply_level(fine, 3, 10, end_post(fine))

    XIN[...] = jnp.transpose(fine.V[...].reshape(256, 256))
    for i in range(16):
        for r in range(4):
            out_ref[0, r, :, i * 256 : (i + 1) * 256] = XIN[i * SLOTS + r * 4 : i * SLOTS + r * 4 + 3, :]
    for copy in pending:
        copy.wait_send()


def scratch():
    f32, b16 = jnp.float32, jnp.bfloat16
    shapes = []
    for n in (16, 8):
        lanes = n * SLOTS
        shapes += [((n, n, lanes), f32)] * 4
        shapes += [((lanes, lanes), b16)] * 6 + [((lanes, 2 * lanes), b16), ((2 * lanes, lanes), b16)]
        shapes += [((n, lanes), f32)] + [((n, n, lanes), f32)] * 6
        shapes += [((6, n, lanes), f32)] * 3 + [((2, n, lanes), f32)]
        shapes += [((n, n, 2 * lanes), f32)] * 2 + [((4, 4, n, lanes), f32)] * 2
    shapes += [((16, 8, 128), f32), ((8, 16, 128), f32), ((2, 8, 128), f32)]
    shapes += [((256, 128), b16)] * 2 + [((128, 256), b16)] * 2 + [((128, 128), b16)] * 4
    shapes += [((8, 16, 128), f32)] * 2 + [((3, 4, 8, 128), f32)] * 2
    shapes += [((16, 256), f32), ((256, 256), f32)]
    semaphores = [pltpu.SemaphoreType.DMA((44,))] * 2
    return [pltpu.VMEM(shape, dtype) for shape, dtype in shapes] + semaphores


def shards(residual, orders, factors, widths):
    c0, c1, pair0, pair1, taus, coarse = constants()
    vmem = pl.BlockSpec(memory_space=pltpu.VMEM)
    smem = pl.BlockSpec(memory_space=pltpu.SMEM)
    return pl.pallas_call(
        functools.partial(kernel, taus, coarse),
        out_shape=jax.ShapeDtypeStruct(residual.shape, jnp.float32),
        in_specs=[smem] * 3 + [vmem] * 5,
        out_specs=vmem,
        scratch_shapes=scratch(),
        compiler_params=pltpu.CompilerParams(
            collective_id=0, has_side_effects=True, vmem_limit_bytes=48 * 1024 * 1024
        ),
    )(widths, orders, factors, jnp.asarray(c0), jnp.asarray(c1), jnp.asarray(pair0), jnp.asarray(pair1), residual)


def solution(mesh):
    return jax.shard_map(
        shards,
        mesh=mesh,
        in_specs=(
            P("dom", None, "grp", None),
            P("dom", None, "grp"),
            P("dom", None, "grp", None),
            P(),
        ),
        out_specs=P("dom", None, "grp", None),
        check_vma=False,
    )
```

```python
import functools

import jax
import jax.numpy as jnp
import ml_dtypes
import numpy as np
from jax import lax
from jax.experimental import pallas as pl
from jax.experimental.pallas import tpu as pltpu
from jax.sharding import PartitionSpec as P

MESH = pl.DeviceIdType.MESH
SLOTS = 16
REACH = 4
COLUMNS = 2 * REACH + 1
AROUND = [
    (dx, dg)
    for dx in range(-REACH, REACH + 1)
    for dg in (0, 1, -1, 2)
    if (dx, dg) != (0, 0) and abs(dg) <= REACH - abs(dx)
]
mass_weight = 0.5
penalty = 0.5
cheb_high = 4.0
cheb_low = 0.15


def cheb_nodes(degree):
    return -np.cos(np.pi * np.arange(degree + 1) / degree)


def bary_weights(npoints):
    weights = (-1.0) ** np.arange(npoints)
    weights[0] = 0.5 * weights[0]
    weights[-1] = 0.5 * weights[-1]
    return weights


def lagrange_table(source, target):
    weights = bary_weights(source.shape[0])
    spacing = target[:, None] - source[None, :]
    coincide = np.abs(spacing) < 1e-12
    fractions = weights[None, :] / np.where(coincide, 1.0, spacing)
    lookup = fractions / fractions.sum(axis=1, keepdims=True)
    return np.where(coincide.any(axis=1, keepdims=True), np.where(coincide, 1.0, 0.0), lookup)


def quad_weights(degree):
    weights = np.full(degree + 1, np.pi / degree)
    weights[0] = 0.5 * weights[0]
    weights[-1] = 0.5 * weights[-1]
    return weights


def derivative(degree):
    points = cheb_nodes(degree)
    weights = bary_weights(degree + 1)
    spacing = points[:, None] - points[None, :] + np.eye(degree + 1)
    lookup = weights[None, :] / weights[:, None] / spacing
    lookup = lookup * (1.0 - np.eye(degree + 1))
    return lookup - np.eye(degree + 1) * lookup.sum(axis=1)[:, None]


def level_degree(degree, level_index):
    return [degree, degree // 2, 1][level_index]


def split3(table):
    high = table.astype(ml_dtypes.bfloat16)
    rest = table - high.astype(np.float64)
    middle = rest.astype(ml_dtypes.bfloat16)
    low = (rest - middle.astype(np.float64)).astype(ml_dtypes.bfloat16)
    return high, middle, low


def packed(tables):
    rows = np.concatenate([entry.reshape(9, -1) for entry in tables], axis=1).T
    return np.concatenate(list(split3(rows)) + [np.zeros((rows.shape[0], 5), ml_dtypes.bfloat16)], axis=1)


def order_tables(level_index):
    points = [16, 8, 2][level_index]
    common = cheb_nodes(points - 1)
    common_w = quad_weights(points - 1)
    names = ("scaled", "stiff_diag", "quad_w", "interpolate", "face_diag", "living", "prolong")
    table = {name: [] for name in names}
    for degree in range(7, 16):
        local = level_degree(degree, level_index)
        quad = quad_weights(local)
        deriv = derivative(local)
        stiff = deriv.T @ (quad[:, None] * deriv)
        scaled = np.zeros((points, points))
        scaled[: local + 1, : local + 1] = stiff / quad[:, None]
        padded = lambda vector: np.concatenate([vector, np.zeros(points - local - 1)])
        interp = np.zeros((points, points))
        interp[:, : local + 1] = lagrange_table(cheb_nodes(local), common)
        table["scaled"].append(scaled)
        table["stiff_diag"].append(padded(np.diagonal(stiff)))
        table["quad_w"].append(padded(quad))
        table["interpolate"].append(interp)
        table["face_diag"].append((common_w[:, None] * interp**2).sum(axis=0))
        table["living"].append(padded(np.ones(local + 1)))
        if level_index < 2:
            coarse = level_degree(degree, level_index + 1)
            lift = np.zeros((points, [16, 8, 2][level_index + 1]))
            lift[: local + 1, : coarse + 1] = lagrange_table(cheb_nodes(coarse), cheb_nodes(local))
            table["prolong"].append(lift)
    table = {name: np.stack(table[name]) for name in names if table[name]}
    tau = penalty * (points - 1) ** 2
    table["pair"] = tau * np.outer(common_w, common_w)
    table["tau"] = tau
    return table


def flip(table):
    return np.swapaxes(table, 1, 2)


def constants():
    fine, middle, coarse = [order_tables(level_index) for level_index in range(3)]
    vectors = ("quad_w", "face_diag", "living", "stiff_diag")
    matrices = lambda t: [flip(t["scaled"]), t["scaled"], flip(t["interpolate"]), t["interpolate"]]
    c0 = packed(matrices(fine) + [fine[name] for name in vectors])
    c1 = packed(
        matrices(middle)
        + [middle[name] for name in vectors]
        + [fine["prolong"], flip(fine["prolong"]), flip(middle["prolong"])]
    )
    pairs = [np.repeat(t["pair"], SLOTS, axis=1).astype(np.float32) for t in (fine, middle)]
    return c0, c1, pairs[0], pairs[1], (fine["tau"], middle["tau"]), coarse


def split(values):
    high = values.astype(jnp.bfloat16)
    return high, (values - high.astype(jnp.float32)).astype(jnp.bfloat16)


def dot(left, right):
    return jnp.dot(left, right, preferred_element_type=jnp.float32)


def dot3(values, high, low):
    first, second = split(values)
    return dot(first, high[...]) + dot(second, high[...]) + dot(first, low[...])


def roll(values, shift, axis=-1):
    axis = axis % values.ndim
    return pltpu.roll(values, shift % values.shape[axis], axis)


def lanes_iota(lanes):
    return lax.broadcasted_iota(jnp.int32, (1, lanes), 1)


def rows_iota(rows, lanes):
    return lax.broadcasted_iota(jnp.int32, (rows, lanes), 0)


class Level:
    pass


def resolve(table, place):
    own = lax.broadcasted_iota(jnp.int32, table.shape[1:], 0) == place
    return jnp.sum(jnp.where(own[None], table[...], 0.0), axis=1)


def spread(keep, rows, count, target, low=None):
    keep[: rows.shape[0], : rows.shape[1]] = rows
    lanes = rows.shape[1]
    same = rows_iota(SLOTS, lanes) == (lanes_iota(lanes) & (SLOTS - 1))
    for p in range(count):
        block = jnp.where(same, keep[p : p + 1, :lanes], 0.0)
        high = block.astype(jnp.bfloat16)
        target[p * SLOTS : (p + 1) * SLOTS, :] = high
        if low is not None:
            low[p * SLOTS : (p + 1) * SLOTS, :] = (block - high.astype(jnp.float32)).astype(jnp.bfloat16)


def kernel(taus, coarse, *refs):
    names = iter(refs)
    take = lambda count: [next(names) for _ in range(count)]
    given = take(8)
    (out_ref,) = take(1)
    widths_ref, orders_ref, factors_ref, c0_ref, c1_ref, pair0_ref, pair1_ref, res_ref = take(8)
    levels = []
    for index in range(2):
        lv = Level()
        lv.n = [16, 8][index]
        lv.lanes = lv.n * SLOTS
        (lv.T, lv.TT, lv.TI, lv.TIT) = take(4)
        (lv.RS, lv.RSl, lv.RI, lv.RIl, lv.RIT, lv.RITl, lv.PP, lv.PPT) = take(8)
        (lv.IL, lv.DINV, lv.WWW, lv.R, lv.X, lv.V, lv.OUT) = take(7)
        (lv.H, lv.Q, lv.G, lv.RZ, lv.U, lv.Y, lv.SB, lv.RB) = take(8)
        lv.pair = [pair0_ref, pair1_ref][index]
        levels.append(lv)
    TP, TPT, PT1, RP, RPl, RPT, RPTl, RP1, RP1l, RPT1, RPT1l, A8, C8, SB2, RB2, KEEP, XIN = take(17)
    send_sem, recv_sem, load_sem, wide_send, wide_recv = take(5)
    landings = [widths_ref, orders_ref, factors_ref, c0_ref, c1_ref, pair0_ref, pair1_ref, res_ref]
    loads = [pltpu.make_async_copy(*pair, load_sem.at[i]) for i, pair in enumerate(zip(given, landings))]
    for load in loads:
        load.start()

    dom, grp = lax.axis_index("dom"), lax.axis_index("grp")
    n_dom, n_grp = lax.axis_size("dom"), lax.axis_size("grp")
    targets = [
        {"dom": lax.rem(dom + n_dom - 1, n_dom)},
        {"dom": lax.rem(dom + 1, n_dom)},
        {"grp": lax.rem(grp + n_grp - 1, n_grp)},
        {"grp": lax.rem(grp + 1, n_grp)},
    ]
    barrier = pltpu.get_barrier_semaphore()
    around = [
        {"dom": lax.rem(dom + n_dom + dx, n_dom), "grp": lax.rem(grp + n_grp + dg, n_grp)} for dx, dg in AROUND
    ]
    for target in around:
        pl.semaphore_signal(barrier, inc=1, device_id=target, device_id_type=MESH)

    lane = lanes_iota(16 * SLOTS)
    slot = lane & (SLOTS - 1)
    layer = slot >> 2
    row = slot & 3
    for load in loads[:3]:
        load.wait()
    width = jnp.int32(0)
    for g in range(4):
        width = jnp.where(grp == g, widths_ref[g], width)
    order = jnp.full(lane.shape, 7, jnp.int32)
    factor = [jnp.full(lane.shape, 1.0, jnp.float32) for _ in range(4)]
    for r in range(4):
        for t in range(3):
            here = slot == t * 4 + r
            order = jnp.where(here, orders_ref[t, 0, r], order)
            for c in range(4):
                factor[c] = jnp.where(here, factors_ref[0, t, r, c], factor[c])
    alive = layer < width
    mask = jnp.where(alive, 1.0, 0.0)
    at_first = layer == 0
    at_last = layer == width - 1
    line = rows_iota(32, 16 * SLOTS)
    line = jnp.where(line < 9, line, jnp.where(line < 18, line - 9, jnp.where(line < 27, line - 18, -1)))
    onehot = jnp.where(line == order - 7, 1.0, 0.0).astype(jnp.bfloat16)

    def tables(lv, index, which):
        refs = (lv.TI, lv.TIT, lv.T, lv.TT)
        source = [c0_ref, c1_ref][index]
        size = lv.n * lv.n
        at = (2, 3, 0, 1)[which] * size
        refs[which][...] = dot(source[at : at + size, :], lv.hot).reshape(lv.n, lv.n, lv.lanes)

    def setup_first(lv, index):
        n, lanes = lv.n, lv.lanes
        lv.place = lane[:, :lanes] >> 4
        lv.last = [order, order >> 1][index][:, :lanes]
        lv.f = [entry[:, :lanes] for entry in factor]
        lv.cm = lv.f[3] * mass_weight
        lv.at_first, lv.at_last = at_first[:, :lanes], at_last[:, :lanes]
        lv.row = row[:, :lanes]
        lv.last_range = [range(7, 16), range(3, 8)][index]
        lv.hot = onehot[:, :lanes]
        tables(lv, index, 0)
        at = 4 * n * n
        vectors = dot([c0_ref, c1_ref][index][at : at + 4 * n, :], lv.hot)
        quad, face, live, stiff = [vectors[i * n : (i + 1) * n] for i in range(4)]
        inter = resolve(lv.TI, lv.place)
        lv.IL[...] = inter
        spread(KEEP, inter, n, lv.RI, lv.RIl)
        points = rows_iota(n, lanes)
        lv.FM = jnp.where(points == 0, 1.0, 0.0)
        lv.LM = jnp.where(points == lv.last, 1.0, 0.0)
        lv.same = rows_iota(SLOTS, lanes) == (lane[:, :lanes] & (SLOTS - 1))
        for p in range(n):
            rows = slice(p * SLOTS, (p + 1) * SLOTS)
            lv.PP[rows, :lanes] = one(lv.same) if p == 0 else jnp.zeros((SLOTS, lanes), jnp.bfloat16)
            lv.PP[rows, lanes:] = one(lv.same & (lv.last == p))
        pick = lambda table: jnp.sum(jnp.where(points == lv.place, table, 0.0), axis=0, keepdims=True)
        w_i, face_i, live_i, stiff_i = pick(quad), pick(face), pick(live) * mask[:, :lanes], pick(stiff)
        ends = lv.FM + lv.LM
        ends_i = pick(ends)
        f0, f1, f2, _ = lv.f
        for j in range(n):
            one_row = lambda table: table[j : j + 1, :]
            w_j, face_j, live_j, stiff_j, ends_j = [one_row(t) for t in (quad, face, live, stiff, ends)]
            www = (w_i * w_j) * quad
            diagonal = (
                (f0 * stiff_i * w_j) * quad
                + (f1 * w_i * stiff_j) * quad
                + (f2 * w_i * w_j) * stiff
                + lv.cm * www
                + taus[index] * ((ends_j * face_i + face_j * ends_i) * face + (face_j * face_i) * ends)
            )
            node_live = (live_j * live_i) * live
            lv.WWW[j] = www
            lv.DINV[j] = node_live / (diagonal + 1.0 - node_live)
            if index == 0:
                lv.X[j] = node_live

    def setup_rest(lv, index):
        n, lanes = lv.n, lv.lanes
        for which in (1, 2, 3):
            tables(lv, index, which)
        spread(KEEP, resolve(lv.T, lv.place) * lv.f[0], n, lv.RS, lv.RSl)
        spread(KEEP, resolve(lv.TIT, lv.place), n, lv.RIT, lv.RITl)
        for p in range(n):
            lv.PPT[p * SLOTS : (p + 1) * SLOTS, :] = one(lv.same & (lv.place == 0))
            lv.PPT[lanes + p * SLOTS : lanes + (p + 1) * SLOTS, :] = one(lv.same & (lv.place == lv.last))

    def setup_between():
        at = 4 * 64 + 4 * 8
        TP[...] = dot(c1_ref[at : at + 128, :], middle.hot).reshape(16, 8, 128)
        TPT[...] = dot(c1_ref[at + 128 : at + 256, :], middle.hot).reshape(8, 16, 128)
        PT1[...] = dot(c1_ref[at + 256 : at + 272, :], middle.hot).reshape(2, 8, 128)
        place1 = middle.place
        spread(KEEP, resolve(TP, place1), 16, RP, RPl)
        wide = jnp.concatenate([TPT[...], TPT[...]], axis=2)
        spread(KEEP, resolve(wide, fine.place), 8, RPT, RPTl)
        spread(KEEP, jnp.where(place1 == 0, PT1[0], jnp.where(place1 == 1, PT1[1], 0.0)), 8, RP1, RP1l)
        RPT1[...] = jnp.zeros(RPT1.shape, jnp.bfloat16)
        RPT1l[...] = jnp.zeros(RPT1l.shape, jnp.bfloat16)
        spread(KEEP, resolve(PT1, place1), 2, RPT1, RPT1l)

    def setup_middle():
        setup_first(middle, 1)
        setup_rest(middle, 1)
        setup_between()

    one = lambda cond: jnp.where(cond, 1.0, 0.0).astype(jnp.bfloat16)
    fine, middle = levels
    for load in loads[3:7]:
        load.wait()
    setup_first(fine, 0)

    loads[7].wait()
    for i in range(16):
        for t in range(3):
            XIN[i * SLOTS + t * 4 : i * SLOTS + t * 4 + 4, :] = res_ref[0, t, :, i * 256 : (i + 1) * 256]
        XIN[i * SLOTS + 12 : i * SLOTS + 16, :] = jnp.zeros((4, 256), jnp.float32)
    fine.R[...] = jnp.transpose(XIN[...]).reshape(16, 16, 256) * fine.X[...]

    pl.semaphore_wait(barrier, len(AROUND))
    pending = []
    lane1 = lane[:, :128]
    group1 = lane1 >> 5

    def gather_start(which, value):
        SB2[which] = value
        for q in range(len(AROUND)):
            where = which * len(AROUND) + q
            copy = pltpu.make_async_remote_copy(
                src_ref=SB2.at[which],
                dst_ref=RB2.at[which, q],
                send_sem=wide_send.at[where],
                recv_sem=wide_recv.at[where],
                device_id=around[q],
                device_id_type=MESH,
            )
            copy.start()
            pending.append(copy)
        return pending[-len(AROUND) :]

    def gather_end(which, value, copies):
        for copy in copies:
            copy.wait_recv()
        columns = []
        for column in range(-REACH, REACH + 1):
            total = value if column == 0 else None
            for q, (dx, _) in enumerate(AROUND):
                if -dx == column:
                    total = RB2[which, q] if total is None else total + RB2[which, q]
            columns.append(total)
        return jnp.stack(columns)

    own_group = group1 == grp
    own_factors = jnp.concatenate(
        [jnp.where(own_group, entry[:, :128], 0.0) for entry in factor] + [jnp.zeros((4, 128), jnp.float32)], axis=0
    )
    factor_copies = gather_start(0, own_factors)

    def send(number, direction, value, source, landing):
        source[...] = value
        where = number * 4 + direction
        copy = pltpu.make_async_remote_copy(
            src_ref=source,
            dst_ref=landing,
            send_sem=send_sem.at[where],
            recv_sem=recv_sem.at[where],
            device_id=targets[direction],
            device_id_type=MESH,
        )
        copy.start()
        pending.append(copy)
        return copy

    def towards_first(value, last):
        value = jnp.where(last, value, 0.0)
        return value + roll(value, -4) + roll(value, -8)

    def towards_last(value):
        return jnp.where(width == 1, value, jnp.where(width == 2, roll(value, 4), roll(value, 8)))

    def contract(table, source, first, count):
        total = None
        for k in range(table.shape[0]):
            term = table[k][None] * source[first : first + count, k : k + 1, :]
            total = term if total is None else total + term
        return total

    def apply_level(lv, slot_of, number, consume, meanwhile=None, near=None):
        n, lanes = lv.n, lv.lanes
        flat = lv.V[...].reshape(n * n, lanes)
        high, low = split(flat)
        lv.U[...] = (dot(high, lv.PP[...]) + dot(low, lv.PP[...])).reshape(n, n, 2 * lanes)
        y0, z0 = lv.V[0], lv.V[:, 0, :]
        y1, z1 = jnp.zeros_like(y0), jnp.zeros_like(z0)
        for p in lv.last_range:
            here = lv.last == p
            y1 = jnp.where(here, lv.V[p], y1)
            z1 = jnp.where(here, lv.V[:, p, :], z1)
        turned = dot3(jnp.concatenate([z0, z1, y0, y1], axis=0), lv.RI, lv.RIl)
        lv.H[2:6] = turned.reshape(4, n, lanes)
        for f in range(2):
            total = None
            for j in range(n):
                term = lv.IL[j : j + 1, :] * lv.U[j, :, f * lanes : (f + 1) * lanes]
                total = term if total is None else total + term
            lv.H[f] = total
        lv.Q[...] = contract(lv.TI, lv.H, 0, 6)
        copies = []
        if near is None:
            outgoing = [lv.Q[0], lv.Q[1], lv.Q[2], towards_first(lv.Q[3], lv.at_last)]
            copies = [
                send(number, d, outgoing[d], lv.SB.at[slot_of, d], lv.RB.at[slot_of, d]) for d in range(4)
            ]
        if meanwhile is not None:
            meanwhile()
        lv.G[4] = lv.pair[...] * (lv.Q[4] - jnp.where(lv.row > 0, roll(lv.Q[5], 1), 0.0))
        lv.G[5] = lv.pair[...] * (lv.Q[5] - jnp.where(lv.row < 3, roll(lv.Q[4], -1), 0.0))
        back = contract(lv.TIT, lv.G, 4, 2).reshape(2 * n, lanes)
        back = dot3(back, lv.RIT, lv.RITl)
        y_back = [back[:n], back[n:]]
        lv.OUT[...] = (
            dot(high, lv.RS[...]) + dot(low, lv.RS[...]) + dot(high, lv.RSl[...])
        ).reshape(n, n, lanes)
        size = 4 if n == 16 else 8
        for a in range(0, n, size):
            block = slice(a, a + size)
            along_j, along_k = None, None
            for j in range(n):
                term = lv.TT[block, j : j + 1, :] * lv.V[j][None]
                along_j = term if along_j is None else along_j + term
            for k in range(n):
                term = lv.T[k][None] * lv.V[block, k : k + 1, :]
                along_k = term if along_k is None else along_k + term
            lv.OUT[block] = lv.WWW[block] * (
                lv.OUT[block] + lv.f[1] * along_j + lv.f[2] * along_k + lv.cm * lv.V[block]
            )
        lv.OUT[0] = lv.OUT[0] + y_back[0]
        for p in lv.last_range:
            lv.OUT[p] = lv.OUT[p] + jnp.where(lv.last == p, y_back[1], 0.0)
        for copy in copies:
            copy.wait_recv()
        pair = lv.pair[...]
        landed = lambda d: lv.RB[slot_of, d]
        if near is None:
            x_low, x_high, z_low, z_high = landed(1), landed(0), landed(3), towards_last(landed(2))
        else:
            x_low, x_high, z_low, z_high = near
        lv.G[0] = pair * (lv.Q[0] - x_low)
        lv.G[1] = pair * (lv.Q[1] - x_high)
        lv.G[2] = pair * (lv.Q[2] - jnp.where(lv.at_first, z_low, roll(lv.Q[3], 4)))
        lv.G[3] = pair * (lv.Q[3] - jnp.where(lv.at_last, z_high, roll(lv.Q[2], -4)))
        back = contract(lv.TIT, lv.G, 0, 4)
        for f in range(2):
            for j in range(n):
                lv.Y[j, :, f * lanes : (f + 1) * lanes] = lv.IL[j : j + 1, :] * back[f]
        lv.RZ[...] = dot3(back[2:4].reshape(2 * n, lanes), lv.RIT, lv.RITl).reshape(2, n, lanes)
        first, second = split(lv.Y[...].reshape(n * n, 2 * lanes))
        x_back = (dot(first, lv.PPT[...]) + dot(second, lv.PPT[...])).reshape(n, n, lanes)
        for j in range(n):
            z_back = lv.FM * lv.RZ[0, j : j + 1, :] + lv.LM * lv.RZ[1, j : j + 1, :]
            consume(j, lv.OUT[j] + x_back[j] + z_back)

    centre = 0.5 * (cheb_high + cheb_low)
    radius = 0.5 * (cheb_high - cheb_low)
    rho_first = radius / centre
    rho_next = 1.0 / (2.0 * centre / radius - rho_first)
    keep_d = 1.0 + rho_next * rho_first
    take_e = 2.0 * rho_next / radius

    def first_step(lv):
        lv.V[...] = lv.DINV[...] * lv.R[...] * (1.0 / centre)

    def end_pre(lv):
        def consume(j, applied):
            lv.V[j] = keep_d * lv.V[j] + take_e * lv.DINV[j] * (lv.R[j] - applied)

        return consume

    def remainder(lv):
        def consume(j, applied):
            lv.OUT[j] = lv.R[j] - applied

        return consume

    def begin_post(lv):
        def consume(j, applied):
            rest = lv.R[j] - applied
            lv.R[j] = rest
            lv.X[j] = lv.V[j]
            lv.V[j] = lv.DINV[j] * rest * (1.0 / centre)

        return consume

    def end_post(lv):
        def consume(j, applied):
            lv.V[j] = lv.X[j] + keep_d * lv.V[j] + take_e * lv.DINV[j] * (lv.R[j] - applied)

        return consume

    first_step(fine)
    apply_level(fine, 0, 0, end_pre(fine), lambda: setup_rest(fine, 0))
    apply_level(fine, 1, 1, remainder(fine), setup_middle)

    lanes_down = dot3(fine.OUT[...].reshape(256, 256), RP, RPl).reshape(16, 16, 128)
    total = None
    for j in range(16):
        term = TPT[:, j : j + 1, :] * lanes_down[j][None]
        total = term if total is None else total + term
    A8[...] = total
    middle.R[...] = contract(TP, A8, 0, 8)
    first_step(middle)
    apply_level(middle, 0, 2, end_pre(middle))
    apply_level(middle, 1, 3, remainder(middle))

    parts = []
    for a in range(2):
        total = None
        for j in range(8):
            term = PT1[a, j : j + 1, :] * middle.OUT[j]
            total = term if total is None else total + term
        for b in range(2):
            parts.append(jnp.sum(PT1[b] * total, axis=0, keepdims=True))
    coarse_r = dot3(jnp.concatenate(parts + [jnp.zeros((4, 128), jnp.float32)], axis=0), RP1, RP1l)

    def placed(value):
        total = value
        for g in range(1, 4):
            total = jnp.where(grp == g, roll(value, 32 * g), total)
        return total

    def unplaced(value):
        total = value
        for g in range(1, 4):
            total = jnp.where(grp == g, roll(value, -32 * g), total)
        return jnp.where(lane1 < 32, total, 0.0)

    own_r = placed(coarse_r)
    r_copies = gather_start(1, own_r)

    fs = gather_end(0, own_factors, factor_copies)
    f0, f1, f2, f3 = [fs[:, c : c + 1, :] for c in range(4)]
    line2 = rows_iota(8, 128)
    low_i = ((lane1 >> 4) & 1) == 0
    low_j = line2 < 2
    low_k = (line2 & 1) == 0
    row2, layer2 = lane1 & 3, (lane1 >> 2) & 3
    width2, before2 = jnp.zeros((1, 128), jnp.int32), jnp.zeros((1, 128), jnp.int32)
    for g in range(4):
        width2 = jnp.where(group1 == g, widths_ref[g], width2)
        before2 = jnp.where(group1 == (g + 1) % 4, widths_ref[g], before2)
    s00, s01 = float(coarse["scaled"][0, 0, 0]), float(coarse["scaled"][0, 0, 1])
    w0 = float(coarse["quad_w"][0, 0])
    www = w0**3
    pair2 = float(coarse["pair"][0, 0])
    centre_coeff = www * (s00 * (f0 + f1 + f2) + mass_weight * f3) + 3.0 * pair2
    live2 = jnp.where((layer2 < width2) & (line2 < 4), 1.0, 0.0)[None]
    dinv2 = live2 / (centre_coeff + 1.0 - live2)
    f0, f1, f2 = [(www * s01) * entry for entry in (f0, f1, f2)]

    def sideways(value, shift):
        return roll(value.reshape(-1, 128), shift).reshape(value.shape)

    def next_layer(value):
        across = jnp.where(
            width2 == 1, sideways(value, -32), jnp.where(width2 == 2, sideways(value, -28), sideways(value, -24))
        )
        return jnp.where(layer2 < width2 - 1, sideways(value, -4), across)

    def last_layer(value):
        across = jnp.where(
            before2 == 1, sideways(value, 32), jnp.where(before2 == 2, sideways(value, 28), sideways(value, 24))
        )
        return jnp.where(layer2 > 0, sideways(value, 4), across)

    def other_k(value):
        return jnp.where(low_k, roll(value, -1, 1), roll(value, 1, 1))

    def coarse_apply(value, skip):
        mid = value[1:-1]
        part = slice(skip, COLUMNS - skip)
        flip_i = jnp.where(low_i, sideways(mid, -16), sideways(mid, 16))
        flip_j = jnp.where(low_j, roll(mid, -2, 1), roll(mid, 2, 1))
        flip_k = other_k(mid)
        near_x = jnp.where(low_i, sideways(value[:-2], -16), sideways(value[2:], 16))
        near_y = jnp.where(
            low_j,
            jnp.where(row2 > 0, sideways(flip_j, 1), 0.0),
            jnp.where(row2 < 3, sideways(flip_j, -1), 0.0),
        )
        near_z = jnp.where(low_k, last_layer(flip_k), next_layer(flip_k))
        return (
            centre_coeff[part] * mid
            + (f0[part] * flip_i + f1[part] * flip_j + f2[part] * flip_k)
            - pair2 * (near_x + near_y + near_z)
        )

    rs = gather_end(1, own_r, r_copies)
    d = dinv2 * rs * (1.0 / centre)
    xs = keep_d * d[1:-1] + take_e * dinv2[1:-1] * (rs[1:-1] - coarse_apply(d, 1))
    rest = rs[2:-2] - coarse_apply(xs, 2)
    d = dinv2[2:-2] * rest * (1.0 / centre)
    xs = xs[2:-2] + keep_d * d[1:-1] + take_e * dinv2[3:-3] * (rest[1:-1] - coarse_apply(d, 3))
    x = unplaced(xs[1])

    points = cheb_nodes(7)
    along_lane, along_row = jnp.zeros((1, 128), jnp.float32), jnp.zeros((8, 128), jnp.float32)
    for b in range(8):
        along_lane = jnp.where((lane1 >> 4) == b, float(points[b]), along_lane)
        along_row = jnp.where(line2 == b, float(points[b]), along_row)
    lane_ends = [0.5 - 0.5 * along_lane, 0.5 + 0.5 * along_lane]
    row_ends = [0.5 - 0.5 * along_row, 0.5 + 0.5 * along_row]

    def all_lanes(value, end):
        value = jnp.where(lane1 < 16, roll(value, -16) if end else value, 0.0)
        value = value + roll(value, 16)
        value = value + roll(value, 32)
        return value + roll(value, 64)

    def x_trace(column, end):
        face = all_lanes(unplaced(column), end)
        total = 0.0
        for k in range(2):
            line = lane_ends[0] * face[k : k + 1, :] + lane_ends[1] * face[2 + k : 3 + k, :]
            total = total + row_ends[k] * line
        return total

    def z_trace(column, k):
        column = unplaced(column)
        face = lane_ends[0] * all_lanes(column, 0) + lane_ends[1] * all_lanes(column, 1)
        return row_ends[0] * face[k : k + 1, :] + row_ends[1] * face[2 + k : 3 + k, :]

    turned = other_k(xs[1:2])
    correction_traces = [
        x_trace(xs[0], 1),
        x_trace(xs[2], 0),
        z_trace(last_layer(turned)[0], 0),
        z_trace(next_layer(turned)[0], 1),
    ]
    before = [middle.RB[1, 1], middle.RB[1, 0], middle.RB[1, 3], towards_last(middle.RB[1, 2])]
    middle_near = [old + new for old, new in zip(before, correction_traces)]

    lifted = dot3(x, RPT1, RPT1l)
    columns = []
    for a in range(2):
        columns.append(PT1[0] * lifted[2 * a : 2 * a + 1, :] + PT1[1] * lifted[2 * a + 1 : 2 * a + 2, :])
    for j in range(8):
        middle.V[j] = middle.V[j] + PT1[0, j : j + 1, :] * columns[0] + PT1[1, j : j + 1, :] * columns[1]
    apply_level(middle, 2, None, begin_post(middle), near=middle_near)
    apply_level(middle, 3, 8, end_post(middle))

    C8[...] = contract(TPT, middle.V, 0, 8)
    for j0 in (0, 8):
        total = None
        for a in range(8):
            term = TP[j0 : j0 + 8, a : a + 1, :] * C8[a][None]
            total = term if total is None else total + term
        fine.U[j0 : j0 + 8, :, :128] = total
    lifted = dot3(fine.U[:, :, :128].reshape(256, 128), RPT, RPTl)
    fine.V[...] = fine.V[...] + lifted.reshape(16, 16, 256)
    apply_level(fine, 2, 9, begin_post(fine))
    apply_level(fine, 3, 10, end_post(fine))

    XIN[...] = jnp.transpose(fine.V[...].reshape(256, 256))
    for i in range(16):
        for t in range(3):
            out_ref[0, t, :, i * 256 : (i + 1) * 256] = XIN[i * SLOTS + t * 4 : i * SLOTS + t * 4 + 4, :]
    for copy in pending:
        copy.wait_send()


def scratch(given):
    f32, b16 = jnp.float32, jnp.bfloat16
    shapes = []
    for n in (16, 8):
        lanes = n * SLOTS
        shapes += [((n, n, lanes), f32)] * 4
        shapes += [((lanes, lanes), b16)] * 6 + [((lanes, 2 * lanes), b16), ((2 * lanes, lanes), b16)]
        shapes += [((n, lanes), f32)] + [((n, n, lanes), f32)] * 6
        shapes += [((6, n, lanes), f32)] * 3 + [((2, n, lanes), f32)]
        shapes += [((n, n, 2 * lanes), f32)] * 2 + [((4, 4, n, lanes), f32)] * 2
    shapes += [((16, 8, 128), f32), ((8, 16, 128), f32), ((2, 8, 128), f32)]
    shapes += [((256, 128), b16)] * 2 + [((128, 256), b16)] * 2 + [((128, 128), b16)] * 4
    shapes += [((8, 16, 128), f32)] * 2 + [((2, 8, 128), f32), ((2, len(AROUND), 8, 128), f32)]
    shapes += [((16, 256), f32), ((256, 256), f32)]
    semaphores = [pltpu.SemaphoreType.DMA((44,))] * 2 + [pltpu.SemaphoreType.DMA((8,))]
    semaphores += [pltpu.SemaphoreType.DMA((2 * len(AROUND),))] * 2
    landings = [pltpu.SMEM(x.shape, x.dtype) for x in given[:3]] + [pltpu.VMEM(x.shape, x.dtype) for x in given[3:]]
    return landings + [pltpu.VMEM(shape, dtype) for shape, dtype in shapes] + semaphores


def shards(residual, orders, factors, widths):
    c0, c1, pair0, pair1, taus, coarse = constants()
    given = [
        widths,
        jnp.transpose(orders, (2, 0, 1)),
        jnp.transpose(factors, (0, 2, 1, 3)),
        jnp.asarray(c0),
        jnp.asarray(c1),
        jnp.asarray(pair0),
        jnp.asarray(pair1),
        jnp.transpose(residual, (0, 2, 1, 3)),
    ]
    out = pl.pallas_call(
        functools.partial(kernel, taus, coarse),
        out_shape=jax.ShapeDtypeStruct((1, 3, 4, 4096), jnp.float32),
        in_specs=[pl.BlockSpec(memory_space=pltpu.HBM)] * 8,
        out_specs=pl.BlockSpec(memory_space=pltpu.VMEM),
        scratch_shapes=scratch(given),
        compiler_params=pltpu.CompilerParams(
            collective_id=0, has_side_effects=True, vmem_limit_bytes=62 * 1024 * 1024
        ),
    )(*given)
    return jnp.transpose(out, (0, 2, 1, 3))


def solution(mesh):
    return jax.shard_map(
        shards,
        mesh=mesh,
        in_specs=(
            P("dom", None, "grp", None),
            P("dom", None, "grp"),
            P("dom", None, "grp", None),
            P(),
        ),
        out_specs=P("dom", None, "grp", None),
        check_vma=False,
    )
```

```python
import functools

import jax
import jax.numpy as jnp
import ml_dtypes
import numpy as np
from jax import lax
from jax.experimental import pallas as pl
from jax.experimental.pallas import tpu as pltpu
from jax.sharding import PartitionSpec as P

MESH = pl.DeviceIdType.MESH
SLOTS = 16
REACH = 5
COLUMNS = 2 * REACH + 1
AROUND = [
    (dx, dg)
    for dx in range(-REACH, REACH + 1)
    for dg in (0, 1, -1, 2)
    if (dx, dg) != (0, 0) and abs(dg) <= REACH - abs(dx)
]
mass_weight = 0.5
penalty = 0.5
cheb_high = 4.0
cheb_low = 0.15


def cheb_nodes(degree):
    return -np.cos(np.pi * np.arange(degree + 1) / degree)


def bary_weights(npoints):
    weights = (-1.0) ** np.arange(npoints)
    weights[0] = 0.5 * weights[0]
    weights[-1] = 0.5 * weights[-1]
    return weights


def lagrange_table(source, target):
    weights = bary_weights(source.shape[0])
    spacing = target[:, None] - source[None, :]
    coincide = np.abs(spacing) < 1e-12
    fractions = weights[None, :] / np.where(coincide, 1.0, spacing)
    lookup = fractions / fractions.sum(axis=1, keepdims=True)
    return np.where(coincide.any(axis=1, keepdims=True), np.where(coincide, 1.0, 0.0), lookup)


def quad_weights(degree):
    weights = np.full(degree + 1, np.pi / degree)
    weights[0] = 0.5 * weights[0]
    weights[-1] = 0.5 * weights[-1]
    return weights


def derivative(degree):
    points = cheb_nodes(degree)
    weights = bary_weights(degree + 1)
    spacing = points[:, None] - points[None, :] + np.eye(degree + 1)
    lookup = weights[None, :] / weights[:, None] / spacing
    lookup = lookup * (1.0 - np.eye(degree + 1))
    return lookup - np.eye(degree + 1) * lookup.sum(axis=1)[:, None]


def level_degree(degree, level_index):
    return [degree, degree // 2, 1][level_index]


def split3(table):
    high = table.astype(ml_dtypes.bfloat16)
    rest = table - high.astype(np.float64)
    middle = rest.astype(ml_dtypes.bfloat16)
    low = (rest - middle.astype(np.float64)).astype(ml_dtypes.bfloat16)
    return high, middle, low


def packed(tables):
    rows = np.concatenate([entry.reshape(9, -1) for entry in tables], axis=1).T
    return np.concatenate(list(split3(rows)) + [np.zeros((rows.shape[0], 5), ml_dtypes.bfloat16)], axis=1)


def order_tables(level_index):
    points = [16, 8, 2][level_index]
    common = cheb_nodes(points - 1)
    common_w = quad_weights(points - 1)
    names = ("scaled", "stiff_diag", "quad_w", "interpolate", "face_diag", "living", "prolong")
    table = {name: [] for name in names}
    for degree in range(7, 16):
        local = level_degree(degree, level_index)
        quad = quad_weights(local)
        deriv = derivative(local)
        stiff = deriv.T @ (quad[:, None] * deriv)
        scaled = np.zeros((points, points))
        scaled[: local + 1, : local + 1] = stiff / quad[:, None]
        padded = lambda vector: np.concatenate([vector, np.zeros(points - local - 1)])
        interp = np.zeros((points, points))
        interp[:, : local + 1] = lagrange_table(cheb_nodes(local), common)
        table["scaled"].append(scaled)
        table["stiff_diag"].append(padded(np.diagonal(stiff)))
        table["quad_w"].append(padded(quad))
        table["interpolate"].append(interp)
        table["face_diag"].append((common_w[:, None] * interp**2).sum(axis=0))
        table["living"].append(padded(np.ones(local + 1)))
        if level_index < 2:
            coarse = level_degree(degree, level_index + 1)
            lift = np.zeros((points, [16, 8, 2][level_index + 1]))
            lift[: local + 1, : coarse + 1] = lagrange_table(cheb_nodes(coarse), cheb_nodes(local))
            table["prolong"].append(lift)
    table = {name: np.stack(table[name]) for name in names if table[name]}
    tau = penalty * (points - 1) ** 2
    table["pair"] = tau * np.outer(common_w, common_w)
    table["tau"] = tau
    return table


def flip(table):
    return np.swapaxes(table, 1, 2)


def constants():
    fine, middle, coarse = [order_tables(level_index) for level_index in range(3)]
    vectors = ("quad_w", "face_diag", "living", "stiff_diag")
    matrices = lambda t: [flip(t["scaled"]), t["scaled"], flip(t["interpolate"]), t["interpolate"]]
    c0 = packed(matrices(fine) + [fine[name] for name in vectors])
    c1 = packed(
        matrices(middle)
        + [middle[name] for name in vectors]
        + [fine["prolong"], flip(fine["prolong"]), flip(middle["prolong"])]
    )
    pairs = [np.repeat(t["pair"], SLOTS, axis=1).astype(np.float32) for t in (fine, middle)]
    return c0, c1, pairs[0], pairs[1], (fine["tau"], middle["tau"]), coarse


def split(values):
    high = values.astype(jnp.bfloat16)
    return high, (values - high.astype(jnp.float32)).astype(jnp.bfloat16)


def dot(left, right):
    return jnp.dot(left, right, preferred_element_type=jnp.float32)


def dot3(values, high, low):
    first, second = split(values)
    return dot(first, high[...]) + dot(second, high[...]) + dot(first, low[...])


def roll(values, shift, axis=-1):
    axis = axis % values.ndim
    return pltpu.roll(values, shift % values.shape[axis], axis)


def lanes_iota(lanes):
    return lax.broadcasted_iota(jnp.int32, (1, lanes), 1)


def rows_iota(rows, lanes):
    return lax.broadcasted_iota(jnp.int32, (rows, lanes), 0)


class Level:
    pass


def resolve(table, place):
    own = lax.broadcasted_iota(jnp.int32, table.shape[1:], 0) == place
    return jnp.sum(jnp.where(own[None], table[...], 0.0), axis=1)


def spread(keep, rows, count, target, low=None):
    keep[: rows.shape[0], : rows.shape[1]] = rows
    lanes = rows.shape[1]
    same = rows_iota(SLOTS, lanes) == (lanes_iota(lanes) & (SLOTS - 1))
    for p in range(count):
        block = jnp.where(same, keep[p : p + 1, :lanes], 0.0)
        high = block.astype(jnp.bfloat16)
        target[p * SLOTS : (p + 1) * SLOTS, :] = high
        if low is not None:
            low[p * SLOTS : (p + 1) * SLOTS, :] = (block - high.astype(jnp.float32)).astype(jnp.bfloat16)


def kernel(taus, coarse, *refs):
    names = iter(refs)
    take = lambda count: [next(names) for _ in range(count)]
    given = take(8)
    (out_ref,) = take(1)
    widths_ref, orders_ref, factors_ref, c0_ref, c1_ref, pair0_ref, pair1_ref, res_ref = take(8)
    levels = []
    for index in range(2):
        lv = Level()
        lv.n = [16, 8][index]
        lv.lanes = lv.n * SLOTS
        (lv.T, lv.TT, lv.TI, lv.TIT) = take(4)
        (lv.RS, lv.RSl, lv.RI, lv.RIl, lv.RIT, lv.RITl, lv.PP, lv.PPT) = take(8)
        (lv.IL, lv.DINV, lv.WWW, lv.R, lv.X, lv.V, lv.OUT) = take(7)
        (lv.H, lv.Q, lv.G, lv.RZ, lv.U, lv.Y, lv.SB, lv.RB) = take(8)
        lv.pair = [pair0_ref, pair1_ref][index]
        levels.append(lv)
    TP, TPT, PT1, RP, RPl, RPT, RPTl, RP1, RP1l, RPT1, RPT1l, A8, C8, SBF, RBF, SBR, RBR, KEEP, XIN = take(19)
    send_sem, recv_sem, load_sem, wide_send, wide_recv = take(5)
    landings = [widths_ref, orders_ref, factors_ref, c0_ref, c1_ref, pair0_ref, pair1_ref, res_ref]
    loads = [pltpu.make_async_copy(*pair, load_sem.at[i]) for i, pair in enumerate(zip(given, landings))]
    for load in loads:
        load.start()

    dom, grp = lax.axis_index("dom"), lax.axis_index("grp")
    n_dom, n_grp = lax.axis_size("dom"), lax.axis_size("grp")
    targets = [
        {"dom": lax.rem(dom + n_dom - 1, n_dom)},
        {"dom": lax.rem(dom + 1, n_dom)},
        {"grp": lax.rem(grp + n_grp - 1, n_grp)},
        {"grp": lax.rem(grp + 1, n_grp)},
    ]
    barrier = pltpu.get_barrier_semaphore()
    around = [
        {"dom": lax.rem(dom + n_dom + dx, n_dom), "grp": lax.rem(grp + n_grp + dg, n_grp)} for dx, dg in AROUND
    ]
    for target in around:
        pl.semaphore_signal(barrier, inc=1, device_id=target, device_id_type=MESH)

    lane = lanes_iota(16 * SLOTS)
    slot = lane & (SLOTS - 1)
    layer = slot >> 2
    row = slot & 3
    for load in loads[:3]:
        load.wait()
    width = jnp.int32(0)
    for g in range(4):
        width = jnp.where(grp == g, widths_ref[g], width)
    order = jnp.full(lane.shape, 7, jnp.int32)
    factor = [jnp.full(lane.shape, 1.0, jnp.float32) for _ in range(4)]
    for r in range(4):
        for t in range(3):
            here = slot == t * 4 + r
            order = jnp.where(here, orders_ref[t, 0, r], order)
            for c in range(4):
                factor[c] = jnp.where(here, factors_ref[0, t, r, c], factor[c])
    alive = layer < width
    mask = jnp.where(alive, 1.0, 0.0)
    at_first = layer == 0
    at_last = layer == width - 1
    line = rows_iota(32, 16 * SLOTS)
    line = jnp.where(line < 9, line, jnp.where(line < 18, line - 9, jnp.where(line < 27, line - 18, -1)))
    onehot = jnp.where(line == order - 7, 1.0, 0.0).astype(jnp.bfloat16)

    def tables(lv, index, which):
        refs = (lv.TI, lv.TIT, lv.T, lv.TT)
        source = [c0_ref, c1_ref][index]
        size = lv.n * lv.n
        at = (2, 3, 0, 1)[which] * size
        refs[which][...] = dot(source[at : at + size, :], lv.hot).reshape(lv.n, lv.n, lv.lanes)

    def setup_first(lv, index):
        n, lanes = lv.n, lv.lanes
        lv.place = lane[:, :lanes] >> 4
        lv.last = [order, order >> 1][index][:, :lanes]
        lv.f = [entry[:, :lanes] for entry in factor]
        lv.cm = lv.f[3] * mass_weight
        lv.at_first, lv.at_last = at_first[:, :lanes], at_last[:, :lanes]
        lv.row = row[:, :lanes]
        lv.last_range = [range(7, 16), range(3, 8)][index]
        lv.hot = onehot[:, :lanes]
        tables(lv, index, 0)
        at = 4 * n * n
        vectors = dot([c0_ref, c1_ref][index][at : at + 4 * n, :], lv.hot)
        quad, face, live, stiff = [vectors[i * n : (i + 1) * n] for i in range(4)]
        inter = resolve(lv.TI, lv.place)
        lv.IL[...] = inter
        spread(KEEP, inter, n, lv.RI, lv.RIl)
        points = rows_iota(n, lanes)
        lv.FM = jnp.where(points == 0, 1.0, 0.0)
        lv.LM = jnp.where(points == lv.last, 1.0, 0.0)
        lv.same = rows_iota(SLOTS, lanes) == (lane[:, :lanes] & (SLOTS - 1))
        for p in range(n):
            rows = slice(p * SLOTS, (p + 1) * SLOTS)
            lv.PP[rows, :lanes] = one(lv.same) if p == 0 else jnp.zeros((SLOTS, lanes), jnp.bfloat16)
            lv.PP[rows, lanes:] = one(lv.same & (lv.last == p))
        pick = lambda table: jnp.sum(jnp.where(points == lv.place, table, 0.0), axis=0, keepdims=True)
        w_i, face_i, live_i, stiff_i = pick(quad), pick(face), pick(live) * mask[:, :lanes], pick(stiff)
        ends = lv.FM + lv.LM
        ends_i = pick(ends)
        f0, f1, f2, _ = lv.f
        for j in range(n):
            one_row = lambda table: table[j : j + 1, :]
            w_j, face_j, live_j, stiff_j, ends_j = [one_row(t) for t in (quad, face, live, stiff, ends)]
            www = (w_i * w_j) * quad
            diagonal = (
                (f0 * stiff_i * w_j) * quad
                + (f1 * w_i * stiff_j) * quad
                + (f2 * w_i * w_j) * stiff
                + lv.cm * www
                + taus[index] * ((ends_j * face_i + face_j * ends_i) * face + (face_j * face_i) * ends)
            )
            node_live = (live_j * live_i) * live
            lv.WWW[j] = www
            lv.DINV[j] = node_live / (diagonal + 1.0 - node_live)
            if index == 0:
                lv.X[j] = node_live

    def setup_rest(lv, index):
        n, lanes = lv.n, lv.lanes
        for which in (1, 2, 3):
            tables(lv, index, which)
        spread(KEEP, resolve(lv.T, lv.place) * lv.f[0], n, lv.RS, lv.RSl)
        spread(KEEP, resolve(lv.TIT, lv.place), n, lv.RIT, lv.RITl)
        for p in range(n):
            lv.PPT[p * SLOTS : (p + 1) * SLOTS, :] = one(lv.same & (lv.place == 0))
            lv.PPT[lanes + p * SLOTS : lanes + (p + 1) * SLOTS, :] = one(lv.same & (lv.place == lv.last))

    def setup_between():
        at = 4 * 64 + 4 * 8
        TP[...] = dot(c1_ref[at : at + 128, :], middle.hot).reshape(16, 8, 128)
        TPT[...] = dot(c1_ref[at + 128 : at + 256, :], middle.hot).reshape(8, 16, 128)
        PT1[...] = dot(c1_ref[at + 256 : at + 272, :], middle.hot).reshape(2, 8, 128)
        place1 = middle.place
        spread(KEEP, resolve(TP, place1), 16, RP, RPl)
        wide = jnp.concatenate([TPT[...], TPT[...]], axis=2)
        spread(KEEP, resolve(wide, fine.place), 8, RPT, RPTl)
        spread(KEEP, jnp.where(place1 == 0, PT1[0], jnp.where(place1 == 1, PT1[1], 0.0)), 8, RP1, RP1l)
        RPT1[...] = jnp.zeros(RPT1.shape, jnp.bfloat16)
        RPT1l[...] = jnp.zeros(RPT1l.shape, jnp.bfloat16)
        spread(KEEP, resolve(PT1, place1), 2, RPT1, RPT1l)

    def setup_middle():
        setup_first(middle, 1)
        setup_rest(middle, 1)
        setup_between()

    one = lambda cond: jnp.where(cond, 1.0, 0.0).astype(jnp.bfloat16)
    fine, middle = levels
    for load in loads[3:7]:
        load.wait()
    setup_first(fine, 0)

    loads[7].wait()
    for i in range(16):
        for t in range(3):
            XIN[i * SLOTS + t * 4 : i * SLOTS + t * 4 + 4, :] = res_ref[0, t, :, i * 256 : (i + 1) * 256]
        XIN[i * SLOTS + 12 : i * SLOTS + 16, :] = jnp.zeros((4, 256), jnp.float32)
    fine.R[...] = jnp.transpose(XIN[...]).reshape(16, 16, 256) * fine.X[...]

    pl.semaphore_wait(barrier, len(AROUND))
    pending = []
    lane1 = lane[:, :128]
    group1 = lane1 >> 5

    def gather_start(which, value, reach):
        source, landing = [(SBF, RBF), (SBR, RBR)][which]
        source[...] = value
        copies = {}
        for q, (dx, dg) in enumerate(AROUND):
            if abs(dx) + abs(dg) > reach:
                continue
            where = which * len(AROUND) + q
            copies[q] = pltpu.make_async_remote_copy(
                src_ref=source,
                dst_ref=landing.at[q],
                send_sem=wide_send.at[where],
                recv_sem=wide_recv.at[where],
                device_id=around[q],
                device_id_type=MESH,
            )
            copies[q].start()
            pending.append(copies[q])
        return copies

    def gather_end(which, value, reach, copies):
        landing = [RBF, RBR][which]
        for q in copies:
            copies[q].wait_recv()
        columns = []
        for column in range(-reach, reach + 1):
            total = value if column == 0 else None
            for q in copies:
                if -AROUND[q][0] == column:
                    total = landing[q] if total is None else total + landing[q]
            columns.append(total)
        return jnp.stack(columns)

    own_group = group1 == grp
    own_factors = jnp.concatenate(
        [jnp.where(own_group, entry[:, :128], 0.0) for entry in factor] + [jnp.zeros((4, 128), jnp.float32)], axis=0
    )
    factor_copies = gather_start(0, own_factors, REACH - 1)

    def send(number, direction, value, source, landing):
        source[...] = value
        where = number * 4 + direction
        copy = pltpu.make_async_remote_copy(
            src_ref=source,
            dst_ref=landing,
            send_sem=send_sem.at[where],
            recv_sem=recv_sem.at[where],
            device_id=targets[direction],
            device_id_type=MESH,
        )
        copy.start()
        pending.append(copy)
        return copy

    def towards_first(value, last):
        value = jnp.where(last, value, 0.0)
        return value + roll(value, -4) + roll(value, -8)

    def towards_last(value):
        return jnp.where(width == 1, value, jnp.where(width == 2, roll(value, 4), roll(value, 8)))

    def contract(table, source, first, count):
        total = None
        for k in range(table.shape[0]):
            term = table[k][None] * source[first : first + count, k : k + 1, :]
            total = term if total is None else total + term
        return total

    def apply_level(lv, slot_of, number, consume, meanwhile=None, near=None, defer=False):
        n, lanes = lv.n, lv.lanes
        flat = lv.V[...].reshape(n * n, lanes)
        high, low = split(flat)
        lv.U[...] = (dot(high, lv.PP[...]) + dot(low, lv.PP[...])).reshape(n, n, 2 * lanes)
        y0, z0 = lv.V[0], lv.V[:, 0, :]
        y1, z1 = jnp.zeros_like(y0), jnp.zeros_like(z0)
        for p in lv.last_range:
            here = lv.last == p
            y1 = jnp.where(here, lv.V[p], y1)
            z1 = jnp.where(here, lv.V[:, p, :], z1)
        turned = dot3(jnp.concatenate([z0, z1, y0, y1], axis=0), lv.RI, lv.RIl)
        lv.H[2:6] = turned.reshape(4, n, lanes)
        for f in range(2):
            total = None
            for j in range(n):
                term = lv.IL[j : j + 1, :] * lv.U[j, :, f * lanes : (f + 1) * lanes]
                total = term if total is None else total + term
            lv.H[f] = total
        lv.Q[...] = contract(lv.TI, lv.H, 0, 6)
        copies = []
        if near is None:
            outgoing = [lv.Q[0], lv.Q[1], lv.Q[2], towards_first(lv.Q[3], lv.at_last)]
            copies = [
                send(number, d, outgoing[d], lv.SB.at[slot_of, d], lv.RB.at[slot_of, d]) for d in range(4)
            ]
        if meanwhile is not None:
            meanwhile()
        lv.G[4] = lv.pair[...] * (lv.Q[4] - jnp.where(lv.row > 0, roll(lv.Q[5], 1), 0.0))
        lv.G[5] = lv.pair[...] * (lv.Q[5] - jnp.where(lv.row < 3, roll(lv.Q[4], -1), 0.0))
        back = contract(lv.TIT, lv.G, 4, 2).reshape(2 * n, lanes)
        back = dot3(back, lv.RIT, lv.RITl)
        y_back = [back[:n], back[n:]]
        lv.OUT[...] = (
            dot(high, lv.RS[...]) + dot(low, lv.RS[...]) + dot(high, lv.RSl[...])
        ).reshape(n, n, lanes)
        size = 4 if n == 16 else 8
        for a in range(0, n, size):
            block = slice(a, a + size)
            along_j, along_k = None, None
            for j in range(n):
                term = lv.TT[block, j : j + 1, :] * lv.V[j][None]
                along_j = term if along_j is None else along_j + term
            for k in range(n):
                term = lv.T[k][None] * lv.V[block, k : k + 1, :]
                along_k = term if along_k is None else along_k + term
            lv.OUT[block] = lv.WWW[block] * (
                lv.OUT[block] + lv.f[1] * along_j + lv.f[2] * along_k + lv.cm * lv.V[block]
            )
        lv.OUT[0] = lv.OUT[0] + y_back[0]
        for p in lv.last_range:
            lv.OUT[p] = lv.OUT[p] + jnp.where(lv.last == p, y_back[1], 0.0)
        if defer:
            lv.deferred, near = copies, [0.0] * 4
        else:
            for copy in copies:
                copy.wait_recv()
        pair = lv.pair[...]
        landed = lambda d: lv.RB[slot_of, d]
        if near is None:
            x_low, x_high, z_low, z_high = landed(1), landed(0), landed(3), towards_last(landed(2))
        else:
            x_low, x_high, z_low, z_high = near
        lv.G[0] = pair * (lv.Q[0] - x_low)
        lv.G[1] = pair * (lv.Q[1] - x_high)
        lv.G[2] = pair * (lv.Q[2] - jnp.where(lv.at_first, z_low, roll(lv.Q[3], 4)))
        lv.G[3] = pair * (lv.Q[3] - jnp.where(lv.at_last, z_high, roll(lv.Q[2], -4)))
        back = contract(lv.TIT, lv.G, 0, 4)
        for f in range(2):
            for j in range(n):
                lv.Y[j, :, f * lanes : (f + 1) * lanes] = lv.IL[j : j + 1, :] * back[f]
        lv.RZ[...] = dot3(back[2:4].reshape(2 * n, lanes), lv.RIT, lv.RITl).reshape(2, n, lanes)
        first, second = split(lv.Y[...].reshape(n * n, 2 * lanes))
        x_back = (dot(first, lv.PPT[...]) + dot(second, lv.PPT[...])).reshape(n, n, lanes)
        for j in range(n):
            z_back = lv.FM * lv.RZ[0, j : j + 1, :] + lv.LM * lv.RZ[1, j : j + 1, :]
            consume(j, lv.OUT[j] + x_back[j] + z_back)

    centre = 0.5 * (cheb_high + cheb_low)
    radius = 0.5 * (cheb_high - cheb_low)
    rho_first = radius / centre
    rho_next = 1.0 / (2.0 * centre / radius - rho_first)
    keep_d = 1.0 + rho_next * rho_first
    take_e = 2.0 * rho_next / radius

    def first_step(lv):
        lv.V[...] = lv.DINV[...] * lv.R[...] * (1.0 / centre)

    def end_pre(lv):
        def consume(j, applied):
            lv.V[j] = keep_d * lv.V[j] + take_e * lv.DINV[j] * (lv.R[j] - applied)

        return consume

    def remainder(lv):
        def consume(j, applied):
            lv.OUT[j] = lv.R[j] - applied

        return consume

    def begin_post(lv):
        def consume(j, applied):
            rest = lv.R[j] - applied
            lv.R[j] = rest
            lv.X[j] = lv.V[j]
            lv.V[j] = lv.DINV[j] * rest * (1.0 / centre)

        return consume

    def end_post(lv):
        def consume(j, applied):
            lv.V[j] = lv.X[j] + keep_d * lv.V[j] + take_e * lv.DINV[j] * (lv.R[j] - applied)

        return consume

    first_step(fine)
    apply_level(fine, 0, 0, end_pre(fine), lambda: setup_rest(fine, 0))
    apply_level(fine, 1, 1, remainder(fine), setup_middle)

    lanes_down = dot3(fine.OUT[...].reshape(256, 256), RP, RPl).reshape(16, 16, 128)
    total = None
    for j in range(16):
        term = TPT[:, j : j + 1, :] * lanes_down[j][None]
        total = term if total is None else total + term
    A8[...] = total
    middle.R[...] = contract(TP, A8, 0, 8)
    first_step(middle)
    apply_level(middle, 0, 2, end_pre(middle))
    apply_level(middle, 1, 3, remainder(middle), defer=True)

    parts = []
    for a in range(2):
        total = None
        for j in range(8):
            term = PT1[a, j : j + 1, :] * middle.OUT[j]
            total = term if total is None else total + term
        for b in range(2):
            parts.append(jnp.sum(PT1[b] * total, axis=0, keepdims=True))
    coarse_r = dot3(jnp.concatenate(parts + [jnp.zeros((4, 128), jnp.float32)], axis=0), RP1, RP1l)

    def placed(value):
        total = value
        for g in range(1, 4):
            total = jnp.where(grp == g, roll(value, 32 * g), total)
        return total

    def unplaced(value):
        total = value
        for g in range(1, 4):
            total = jnp.where(grp == g, roll(value, -32 * g), total)
        return jnp.where(lane1 < 32, total, 0.0)

    points = cheb_nodes(7)
    line2 = rows_iota(8, 128)
    along_lane, along_row = jnp.zeros((1, 128), jnp.float32), jnp.zeros((8, 128), jnp.float32)
    for b in range(8):
        along_lane = jnp.where((lane1 >> 4) == b, float(points[b]), along_lane)
        along_row = jnp.where(line2 == b, float(points[b]), along_row)
    lane_ends = [0.5 - 0.5 * along_lane, 0.5 + 0.5 * along_lane]
    row_ends = [0.5 - 0.5 * along_row, 0.5 + 0.5 * along_row]

    def row_sums(face):
        weighted = middle.pair[...] * middle.Q[face]
        return [jnp.sum(row_ends[end] * weighted, axis=0, keepdims=True) for end in range(2)]

    def group_sums(rows):
        total = jnp.concatenate(rows, axis=0)
        for shift in (16, 32, 64):
            total = total + roll(total, shift)
        return total

    def two_groups(low, high):
        return jnp.where(lane1 < 16, low, jnp.where(lane1 < 32, high, 0.0))

    x_rows = [lane_ends[j] * row_sums(f)[k] for f in range(2) for j in range(2) for k in range(2)]
    x_sums = group_sums(x_rows)
    z_rows = [lane_ends[i] * row_sums(2 + k)[j] for i in range(2) for j in range(2) for k in range(2)]
    z_sums = group_sums(z_rows)
    x_given = two_groups(x_sums[:4], x_sums[4:])
    z_given = two_groups(z_sums[:4], z_sums[4:])
    own_r = placed(jnp.concatenate([coarse_r[:4], x_given, z_given, jnp.zeros((4, 128), jnp.float32)], axis=0))
    r_copies = gather_start(1, own_r, REACH)

    fs = gather_end(0, own_factors, REACH - 1, factor_copies)
    f0, f1, f2, f3 = [fs[:, c : c + 1, :] for c in range(4)]
    low_i = ((lane1 >> 4) & 1) == 0
    low_j = line2 < 2
    low_k = (line2 & 1) == 0
    row2, layer2 = lane1 & 3, (lane1 >> 2) & 3
    width2, before2 = jnp.zeros((1, 128), jnp.int32), jnp.zeros((1, 128), jnp.int32)
    for g in range(4):
        width2 = jnp.where(group1 == g, widths_ref[g], width2)
        before2 = jnp.where(group1 == (g + 1) % 4, widths_ref[g], before2)
    s00, s01 = float(coarse["scaled"][0, 0, 0]), float(coarse["scaled"][0, 0, 1])
    w0 = float(coarse["quad_w"][0, 0])
    www = w0**3
    pair2 = float(coarse["pair"][0, 0])
    centre_coeff = www * (s00 * (f0 + f1 + f2) + mass_weight * f3) + 3.0 * pair2
    live2 = jnp.where((layer2 < width2) & (line2 < 4), 1.0, 0.0)[None]
    dinv2 = live2 / (centre_coeff + 1.0 - live2)
    f0, f1, f2 = [(www * s01) * entry for entry in (f0, f1, f2)]

    def sideways(value, shift):
        return roll(value.reshape(-1, 128), shift).reshape(value.shape)

    def next_layer(value):
        across = jnp.where(
            width2 == 1, sideways(value, -32), jnp.where(width2 == 2, sideways(value, -28), sideways(value, -24))
        )
        return jnp.where(layer2 < width2 - 1, sideways(value, -4), across)

    def last_layer(value):
        across = jnp.where(
            before2 == 1, sideways(value, 32), jnp.where(before2 == 2, sideways(value, 28), sideways(value, 24))
        )
        return jnp.where(layer2 > 0, sideways(value, 4), across)

    def other_k(value):
        return jnp.where(low_k, roll(value, -1, 1), roll(value, 1, 1))

    def coarse_apply(value, skip):
        mid = value[1:-1]
        part = slice(skip, COLUMNS - 2 - skip)
        flip_i = jnp.where(low_i, sideways(mid, -16), sideways(mid, 16))
        flip_j = jnp.where(low_j, roll(mid, -2, 1), roll(mid, 2, 1))
        flip_k = other_k(mid)
        near_x = jnp.where(low_i, sideways(value[:-2], -16), sideways(value[2:], 16))
        near_y = jnp.where(
            low_j,
            jnp.where(row2 > 0, sideways(flip_j, 1), 0.0),
            jnp.where(row2 < 3, sideways(flip_j, -1), 0.0),
        )
        near_z = jnp.where(low_k, last_layer(flip_k), next_layer(flip_k))
        return (
            centre_coeff[part] * mid
            + (f0[part] * flip_i + f1[part] * flip_j + f2[part] * flip_k)
            - pair2 * (near_x + near_y + near_z)
        )

    both = gather_end(1, own_r, REACH, r_copies)
    upper, lower = both[:, :8], both[:, 8:]
    given = roll(upper, 4, 1)
    rs = upper[1:-1] + jnp.where(low_i, sideways(given[:-2], -16), sideways(given[2:], 16))
    given = other_k(lower[1:-1])
    rs = rs + jnp.where(
        low_k,
        jnp.where(layer2 == 0, last_layer(given), 0.0),
        jnp.where(layer2 == width2 - 1, next_layer(given), 0.0),
    )
    d = dinv2 * rs * (1.0 / centre)
    xs = keep_d * d[1:-1] + take_e * dinv2[1:-1] * (rs[1:-1] - coarse_apply(d, 1))
    rest = rs[2:-2] - coarse_apply(xs, 2)
    d = dinv2[2:-2] * rest * (1.0 / centre)
    xs = xs[2:-2] + keep_d * d[1:-1] + take_e * dinv2[3:-3] * (rest[1:-1] - coarse_apply(d, 3))
    x = unplaced(xs[1])

    def all_lanes(value, end):
        value = jnp.where(lane1 < 16, roll(value, -16) if end else value, 0.0)
        value = value + roll(value, 16)
        value = value + roll(value, 32)
        return value + roll(value, 64)

    def x_trace(column, end):
        face = all_lanes(unplaced(column), end)
        total = 0.0
        for k in range(2):
            line = lane_ends[0] * face[k : k + 1, :] + lane_ends[1] * face[2 + k : 3 + k, :]
            total = total + row_ends[k] * line
        return total

    def z_trace(column, k):
        column = unplaced(column)
        face = lane_ends[0] * all_lanes(column, 0) + lane_ends[1] * all_lanes(column, 1)
        return row_ends[0] * face[k : k + 1, :] + row_ends[1] * face[2 + k : 3 + k, :]

    turned = other_k(xs[1:2])
    correction_traces = [
        x_trace(xs[0], 1),
        x_trace(xs[2], 0),
        z_trace(last_layer(turned)[0], 0),
        z_trace(next_layer(turned)[0], 1),
    ]
    for copy in middle.deferred:
        copy.wait_recv()
    before = [middle.RB[1, 1], middle.RB[1, 0], middle.RB[1, 3], towards_last(middle.RB[1, 2])]
    middle_near = [old + new for old, new in zip(before, correction_traces)]

    lifted = dot3(x, RPT1, RPT1l)
    columns = []
    for a in range(2):
        columns.append(PT1[0] * lifted[2 * a : 2 * a + 1, :] + PT1[1] * lifted[2 * a + 1 : 2 * a + 2, :])
    for j in range(8):
        middle.V[j] = middle.V[j] + PT1[0, j : j + 1, :] * columns[0] + PT1[1, j : j + 1, :] * columns[1]
    apply_level(middle, 2, None, begin_post(middle), near=middle_near)
    apply_level(middle, 3, 8, end_post(middle))

    C8[...] = contract(TPT, middle.V, 0, 8)
    for j0 in (0, 8):
        total = None
        for a in range(8):
            term = TP[j0 : j0 + 8, a : a + 1, :] * C8[a][None]
            total = term if total is None else total + term
        fine.U[j0 : j0 + 8, :, :128] = total
    lifted = dot3(fine.U[:, :, :128].reshape(256, 128), RPT, RPTl)
    fine.V[...] = fine.V[...] + lifted.reshape(16, 16, 256)
    apply_level(fine, 2, 9, begin_post(fine))
    apply_level(fine, 3, 10, end_post(fine))

    XIN[...] = jnp.transpose(fine.V[...].reshape(256, 256))
    for i in range(16):
        for t in range(3):
            out_ref[0, t, :, i * 256 : (i + 1) * 256] = XIN[i * SLOTS + t * 4 : i * SLOTS + t * 4 + 4, :]
    for copy in pending:
        copy.wait_send()


def scratch(given):
    f32, b16 = jnp.float32, jnp.bfloat16
    shapes = []
    for n in (16, 8):
        lanes = n * SLOTS
        shapes += [((n, n, lanes), f32)] * 4
        shapes += [((lanes, lanes), b16)] * 6 + [((lanes, 2 * lanes), b16), ((2 * lanes, lanes), b16)]
        shapes += [((n, lanes), f32)] + [((n, n, lanes), f32)] * 6
        shapes += [((6, n, lanes), f32)] * 3 + [((2, n, lanes), f32)]
        shapes += [((n, n, 2 * lanes), f32)] * 2 + [((4, 4, n, lanes), f32)] * 2
    shapes += [((16, 8, 128), f32), ((8, 16, 128), f32), ((2, 8, 128), f32)]
    shapes += [((256, 128), b16)] * 2 + [((128, 256), b16)] * 2 + [((128, 128), b16)] * 4
    shapes += [((8, 16, 128), f32)] * 2 + [((8, 128), f32), ((len(AROUND), 8, 128), f32)]
    shapes += [((16, 128), f32), ((len(AROUND), 16, 128), f32)]
    shapes += [((16, 256), f32), ((256, 256), f32)]
    semaphores = [pltpu.SemaphoreType.DMA((44,))] * 2 + [pltpu.SemaphoreType.DMA((8,))]
    semaphores += [pltpu.SemaphoreType.DMA((2 * len(AROUND),))] * 2
    landings = [pltpu.SMEM(x.shape, x.dtype) for x in given[:3]] + [pltpu.VMEM(x.shape, x.dtype) for x in given[3:]]
    return landings + [pltpu.VMEM(shape, dtype) for shape, dtype in shapes] + semaphores


def shards(residual, orders, factors, widths):
    c0, c1, pair0, pair1, taus, coarse = constants()
    given = [
        widths,
        jnp.transpose(orders, (2, 0, 1)),
        jnp.transpose(factors, (0, 2, 1, 3)),
        jnp.asarray(c0),
        jnp.asarray(c1),
        jnp.asarray(pair0),
        jnp.asarray(pair1),
        jnp.transpose(residual, (0, 2, 1, 3)),
    ]
    out = pl.pallas_call(
        functools.partial(kernel, taus, coarse),
        out_shape=jax.ShapeDtypeStruct((1, 3, 4, 4096), jnp.float32),
        in_specs=[pl.BlockSpec(memory_space=pltpu.HBM)] * 8,
        out_specs=pl.BlockSpec(memory_space=pltpu.VMEM),
        scratch_shapes=scratch(given),
        compiler_params=pltpu.CompilerParams(
            collective_id=0, has_side_effects=True, vmem_limit_bytes=62 * 1024 * 1024
        ),
    )(*given)
    return jnp.transpose(out, (0, 2, 1, 3))


def solution(mesh):
    return jax.shard_map(
        shards,
        mesh=mesh,
        in_specs=(
            P("dom", None, "grp", None),
            P("dom", None, "grp"),
            P("dom", None, "grp", None),
            P(),
        ),
        out_specs=P("dom", None, "grp", None),
        check_vma=False,
    )
```

```python
import functools

import jax
import jax.numpy as jnp
import ml_dtypes
import numpy as np
from jax import lax
from jax.experimental import pallas as pl
from jax.experimental.pallas import tpu as pltpu
from jax.sharding import PartitionSpec as P

MESH = pl.DeviceIdType.MESH
SLOTS = 16
REACH = 5
COLUMNS = 2 * REACH + 1
AROUND = sorted(
    [
        (dx, dg)
        for dx in range(-REACH, REACH + 1)
        for dg in (0, 1, -1, 2)
        if (dx, dg) != (0, 0) and abs(dg) <= REACH - abs(dx)
    ],
    key=lambda place: -(abs(place[0]) + 3 * abs(place[1])),
)
mass_weight = 0.5
penalty = 0.5
cheb_high = 4.0
cheb_low = 0.15


def cheb_nodes(degree):
    return -np.cos(np.pi * np.arange(degree + 1) / degree)


def bary_weights(npoints):
    weights = (-1.0) ** np.arange(npoints)
    weights[0] = 0.5 * weights[0]
    weights[-1] = 0.5 * weights[-1]
    return weights


def lagrange_table(source, target):
    weights = bary_weights(source.shape[0])
    spacing = target[:, None] - source[None, :]
    coincide = np.abs(spacing) < 1e-12
    fractions = weights[None, :] / np.where(coincide, 1.0, spacing)
    lookup = fractions / fractions.sum(axis=1, keepdims=True)
    return np.where(coincide.any(axis=1, keepdims=True), np.where(coincide, 1.0, 0.0), lookup)


def quad_weights(degree):
    weights = np.full(degree + 1, np.pi / degree)
    weights[0] = 0.5 * weights[0]
    weights[-1] = 0.5 * weights[-1]
    return weights


def derivative(degree):
    points = cheb_nodes(degree)
    weights = bary_weights(degree + 1)
    spacing = points[:, None] - points[None, :] + np.eye(degree + 1)
    lookup = weights[None, :] / weights[:, None] / spacing
    lookup = lookup * (1.0 - np.eye(degree + 1))
    return lookup - np.eye(degree + 1) * lookup.sum(axis=1)[:, None]


def level_degree(degree, level_index):
    return [degree, degree // 2, 1][level_index]


def split3(table):
    high = table.astype(ml_dtypes.bfloat16)
    rest = table - high.astype(np.float64)
    middle = rest.astype(ml_dtypes.bfloat16)
    low = (rest - middle.astype(np.float64)).astype(ml_dtypes.bfloat16)
    return high, middle, low


def packed(tables):
    rows = np.concatenate([entry.reshape(9, -1) for entry in tables], axis=1).T
    return np.concatenate(list(split3(rows)) + [np.zeros((rows.shape[0], 5), ml_dtypes.bfloat16)], axis=1)


def order_tables(level_index):
    points = [16, 8, 2][level_index]
    common = cheb_nodes(points - 1)
    common_w = quad_weights(points - 1)
    names = ("scaled", "stiff_diag", "quad_w", "interpolate", "face_diag", "living", "prolong")
    table = {name: [] for name in names}
    for degree in range(7, 16):
        local = level_degree(degree, level_index)
        quad = quad_weights(local)
        deriv = derivative(local)
        stiff = deriv.T @ (quad[:, None] * deriv)
        scaled = np.zeros((points, points))
        scaled[: local + 1, : local + 1] = stiff / quad[:, None]
        padded = lambda vector: np.concatenate([vector, np.zeros(points - local - 1)])
        interp = np.zeros((points, points))
        interp[:, : local + 1] = lagrange_table(cheb_nodes(local), common)
        table["scaled"].append(scaled)
        table["stiff_diag"].append(padded(np.diagonal(stiff)))
        table["quad_w"].append(padded(quad))
        table["interpolate"].append(interp)
        table["face_diag"].append((common_w[:, None] * interp**2).sum(axis=0))
        table["living"].append(padded(np.ones(local + 1)))
        if level_index < 2:
            coarse = level_degree(degree, level_index + 1)
            lift = np.zeros((points, [16, 8, 2][level_index + 1]))
            lift[: local + 1, : coarse + 1] = lagrange_table(cheb_nodes(coarse), cheb_nodes(local))
            table["prolong"].append(lift)
    table = {name: np.stack(table[name]) for name in names if table[name]}
    tau = penalty * (points - 1) ** 2
    table["pair"] = tau * np.outer(common_w, common_w)
    table["tau"] = tau
    return table


def flip(table):
    return np.swapaxes(table, 1, 2)


def constants():
    fine, middle, coarse = [order_tables(level_index) for level_index in range(3)]
    vectors = ("quad_w", "face_diag", "living", "stiff_diag")
    matrices = lambda t: [flip(t["scaled"]), t["scaled"], flip(t["interpolate"]), t["interpolate"]]
    c0 = packed(matrices(fine) + [fine[name] for name in vectors])
    c1 = packed(
        matrices(middle)
        + [middle[name] for name in vectors]
        + [fine["prolong"], flip(fine["prolong"]), flip(middle["prolong"])]
    )
    pairs = [np.repeat(t["pair"], SLOTS, axis=1).astype(np.float32) for t in (fine, middle)]
    lift = lagrange_table(cheb_nodes(7), cheb_nodes(15))
    wide = np.kron(lift, np.eye(SLOTS))
    blank = lambda table, rows, cols: np.pad(table, ((0, rows - table.shape[0]), (0, cols - table.shape[1])))
    lifts = []
    for table in (blank(lift, 16, 16), blank(lift.T, 16, 16), wide, wide.T):
        high = table.astype(ml_dtypes.bfloat16)
        lifts += [high, (table - high.astype(np.float64)).astype(ml_dtypes.bfloat16)]
    return lifts, c0, c1, pairs[0], pairs[1], (fine["tau"], middle["tau"]), coarse


def split(values):
    high = values.astype(jnp.bfloat16)
    return high, (values - high.astype(jnp.float32)).astype(jnp.bfloat16)


def dot(left, right):
    return jnp.dot(left, right, preferred_element_type=jnp.float32)


def dot3(values, high, low):
    first, second = split(values)
    return dot(first, high[...]) + dot(second, high[...]) + dot(first, low[...])


def roll(values, shift, axis=-1):
    axis = axis % values.ndim
    return pltpu.roll(values, shift % values.shape[axis], axis)


def lanes_iota(lanes):
    return lax.broadcasted_iota(jnp.int32, (1, lanes), 1)


def rows_iota(rows, lanes):
    return lax.broadcasted_iota(jnp.int32, (rows, lanes), 0)


class Level:
    pass


def resolve(table, place):
    own = lax.broadcasted_iota(jnp.int32, table.shape[1:], 0) == place
    return jnp.sum(jnp.where(own[None], table[...], 0.0), axis=1)


def spread(keep, rows, count, target, low=None):
    keep[: rows.shape[0], : rows.shape[1]] = rows
    lanes = rows.shape[1]
    same = rows_iota(SLOTS, lanes) == (lanes_iota(lanes) & (SLOTS - 1))
    for p in range(count):
        block = jnp.where(same, keep[p : p + 1, :lanes], 0.0)
        high = block.astype(jnp.bfloat16)
        target[p * SLOTS : (p + 1) * SLOTS, :] = high
        if low is not None:
            low[p * SLOTS : (p + 1) * SLOTS, :] = (block - high.astype(jnp.float32)).astype(jnp.bfloat16)


def kernel(taus, coarse, *refs):
    names = iter(refs)
    take = lambda count: [next(names) for _ in range(count)]
    given = take(16)
    (out_ref,) = take(1)
    widths_ref, orders_ref, factors_ref, c0_ref, c1_ref, pair0_ref, pair1_ref, res_ref = take(8)
    lift_refs = take(8)
    levels = []
    for index in range(2):
        lv = Level()
        lv.n = [16, 8][index]
        lv.lanes = lv.n * SLOTS
        (lv.T, lv.TT, lv.TI, lv.TIT) = take(4)
        (lv.RS, lv.RSl, lv.RI, lv.RIl, lv.RIT, lv.RITl, lv.PP, lv.PPT) = take(8)
        (lv.IL, lv.DINV, lv.WWW, lv.R, lv.X, lv.V, lv.OUT) = take(7)
        (lv.H, lv.Q, lv.G, lv.RZ, lv.U, lv.Y, lv.SB, lv.RB) = take(8)
        lv.pair = [pair0_ref, pair1_ref][index]
        levels.append(lv)
    TP, TPT, PT1, RP, RPl, RPT, RPTl, RP1, RP1l, RPT1, RPT1l, A8, C8, SBF, RBF, SBR, RBR, KEEP, XIN = take(19)
    send_sem, recv_sem, load_sem, wide_send, wide_recv = take(5)
    landings = [widths_ref, orders_ref, factors_ref, c0_ref, c1_ref, pair0_ref, pair1_ref, res_ref] + lift_refs
    loads = [pltpu.make_async_copy(*pair, load_sem.at[i]) for i, pair in enumerate(zip(given, landings))]
    for load in loads:
        load.start()

    dom, grp = lax.axis_index("dom"), lax.axis_index("grp")
    n_dom, n_grp = lax.axis_size("dom"), lax.axis_size("grp")
    targets = [
        {"dom": lax.rem(dom + n_dom - 1, n_dom)},
        {"dom": lax.rem(dom + 1, n_dom)},
        {"grp": lax.rem(grp + n_grp - 1, n_grp)},
        {"grp": lax.rem(grp + 1, n_grp)},
    ]
    barrier = pltpu.get_barrier_semaphore()
    around = [
        {"dom": lax.rem(dom + n_dom + dx, n_dom), "grp": lax.rem(grp + n_grp + dg, n_grp)} for dx, dg in AROUND
    ]
    for target in around:
        pl.semaphore_signal(barrier, inc=1, device_id=target, device_id_type=MESH)

    lane = lanes_iota(16 * SLOTS)
    slot = lane & (SLOTS - 1)
    layer = slot >> 2
    row = slot & 3
    for load in loads[:3]:
        load.wait()
    width = jnp.int32(0)
    for g in range(4):
        width = jnp.where(grp == g, widths_ref[g], width)
    order = jnp.full(lane.shape, 7, jnp.int32)
    factor = [jnp.full(lane.shape, 1.0, jnp.float32) for _ in range(4)]
    for r in range(4):
        for t in range(3):
            here = slot == t * 4 + r
            order = jnp.where(here, orders_ref[t, 0, r], order)
            for c in range(4):
                factor[c] = jnp.where(here, factors_ref[0, t, r, c], factor[c])
    alive = layer < width
    mask = jnp.where(alive, 1.0, 0.0)
    at_first = layer == 0
    at_last = layer == width - 1
    line = rows_iota(32, 16 * SLOTS)
    line = jnp.where(line < 9, line, jnp.where(line < 18, line - 9, jnp.where(line < 27, line - 18, -1)))
    onehot = jnp.where(line == order - 7, 1.0, 0.0).astype(jnp.bfloat16)

    def tables(lv, index, which):
        refs = (lv.TI, lv.TIT, lv.T, lv.TT)
        source = [c0_ref, c1_ref][index]
        size = lv.n * lv.n
        at = (2, 3, 0, 1)[which] * size
        refs[which][...] = dot(source[at : at + size, :], lv.hot).reshape(lv.n, lv.n, lv.lanes)

    def setup_first(lv, index):
        n, lanes = lv.n, lv.lanes
        lv.place = lane[:, :lanes] >> 4
        lv.last = [order, order >> 1][index][:, :lanes]
        lv.f = [entry[:, :lanes] for entry in factor]
        lv.cm = lv.f[3] * mass_weight
        lv.at_first, lv.at_last = at_first[:, :lanes], at_last[:, :lanes]
        lv.row = row[:, :lanes]
        lv.last_range = [range(7, 16), range(3, 8)][index]
        lv.hot = onehot[:, :lanes]
        tables(lv, index, 0)
        at = 4 * n * n
        vectors = dot([c0_ref, c1_ref][index][at : at + 4 * n, :], lv.hot)
        quad, face, live, stiff = [vectors[i * n : (i + 1) * n] for i in range(4)]
        inter = resolve(lv.TI, lv.place)
        lv.IL[...] = inter
        spread(KEEP, inter, n, lv.RI, lv.RIl)
        points = rows_iota(n, lanes)
        lv.FM = jnp.where(points == 0, 1.0, 0.0)
        lv.LM = jnp.where(points == lv.last, 1.0, 0.0)
        lv.same = rows_iota(SLOTS, lanes) == (lane[:, :lanes] & (SLOTS - 1))
        for p in range(n):
            rows = slice(p * SLOTS, (p + 1) * SLOTS)
            lv.PP[rows, :lanes] = one(lv.same) if p == 0 else jnp.zeros((SLOTS, lanes), jnp.bfloat16)
            lv.PP[rows, lanes:] = one(lv.same & (lv.last == p))
        pick = lambda table: jnp.sum(jnp.where(points == lv.place, table, 0.0), axis=0, keepdims=True)
        w_i, face_i, live_i, stiff_i = pick(quad), pick(face), pick(live) * mask[:, :lanes], pick(stiff)
        ends = lv.FM + lv.LM
        ends_i = pick(ends)
        f0, f1, f2, _ = lv.f
        for j in range(n):
            one_row = lambda table: table[j : j + 1, :]
            w_j, face_j, live_j, stiff_j, ends_j = [one_row(t) for t in (quad, face, live, stiff, ends)]
            www = (w_i * w_j) * quad
            diagonal = (
                (f0 * stiff_i * w_j) * quad
                + (f1 * w_i * stiff_j) * quad
                + (f2 * w_i * w_j) * stiff
                + lv.cm * www
                + taus[index] * ((ends_j * face_i + face_j * ends_i) * face + (face_j * face_i) * ends)
            )
            node_live = (live_j * live_i) * live
            lv.WWW[j] = www
            lv.DINV[j] = node_live / (diagonal + 1.0 - node_live)
            if index == 0:
                lv.X[j] = node_live

    def setup_rest(lv, index):
        n, lanes = lv.n, lv.lanes
        for which in (1, 2, 3):
            tables(lv, index, which)
        spread(KEEP, resolve(lv.T, lv.place) * lv.f[0], n, lv.RS, lv.RSl)
        spread(KEEP, resolve(lv.TIT, lv.place), n, lv.RIT, lv.RITl)
        for p in range(n):
            lv.PPT[p * SLOTS : (p + 1) * SLOTS, :] = one(lv.same & (lv.place == 0))
            lv.PPT[lanes + p * SLOTS : lanes + (p + 1) * SLOTS, :] = one(lv.same & (lv.place == lv.last))

    def setup_between():
        at = 4 * 64 + 4 * 8
        TP[...] = dot(c1_ref[at : at + 128, :], middle.hot).reshape(16, 8, 128)
        TPT[...] = dot(c1_ref[at + 128 : at + 256, :], middle.hot).reshape(8, 16, 128)
        PT1[...] = dot(c1_ref[at + 256 : at + 272, :], middle.hot).reshape(2, 8, 128)
        place1 = middle.place
        spread(KEEP, resolve(TP, place1), 16, RP, RPl)
        wide = jnp.concatenate([TPT[...], TPT[...]], axis=2)
        spread(KEEP, resolve(wide, fine.place), 8, RPT, RPTl)
        spread(KEEP, jnp.where(place1 == 0, PT1[0], jnp.where(place1 == 1, PT1[1], 0.0)), 8, RP1, RP1l)
        RPT1[...] = jnp.zeros(RPT1.shape, jnp.bfloat16)
        RPT1l[...] = jnp.zeros(RPT1l.shape, jnp.bfloat16)
        spread(KEEP, resolve(PT1, place1), 2, RPT1, RPT1l)

    def setup_middle():
        setup_first(middle, 1)
        setup_rest(middle, 1)
        setup_between()

    one = lambda cond: jnp.where(cond, 1.0, 0.0).astype(jnp.bfloat16)
    fine, middle = levels
    for load in loads[3:7]:
        load.wait()
    setup_first(fine, 0)

    loads[7].wait()
    for i in range(16):
        for t in range(3):
            XIN[i * SLOTS + t * 4 : i * SLOTS + t * 4 + 4, :] = res_ref[0, t, :, i * 256 : (i + 1) * 256]
        XIN[i * SLOTS + 12 : i * SLOTS + 16, :] = jnp.zeros((4, 256), jnp.float32)
    fine.R[...] = jnp.transpose(XIN[...]).reshape(16, 16, 256) * fine.X[...]

    pl.semaphore_wait(barrier, len(AROUND))
    pending = []
    lane1 = lane[:, :128]
    group1 = lane1 >> 5

    def gather_start(which, value, reach):
        source, landing = [(SBF, RBF), (SBR, RBR)][which]
        source[...] = value
        copies = {}
        for q, (dx, dg) in enumerate(AROUND):
            if abs(dx) + abs(dg) > reach:
                continue
            where = which * len(AROUND) + q
            copies[q] = pltpu.make_async_remote_copy(
                src_ref=source,
                dst_ref=landing.at[q],
                send_sem=wide_send.at[where],
                recv_sem=wide_recv.at[where],
                device_id=around[q],
                device_id_type=MESH,
            )
            copies[q].start()
            pending.append(copies[q])
        return copies

    def gather_end(which, value, reach, copies):
        landing = [RBF, RBR][which]
        for q in copies:
            copies[q].wait_recv()
        columns = []
        for column in range(-reach, reach + 1):
            total = value if column == 0 else None
            for q in copies:
                if -AROUND[q][0] == column:
                    total = landing[q] if total is None else total + landing[q]
            columns.append(total)
        return jnp.stack(columns)

    own_group = group1 == grp
    own_factors = jnp.concatenate(
        [jnp.where(own_group, entry[:, :128], 0.0) for entry in factor] + [jnp.zeros((4, 128), jnp.float32)], axis=0
    )
    factor_copies = {}

    def send(number, direction, value, source, landing):
        source[...] = value
        where = number * 4 + direction
        copy = pltpu.make_async_remote_copy(
            src_ref=source,
            dst_ref=landing,
            send_sem=send_sem.at[where],
            recv_sem=recv_sem.at[where],
            device_id=targets[direction],
            device_id_type=MESH,
        )
        copy.start()
        pending.append(copy)
        return copy

    def towards_first(value, last):
        value = jnp.where(last, value, 0.0)
        return value + roll(value, -4) + roll(value, -8)

    def towards_last(value):
        return jnp.where(width == 1, value, jnp.where(width == 2, roll(value, 4), roll(value, 8)))

    def contract(table, source, first, count):
        total = None
        for k in range(table.shape[0]):
            term = table[k][None] * source[first : first + count, k : k + 1, :]
            total = term if total is None else total + term
        return total

    def give_back(lv):
        n, lanes = lv.n, lv.lanes
        back = contract(lv.TIT, lv.G, 0, 4)
        for f in range(2):
            for j in range(n):
                lv.Y[j, :, f * lanes : (f + 1) * lanes] = lv.IL[j : j + 1, :] * back[f]
        lv.RZ[...] = dot3(back[2:4].reshape(2 * n, lanes), lv.RIT, lv.RITl).reshape(2, n, lanes)
        first, second = split(lv.Y[...].reshape(n * n, 2 * lanes))
        x_back = (dot(first, lv.PPT[...]) + dot(second, lv.PPT[...])).reshape(n, n, lanes)
        return x_back, lambda j: lv.FM * lv.RZ[0, j : j + 1, :] + lv.LM * lv.RZ[1, j : j + 1, :]

    def apply_level(lv, slot_of, number, consume, meanwhile=None, near=None, defer=False, lead=False):
        n, lanes = lv.n, lv.lanes
        flat = lv.V[...].reshape(n * n, lanes)
        high, low = split(flat)
        lv.U[...] = (dot(high, lv.PP[...]) + dot(low, lv.PP[...])).reshape(n, n, 2 * lanes)
        y0, z0 = lv.V[0], lv.V[:, 0, :]
        y1, z1 = jnp.zeros_like(y0), jnp.zeros_like(z0)
        for p in lv.last_range:
            here = lv.last == p
            y1 = jnp.where(here, lv.V[p], y1)
            z1 = jnp.where(here, lv.V[:, p, :], z1)
        turned = dot3(jnp.concatenate([z0, z1, y0, y1], axis=0), lv.RI, lv.RIl)
        lv.H[2:6] = turned.reshape(4, n, lanes)
        for f in range(2):
            total = None
            for j in range(n):
                term = lv.IL[j : j + 1, :] * lv.U[j, :, f * lanes : (f + 1) * lanes]
                total = term if total is None else total + term
            lv.H[f] = total
        lv.Q[...] = contract(lv.TI, lv.H, 0, 6)
        copies = []
        if near is None:
            outgoing = [lv.Q[0], lv.Q[1], lv.Q[2], towards_first(lv.Q[3], lv.at_last)]
            copies = [
                send(number, d, outgoing[d], lv.SB.at[slot_of, d], lv.RB.at[slot_of, d]) for d in range(4)
            ]
        if lead:
            return copies
        if meanwhile is not None:
            meanwhile()
        lv.G[4] = lv.pair[...] * (lv.Q[4] - jnp.where(lv.row > 0, roll(lv.Q[5], 1), 0.0))
        lv.G[5] = lv.pair[...] * (lv.Q[5] - jnp.where(lv.row < 3, roll(lv.Q[4], -1), 0.0))
        back = contract(lv.TIT, lv.G, 4, 2).reshape(2 * n, lanes)
        back = dot3(back, lv.RIT, lv.RITl)
        y_back = [back[:n], back[n:]]
        lv.OUT[...] = (
            dot(high, lv.RS[...]) + dot(low, lv.RS[...]) + dot(high, lv.RSl[...])
        ).reshape(n, n, lanes)
        size = 4 if n == 16 else 8
        for a in range(0, n, size):
            block = slice(a, a + size)
            along_j, along_k = None, None
            for j in range(n):
                term = lv.TT[block, j : j + 1, :] * lv.V[j][None]
                along_j = term if along_j is None else along_j + term
            for k in range(n):
                term = lv.T[k][None] * lv.V[block, k : k + 1, :]
                along_k = term if along_k is None else along_k + term
            lv.OUT[block] = lv.WWW[block] * (
                lv.OUT[block] + lv.f[1] * along_j + lv.f[2] * along_k + lv.cm * lv.V[block]
            )
        lv.OUT[0] = lv.OUT[0] + y_back[0]
        for p in lv.last_range:
            lv.OUT[p] = lv.OUT[p] + jnp.where(lv.last == p, y_back[1], 0.0)
        if defer:
            lv.deferred, near = copies, [0.0] * 4
        else:
            for copy in copies:
                copy.wait_recv()
        pair = lv.pair[...]
        landed = lambda d: lv.RB[slot_of, d]
        if near is None:
            x_low, x_high, z_low, z_high = landed(1), landed(0), landed(3), towards_last(landed(2))
        else:
            x_low, x_high, z_low, z_high = near() if callable(near) else near
        lv.G[0] = pair * (lv.Q[0] - x_low)
        lv.G[1] = pair * (lv.Q[1] - x_high)
        lv.G[2] = pair * (lv.Q[2] - jnp.where(lv.at_first, z_low, roll(lv.Q[3], 4)))
        lv.G[3] = pair * (lv.Q[3] - jnp.where(lv.at_last, z_high, roll(lv.Q[2], -4)))
        x_back, z_back = give_back(lv)
        for j in range(n):
            consume(j, lv.OUT[j] + x_back[j] + z_back(j))

    centre = 0.5 * (cheb_high + cheb_low)
    radius = 0.5 * (cheb_high - cheb_low)
    rho_first = radius / centre
    rho_next = 1.0 / (2.0 * centre / radius - rho_first)
    keep_d = 1.0 + rho_next * rho_first
    take_e = 2.0 * rho_next / radius

    def first_step(lv):
        lv.V[...] = lv.DINV[...] * lv.R[...] * (1.0 / centre)

    def end_pre(lv):
        def consume(j, applied):
            lv.V[j] = keep_d * lv.V[j] + take_e * lv.DINV[j] * (lv.R[j] - applied)

        return consume

    def remainder(lv):
        def consume(j, applied):
            lv.OUT[j] = lv.R[j] - applied

        return consume

    def begin_post(lv):
        def consume(j, applied):
            rest = lv.R[j] - applied
            lv.R[j] = rest
            lv.X[j] = lv.V[j]
            lv.V[j] = lv.DINV[j] * rest * (1.0 / centre)

        return consume

    def end_post(lv):
        def consume(j, applied):
            lv.V[j] = lv.X[j] + keep_d * lv.V[j] + take_e * lv.DINV[j] * (lv.R[j] - applied)

        return consume

    def after_first_send():
        for load in loads[8:]:
            load.wait()
        factor_copies.update(gather_start(0, own_factors, REACH - 1))
        setup_rest(fine, 0)

    first_step(fine)
    apply_level(fine, 0, 0, end_pre(fine), after_first_send)
    apply_level(fine, 1, 1, remainder(fine), setup_middle, defer=True)

    lanes_down = dot3(fine.OUT[...].reshape(256, 256), RP, RPl).reshape(16, 16, 128)
    total = None
    for j in range(16):
        term = TPT[:, j : j + 1, :] * lanes_down[j][None]
        total = term if total is None else total + term
    A8[...] = total
    middle.R[...] = contract(TP, A8, 0, 8)

    def on_rows(high, low, values):
        first, second = split(values)
        return dot(high[...], first) + dot(high[...], second) + dot(low[...], first)

    for copy in fine.deferred:
        copy.wait_recv()
    z_low = jnp.where(fine.at_first, fine.RB[1, 3], 0.0)
    z_high = jnp.where(fine.at_last, towards_last(fine.RB[1, 2]), 0.0)
    near_faces = [fine.pair[...] * value for value in (fine.RB[1, 1], fine.RB[1, 0], z_low, z_high)]
    near_faces = on_rows(lift_refs[2], lift_refs[3], jnp.concatenate(near_faces, axis=1))[:8]
    near_faces = jnp.concatenate([near_faces[:, f * 256 : (f + 1) * 256] for f in range(4)], axis=0)
    middle.G[0:4] = dot3(near_faces, lift_refs[4], lift_refs[5]).reshape(4, 8, 128)
    x_back, z_back = give_back(middle)
    for j in range(8):
        middle.R[j] = middle.R[j] + x_back[j] + z_back(j)
    first_step(middle)
    apply_level(middle, 0, 2, end_pre(middle))
    apply_level(middle, 1, 3, remainder(middle), defer=True)

    parts = []
    for a in range(2):
        total = None
        for j in range(8):
            term = PT1[a, j : j + 1, :] * middle.OUT[j]
            total = term if total is None else total + term
        for b in range(2):
            parts.append(jnp.sum(PT1[b] * total, axis=0, keepdims=True))
    coarse_r = dot3(jnp.concatenate(parts + [jnp.zeros((4, 128), jnp.float32)], axis=0), RP1, RP1l)

    def placed(value):
        total = value
        for g in range(1, 4):
            total = jnp.where(grp == g, roll(value, 32 * g), total)
        return total

    def unplaced(value):
        total = value
        for g in range(1, 4):
            total = jnp.where(grp == g, roll(value, -32 * g), total)
        return jnp.where(lane1 < 32, total, 0.0)

    points = cheb_nodes(7)
    line2 = rows_iota(8, 128)
    along_lane, along_row = jnp.zeros((1, 128), jnp.float32), jnp.zeros((8, 128), jnp.float32)
    for b in range(8):
        along_lane = jnp.where((lane1 >> 4) == b, float(points[b]), along_lane)
        along_row = jnp.where(line2 == b, float(points[b]), along_row)
    lane_ends = [0.5 - 0.5 * along_lane, 0.5 + 0.5 * along_lane]
    row_ends = [0.5 - 0.5 * along_row, 0.5 + 0.5 * along_row]

    def row_sums(face):
        weighted = middle.pair[...] * middle.Q[face]
        return [jnp.sum(row_ends[end] * weighted, axis=0, keepdims=True) for end in range(2)]

    def group_sums(rows):
        total = jnp.concatenate(rows, axis=0)
        for shift in (16, 32, 64):
            total = total + roll(total, shift)
        return total

    def two_groups(low, high):
        return jnp.where(lane1 < 16, low, jnp.where(lane1 < 32, high, 0.0))

    x_rows = [lane_ends[j] * row_sums(f)[k] for f in range(2) for j in range(2) for k in range(2)]
    x_sums = group_sums(x_rows)
    z_rows = [lane_ends[i] * row_sums(2 + k)[j] for i in range(2) for j in range(2) for k in range(2)]
    z_sums = group_sums(z_rows)
    x_given = two_groups(x_sums[:4], x_sums[4:])
    z_given = two_groups(z_sums[:4], z_sums[4:])
    own_r = placed(jnp.concatenate([coarse_r[:4], x_given, z_given, jnp.zeros((4, 128), jnp.float32)], axis=0))
    r_copies = gather_start(1, own_r, REACH)

    fs = gather_end(0, own_factors, REACH - 1, factor_copies)
    f0, f1, f2, f3 = [fs[:, c : c + 1, :] for c in range(4)]
    low_i = ((lane1 >> 4) & 1) == 0
    low_j = line2 < 2
    low_k = (line2 & 1) == 0
    row2, layer2 = lane1 & 3, (lane1 >> 2) & 3
    width2, before2 = jnp.zeros((1, 128), jnp.int32), jnp.zeros((1, 128), jnp.int32)
    for g in range(4):
        width2 = jnp.where(group1 == g, widths_ref[g], width2)
        before2 = jnp.where(group1 == (g + 1) % 4, widths_ref[g], before2)
    s00, s01 = float(coarse["scaled"][0, 0, 0]), float(coarse["scaled"][0, 0, 1])
    w0 = float(coarse["quad_w"][0, 0])
    www = w0**3
    pair2 = float(coarse["pair"][0, 0])
    centre_coeff = www * (s00 * (f0 + f1 + f2) + mass_weight * f3) + 3.0 * pair2
    live2 = jnp.where((layer2 < width2) & (line2 < 4), 1.0, 0.0)[None]
    dinv2 = live2 / (centre_coeff + 1.0 - live2)
    f0, f1, f2 = [(www * s01) * entry for entry in (f0, f1, f2)]

    def sideways(value, shift):
        return roll(value.reshape(-1, 128), shift).reshape(value.shape)

    def next_layer(value):
        across = jnp.where(
            width2 == 1, sideways(value, -32), jnp.where(width2 == 2, sideways(value, -28), sideways(value, -24))
        )
        return jnp.where(layer2 < width2 - 1, sideways(value, -4), across)

    def last_layer(value):
        across = jnp.where(
            before2 == 1, sideways(value, 32), jnp.where(before2 == 2, sideways(value, 28), sideways(value, 24))
        )
        return jnp.where(layer2 > 0, sideways(value, 4), across)

    def other_k(value):
        return jnp.where(low_k, roll(value, -1, 1), roll(value, 1, 1))

    def coarse_apply(value, skip):
        mid = value[1:-1]
        part = slice(skip, COLUMNS - 2 - skip)
        flip_i = jnp.where(low_i, sideways(mid, -16), sideways(mid, 16))
        flip_j = jnp.where(low_j, roll(mid, -2, 1), roll(mid, 2, 1))
        flip_k = other_k(mid)
        near_x = jnp.where(low_i, sideways(value[:-2], -16), sideways(value[2:], 16))
        near_y = jnp.where(
            low_j,
            jnp.where(row2 > 0, sideways(flip_j, 1), 0.0),
            jnp.where(row2 < 3, sideways(flip_j, -1), 0.0),
        )
        near_z = jnp.where(low_k, last_layer(flip_k), next_layer(flip_k))
        return (
            centre_coeff[part] * mid
            + (f0[part] * flip_i + f1[part] * flip_j + f2[part] * flip_k)
            - pair2 * (near_x + near_y + near_z)
        )

    both = gather_end(1, own_r, REACH, r_copies)
    upper, lower = both[:, :8], both[:, 8:]
    given = roll(upper, 4, 1)
    rs = upper[1:-1] + jnp.where(low_i, sideways(given[:-2], -16), sideways(given[2:], 16))
    given = other_k(lower[1:-1])
    rs = rs + jnp.where(
        low_k,
        jnp.where(layer2 == 0, last_layer(given), 0.0),
        jnp.where(layer2 == width2 - 1, next_layer(given), 0.0),
    )
    d = dinv2 * rs * (1.0 / centre)
    xs = keep_d * d[1:-1] + take_e * dinv2[1:-1] * (rs[1:-1] - coarse_apply(d, 1))
    rest = rs[2:-2] - coarse_apply(xs, 2)
    d = dinv2[2:-2] * rest * (1.0 / centre)
    xs = xs[2:-2] + keep_d * d[1:-1] + take_e * dinv2[3:-3] * (rest[1:-1] - coarse_apply(d, 3))
    x = unplaced(xs[1])

    def all_lanes(value, end):
        value = jnp.where(lane1 < 16, roll(value, -16) if end else value, 0.0)
        value = value + roll(value, 16)
        value = value + roll(value, 32)
        return value + roll(value, 64)

    def x_trace(column, end):
        face = all_lanes(unplaced(column), end)
        total = 0.0
        for k in range(2):
            line = lane_ends[0] * face[k : k + 1, :] + lane_ends[1] * face[2 + k : 3 + k, :]
            total = total + row_ends[k] * line
        return total

    def z_trace(column, k):
        column = unplaced(column)
        face = lane_ends[0] * all_lanes(column, 0) + lane_ends[1] * all_lanes(column, 1)
        return row_ends[0] * face[k : k + 1, :] + row_ends[1] * face[2 + k : 3 + k, :]

    turned = other_k(xs[1:2])
    correction_traces = [
        x_trace(xs[0], 1),
        x_trace(xs[2], 0),
        z_trace(last_layer(turned)[0], 0),
        z_trace(next_layer(turned)[0], 1),
    ]
    for copy in middle.deferred:
        copy.wait_recv()
    before = [middle.RB[1, 1], middle.RB[1, 0], middle.RB[1, 3], towards_last(middle.RB[1, 2])]
    middle_near = [old + new for old, new in zip(before, correction_traces)]

    lifted = dot3(x, RPT1, RPT1l)
    columns = []
    for a in range(2):
        columns.append(PT1[0] * lifted[2 * a : 2 * a + 1, :] + PT1[1] * lifted[2 * a + 1 : 2 * a + 2, :])
    for j in range(8):
        middle.V[j] = middle.V[j] + PT1[0, j : j + 1, :] * columns[0] + PT1[1, j : j + 1, :] * columns[1]
    apply_level(middle, 2, None, begin_post(middle), near=middle_near)
    apply_level(middle, 3, 8, end_post(middle))

    lead = apply_level(middle, 4, 7, None, lead=True)

    C8[...] = contract(TPT, middle.V, 0, 8)
    for j0 in (0, 8):
        total = None
        for a in range(8):
            term = TP[j0 : j0 + 8, a : a + 1, :] * C8[a][None]
            total = term if total is None else total + term
        fine.U[j0 : j0 + 8, :, :128] = total
    lifted = dot3(fine.U[:, :, :128].reshape(256, 128), RPT, RPTl)
    fine.V[...] = fine.V[...] + lifted.reshape(16, 16, 256)

    def fine_near():
        for copy in lead:
            copy.wait_recv()
        faces = [middle.RB[4, 1], middle.RB[4, 0], middle.RB[4, 3], towards_last(middle.RB[4, 2])]
        wide = dot3(jnp.concatenate(faces, axis=0), lift_refs[6], lift_refs[7])
        wide = jnp.concatenate([wide[f * 8 : (f + 1) * 8] for f in range(4)], axis=1)
        wide = on_rows(lift_refs[0], lift_refs[1], jnp.concatenate([wide, jnp.zeros_like(wide)], axis=0))
        before = [fine.RB[1, 1], fine.RB[1, 0], fine.RB[1, 3], towards_last(fine.RB[1, 2])]
        return [old + wide[:, f * 256 : (f + 1) * 256] for f, old in enumerate(before)]

    apply_level(fine, 2, None, begin_post(fine), near=fine_near)
    apply_level(fine, 3, 10, end_post(fine))

    XIN[...] = jnp.transpose(fine.V[...].reshape(256, 256))
    for i in range(16):
        for t in range(3):
            out_ref[0, t, :, i * 256 : (i + 1) * 256] = XIN[i * SLOTS + t * 4 : i * SLOTS + t * 4 + 4, :]
    for copy in pending:
        copy.wait_send()


def scratch(given):
    f32, b16 = jnp.float32, jnp.bfloat16
    shapes = []
    for n in (16, 8):
        lanes = n * SLOTS
        shapes += [((n, n, lanes), f32)] * 4
        shapes += [((lanes, lanes), b16)] * 6 + [((lanes, 2 * lanes), b16), ((2 * lanes, lanes), b16)]
        shapes += [((n, lanes), f32)] + [((n, n, lanes), f32)] * 6
        shapes += [((6, n, lanes), f32)] * 3 + [((2, n, lanes), f32)]
        shapes += [((n, n, 2 * lanes), f32)] * 2 + [((5, 4, n, lanes), f32)] * 2
    shapes += [((16, 8, 128), f32), ((8, 16, 128), f32), ((2, 8, 128), f32)]
    shapes += [((256, 128), b16)] * 2 + [((128, 256), b16)] * 2 + [((128, 128), b16)] * 4
    shapes += [((8, 16, 128), f32)] * 2 + [((8, 128), f32), ((len(AROUND), 8, 128), f32)]
    shapes += [((16, 128), f32), ((len(AROUND), 16, 128), f32)]
    shapes += [((16, 256), f32), ((256, 256), f32)]
    semaphores = [pltpu.SemaphoreType.DMA((44,))] * 2 + [pltpu.SemaphoreType.DMA((16,))]
    semaphores += [pltpu.SemaphoreType.DMA((2 * len(AROUND),))] * 2
    landings = [pltpu.SMEM(x.shape, x.dtype) for x in given[:3]] + [pltpu.VMEM(x.shape, x.dtype) for x in given[3:]]
    return landings + [pltpu.VMEM(shape, dtype) for shape, dtype in shapes] + semaphores


def shards(residual, orders, factors, widths):
    lifts, c0, c1, pair0, pair1, taus, coarse = constants()
    given = [
        widths,
        jnp.transpose(orders, (2, 0, 1)),
        jnp.transpose(factors, (0, 2, 1, 3)),
        jnp.asarray(c0),
        jnp.asarray(c1),
        jnp.asarray(pair0),
        jnp.asarray(pair1),
        jnp.transpose(residual, (0, 2, 1, 3)),
    ] + [jnp.asarray(table) for table in lifts]
    out = pl.pallas_call(
        functools.partial(kernel, taus, coarse),
        out_shape=jax.ShapeDtypeStruct((1, 3, 4, 4096), jnp.float32),
        in_specs=[pl.BlockSpec(memory_space=pltpu.HBM)] * 16,
        out_specs=pl.BlockSpec(memory_space=pltpu.VMEM),
        scratch_shapes=scratch(given),
        compiler_params=pltpu.CompilerParams(
            collective_id=0, has_side_effects=True, vmem_limit_bytes=62 * 1024 * 1024
        ),
    )(*given)
    return jnp.transpose(out, (0, 2, 1, 3))


def solution(mesh):
    return jax.shard_map(
        shards,
        mesh=mesh,
        in_specs=(
            P("dom", None, "grp", None),
            P("dom", None, "grp"),
            P("dom", None, "grp", None),
            P(),
        ),
        out_specs=P("dom", None, "grp", None),
        check_vma=False,
    )
```

```python
import functools

import jax
import jax.numpy as jnp
import ml_dtypes
import numpy as np
from jax import lax
from jax.experimental import pallas as pl
from jax.experimental.pallas import tpu as pltpu
from jax.sharding import PartitionSpec as P

MESH = pl.DeviceIdType.MESH
SLOTS = 16
REACH = 5
COLUMNS = 2 * REACH + 1
AROUND = sorted(
    [
        (dx, dg)
        for dx in range(-REACH, REACH + 1)
        for dg in (0, 1, -1, 2)
        if (dx, dg) != (0, 0) and abs(dg) <= REACH - abs(dx)
    ],
    key=lambda place: -(abs(place[0]) + 3 * abs(place[1])),
)
mass_weight = 0.5
penalty = 0.5
cheb_high = 4.0
cheb_low = 0.15


def cheb_nodes(degree):
    return -np.cos(np.pi * np.arange(degree + 1) / degree)


def bary_weights(npoints):
    weights = (-1.0) ** np.arange(npoints)
    weights[0] = 0.5 * weights[0]
    weights[-1] = 0.5 * weights[-1]
    return weights


def lagrange_table(source, target):
    weights = bary_weights(source.shape[0])
    spacing = target[:, None] - source[None, :]
    coincide = np.abs(spacing) < 1e-12
    fractions = weights[None, :] / np.where(coincide, 1.0, spacing)
    lookup = fractions / fractions.sum(axis=1, keepdims=True)
    return np.where(coincide.any(axis=1, keepdims=True), np.where(coincide, 1.0, 0.0), lookup)


def quad_weights(degree):
    weights = np.full(degree + 1, np.pi / degree)
    weights[0] = 0.5 * weights[0]
    weights[-1] = 0.5 * weights[-1]
    return weights


def derivative(degree):
    points = cheb_nodes(degree)
    weights = bary_weights(degree + 1)
    spacing = points[:, None] - points[None, :] + np.eye(degree + 1)
    lookup = weights[None, :] / weights[:, None] / spacing
    lookup = lookup * (1.0 - np.eye(degree + 1))
    return lookup - np.eye(degree + 1) * lookup.sum(axis=1)[:, None]


def level_degree(degree, level_index):
    return [degree, degree // 2, 1][level_index]


def split3(table):
    high = table.astype(ml_dtypes.bfloat16)
    rest = table - high.astype(np.float64)
    middle = rest.astype(ml_dtypes.bfloat16)
    low = (rest - middle.astype(np.float64)).astype(ml_dtypes.bfloat16)
    return high, middle, low


def packed(tables):
    rows = np.concatenate([entry.reshape(9, -1) for entry in tables], axis=1).T
    return np.concatenate(list(split3(rows)) + [np.zeros((rows.shape[0], 5), ml_dtypes.bfloat16)], axis=1)


def order_tables(level_index):
    points = [16, 8, 2][level_index]
    common = cheb_nodes(points - 1)
    common_w = quad_weights(points - 1)
    names = ("scaled", "stiff_diag", "quad_w", "interpolate", "face_diag", "living", "prolong")
    table = {name: [] for name in names}
    for degree in range(7, 16):
        local = level_degree(degree, level_index)
        quad = quad_weights(local)
        deriv = derivative(local)
        stiff = deriv.T @ (quad[:, None] * deriv)
        scaled = np.zeros((points, points))
        scaled[: local + 1, : local + 1] = stiff / quad[:, None]
        padded = lambda vector: np.concatenate([vector, np.zeros(points - local - 1)])
        interp = np.zeros((points, points))
        interp[:, : local + 1] = lagrange_table(cheb_nodes(local), common)
        table["scaled"].append(scaled)
        table["stiff_diag"].append(padded(np.diagonal(stiff)))
        table["quad_w"].append(padded(quad))
        table["interpolate"].append(interp)
        table["face_diag"].append((common_w[:, None] * interp**2).sum(axis=0))
        table["living"].append(padded(np.ones(local + 1)))
        if level_index < 2:
            coarse = level_degree(degree, level_index + 1)
            lift = np.zeros((points, [16, 8, 2][level_index + 1]))
            lift[: local + 1, : coarse + 1] = lagrange_table(cheb_nodes(coarse), cheb_nodes(local))
            table["prolong"].append(lift)
    table = {name: np.stack(table[name]) for name in names if table[name]}
    tau = penalty * (points - 1) ** 2
    table["pair"] = tau * np.outer(common_w, common_w)
    table["tau"] = tau
    return table


def flip(table):
    return np.swapaxes(table, 1, 2)


def constants():
    fine, middle, coarse = [order_tables(level_index) for level_index in range(3)]
    vectors = ("quad_w", "face_diag", "living", "stiff_diag")
    matrices = lambda t: [flip(t["scaled"]), t["scaled"], flip(t["interpolate"]), t["interpolate"]]
    c0 = packed(matrices(fine) + [fine[name] for name in vectors])
    c1 = packed(
        matrices(middle)
        + [middle[name] for name in vectors]
        + [fine["prolong"], flip(fine["prolong"]), flip(middle["prolong"])]
    )
    pairs = [np.repeat(t["pair"], SLOTS, axis=1).astype(np.float32) for t in (fine, middle)]
    lift = lagrange_table(cheb_nodes(7), cheb_nodes(15))
    wide = np.kron(lift, np.eye(SLOTS))
    blank = lambda table, rows, cols: np.pad(table, ((0, rows - table.shape[0]), (0, cols - table.shape[1])))
    lifts = []
    for table in (blank(lift, 16, 16), blank(lift.T, 16, 16), wide, wide.T):
        high = table.astype(ml_dtypes.bfloat16)
        lifts += [high, (table - high.astype(np.float64)).astype(ml_dtypes.bfloat16)]
    return lifts, c0, c1, pairs[0], pairs[1], (fine["tau"], middle["tau"]), coarse


def split(values):
    high = values.astype(jnp.bfloat16)
    return high, (values - high.astype(jnp.float32)).astype(jnp.bfloat16)


def dot(left, right):
    return jnp.dot(left, right, preferred_element_type=jnp.float32)


def dot3(values, high, low):
    first, second = split(values)
    return dot(first, high[...]) + dot(second, high[...]) + dot(first, low[...])


def roll(values, shift, axis=-1):
    axis = axis % values.ndim
    return pltpu.roll(values, shift % values.shape[axis], axis)


def lanes_iota(lanes):
    return lax.broadcasted_iota(jnp.int32, (1, lanes), 1)


def rows_iota(rows, lanes):
    return lax.broadcasted_iota(jnp.int32, (rows, lanes), 0)


class Level:
    pass


def resolve(table, place):
    own = lax.broadcasted_iota(jnp.int32, table.shape[1:], 0) == place
    return jnp.sum(jnp.where(own[None], table[...], 0.0), axis=1)


def spread(keep, rows, count, target, low=None):
    keep[: rows.shape[0], : rows.shape[1]] = rows
    lanes = rows.shape[1]
    same = rows_iota(SLOTS, lanes) == (lanes_iota(lanes) & (SLOTS - 1))
    for p in range(count):
        block = jnp.where(same, keep[p : p + 1, :lanes], 0.0)
        high = block.astype(jnp.bfloat16)
        target[p * SLOTS : (p + 1) * SLOTS, :] = high
        if low is not None:
            low[p * SLOTS : (p + 1) * SLOTS, :] = (block - high.astype(jnp.float32)).astype(jnp.bfloat16)


def kernel(taus, coarse, *refs):
    names = iter(refs)
    take = lambda count: [next(names) for _ in range(count)]
    given = take(16)
    (out_ref,) = take(1)
    widths_ref, orders_ref, factors_ref, c0_ref, c1_ref, pair0_ref, pair1_ref, res_ref = take(8)
    lift_refs = take(8)
    levels = []
    for index in range(2):
        lv = Level()
        lv.n = [16, 8][index]
        lv.lanes = lv.n * SLOTS
        (lv.T, lv.TT, lv.TI, lv.TIT) = take(4)
        (lv.RS, lv.RSl, lv.RI, lv.RIl, lv.RIT, lv.RITl, lv.PP, lv.PPT) = take(8)
        (lv.IL, lv.DINV, lv.WWW, lv.R, lv.X, lv.V, lv.OUT) = take(7)
        (lv.H, lv.Q, lv.G, lv.RZ, lv.U, lv.Y, lv.SB, lv.RB) = take(8)
        lv.pair = [pair0_ref, pair1_ref][index]
        levels.append(lv)
    TP, TPT, PT1, RP, RPl, RPT, RPTl, RP1, RP1l, RPT1, RPT1l, A8, C8, SBF, RBF, SBR, RBR, KEEP, XIN = take(19)
    send_sem, recv_sem, load_sem, wide_send, wide_recv = take(5)
    landings = [widths_ref, orders_ref, factors_ref, c0_ref, c1_ref, pair0_ref, pair1_ref, res_ref] + lift_refs
    loads = [pltpu.make_async_copy(*pair, load_sem.at[i]) for i, pair in enumerate(zip(given, landings))]
    for load in loads:
        load.start()

    dom, grp = lax.axis_index("dom"), lax.axis_index("grp")
    n_dom, n_grp = lax.axis_size("dom"), lax.axis_size("grp")
    targets = [
        {"dom": lax.rem(dom + n_dom - 1, n_dom)},
        {"dom": lax.rem(dom + 1, n_dom)},
        {"grp": lax.rem(grp + n_grp - 1, n_grp)},
        {"grp": lax.rem(grp + 1, n_grp)},
    ]
    barrier = pltpu.get_barrier_semaphore()
    around = [
        {"dom": lax.rem(dom + n_dom + dx, n_dom), "grp": lax.rem(grp + n_grp + dg, n_grp)} for dx, dg in AROUND
    ]
    for target in around:
        pl.semaphore_signal(barrier, inc=1, device_id=target, device_id_type=MESH)

    lane = lanes_iota(16 * SLOTS)
    slot = lane & (SLOTS - 1)
    layer = slot >> 2
    row = slot & 3
    for load in loads[:3]:
        load.wait()
    width = jnp.int32(0)
    for g in range(4):
        width = jnp.where(grp == g, widths_ref[g], width)
    order = jnp.full(lane.shape, 7, jnp.int32)
    factor = [jnp.full(lane.shape, 1.0, jnp.float32) for _ in range(4)]
    for r in range(4):
        for t in range(3):
            here = slot == t * 4 + r
            order = jnp.where(here, orders_ref[t, 0, r], order)
            for c in range(4):
                factor[c] = jnp.where(here, factors_ref[0, t, r, c], factor[c])
    alive = layer < width
    mask = jnp.where(alive, 1.0, 0.0)
    at_first = layer == 0
    at_last = layer == width - 1
    line = rows_iota(32, 16 * SLOTS)
    line = jnp.where(line < 9, line, jnp.where(line < 18, line - 9, jnp.where(line < 27, line - 18, -1)))
    onehot = jnp.where(line == order - 7, 1.0, 0.0).astype(jnp.bfloat16)

    def tables(lv, index, which):
        refs = (lv.TI, lv.TIT, lv.T, lv.TT)
        source = [c0_ref, c1_ref][index]
        size = lv.n * lv.n
        at = (2, 3, 0, 1)[which] * size
        refs[which][...] = dot(source[at : at + size, :], lv.hot).reshape(lv.n, lv.n, lv.lanes)

    def setup_first(lv, index):
        n, lanes = lv.n, lv.lanes
        lv.place = lane[:, :lanes] >> 4
        lv.last = [order, order >> 1][index][:, :lanes]
        lv.f = [entry[:, :lanes] for entry in factor]
        lv.cm = lv.f[3] * mass_weight
        lv.at_first, lv.at_last = at_first[:, :lanes], at_last[:, :lanes]
        lv.row = row[:, :lanes]
        lv.last_range = [range(7, 16), range(3, 8)][index]
        lv.hot = onehot[:, :lanes]
        tables(lv, index, 0)
        at = 4 * n * n
        vectors = dot([c0_ref, c1_ref][index][at : at + 4 * n, :], lv.hot)
        quad, face, live, stiff = [vectors[i * n : (i + 1) * n] for i in range(4)]
        inter = resolve(lv.TI, lv.place)
        lv.IL[...] = inter
        spread(KEEP, inter, n, lv.RI, lv.RIl)
        points = rows_iota(n, lanes)
        lv.FM = jnp.where(points == 0, 1.0, 0.0)
        lv.LM = jnp.where(points == lv.last, 1.0, 0.0)
        lv.same = rows_iota(SLOTS, lanes) == (lane[:, :lanes] & (SLOTS - 1))
        for p in range(n):
            rows = slice(p * SLOTS, (p + 1) * SLOTS)
            lv.PP[rows, :lanes] = one(lv.same) if p == 0 else jnp.zeros((SLOTS, lanes), jnp.bfloat16)
            lv.PP[rows, lanes:] = one(lv.same & (lv.last == p))
        pick = lambda table: jnp.sum(jnp.where(points == lv.place, table, 0.0), axis=0, keepdims=True)
        w_i, face_i, live_i, stiff_i = pick(quad), pick(face), pick(live) * mask[:, :lanes], pick(stiff)
        ends = lv.FM + lv.LM
        ends_i = pick(ends)
        f0, f1, f2, _ = lv.f
        for j in range(n):
            one_row = lambda table: table[j : j + 1, :]
            w_j, face_j, live_j, stiff_j, ends_j = [one_row(t) for t in (quad, face, live, stiff, ends)]
            www = (w_i * w_j) * quad
            diagonal = (
                (f0 * stiff_i * w_j) * quad
                + (f1 * w_i * stiff_j) * quad
                + (f2 * w_i * w_j) * stiff
                + lv.cm * www
                + taus[index] * ((ends_j * face_i + face_j * ends_i) * face + (face_j * face_i) * ends)
            )
            node_live = (live_j * live_i) * live
            lv.WWW[j] = www
            lv.DINV[j] = node_live / (diagonal + 1.0 - node_live)
            if index == 0:
                lv.X[j] = node_live

    def setup_return(lv, index):
        n, lanes = lv.n, lv.lanes
        tables(lv, index, 1)
        spread(KEEP, resolve(lv.TIT, lv.place), n, lv.RIT, lv.RITl)
        for p in range(n):
            lv.PPT[p * SLOTS : (p + 1) * SLOTS, :] = one(lv.same & (lv.place == 0))
            lv.PPT[lanes + p * SLOTS : lanes + (p + 1) * SLOTS, :] = one(lv.same & (lv.place == lv.last))

    def setup_volume(lv, index):
        tables(lv, index, 2)
        tables(lv, index, 3)
        spread(KEEP, resolve(lv.T, lv.place) * lv.f[0], lv.n, lv.RS, lv.RSl)

    def setup_between():
        at = 4 * 64 + 4 * 8
        TP[...] = dot(c1_ref[at : at + 128, :], middle.hot).reshape(16, 8, 128)
        TPT[...] = dot(c1_ref[at + 128 : at + 256, :], middle.hot).reshape(8, 16, 128)
        spread(KEEP, resolve(TP, middle.place), 16, RP, RPl)

    def setup_coarse():
        at = 4 * 64 + 4 * 8 + 256
        PT1[...] = dot(c1_ref[at : at + 16, :], middle.hot).reshape(2, 8, 128)
        place1 = middle.place
        wide = jnp.concatenate([TPT[...], TPT[...]], axis=2)
        spread(KEEP, resolve(wide, fine.place), 8, RPT, RPTl)
        spread(KEEP, jnp.where(place1 == 0, PT1[0], jnp.where(place1 == 1, PT1[1], 0.0)), 8, RP1, RP1l)
        RPT1[...] = jnp.zeros(RPT1.shape, jnp.bfloat16)
        RPT1l[...] = jnp.zeros(RPT1l.shape, jnp.bfloat16)
        spread(KEEP, resolve(PT1, place1), 2, RPT1, RPT1l)

    def after_second_send():
        for load in loads[8:]:
            load.wait()
        setup_first(middle, 1)
        setup_return(middle, 1)
        setup_between()

    one = lambda cond: jnp.where(cond, 1.0, 0.0).astype(jnp.bfloat16)
    fine, middle = levels
    for load in loads[3:7]:
        load.wait()
    setup_first(fine, 0)

    loads[7].wait()
    for i in range(16):
        for t in range(3):
            XIN[i * SLOTS + t * 4 : i * SLOTS + t * 4 + 4, :] = res_ref[0, t, :, i * 256 : (i + 1) * 256]
        XIN[i * SLOTS + 12 : i * SLOTS + 16, :] = jnp.zeros((4, 256), jnp.float32)
    fine.R[...] = jnp.transpose(XIN[...]).reshape(16, 16, 256) * fine.X[...]

    pl.semaphore_wait(barrier, len(AROUND))
    pending = []
    lane1 = lane[:, :128]
    group1 = lane1 >> 5

    def gather_start(which, value, reach):
        source, landing = [(SBF, RBF), (SBR, RBR)][which]
        source[...] = value
        copies = {}
        for q, (dx, dg) in enumerate(AROUND):
            if abs(dx) + abs(dg) > reach:
                continue
            where = which * len(AROUND) + q
            copies[q] = pltpu.make_async_remote_copy(
                src_ref=source,
                dst_ref=landing.at[q],
                send_sem=wide_send.at[where],
                recv_sem=wide_recv.at[where],
                device_id=around[q],
                device_id_type=MESH,
            )
            copies[q].start()
            pending.append(copies[q])
        return copies

    def gather_end(which, value, reach, copies):
        landing = [RBF, RBR][which]
        for q in copies:
            copies[q].wait_recv()
        columns = []
        for column in range(-reach, reach + 1):
            total = value if column == 0 else None
            for q in copies:
                if -AROUND[q][0] == column:
                    total = landing[q] if total is None else total + landing[q]
            columns.append(total)
        return jnp.stack(columns)

    own_group = group1 == grp
    own_factors = jnp.concatenate(
        [jnp.where(own_group, entry[:, :128], 0.0) for entry in factor] + [jnp.zeros((4, 128), jnp.float32)], axis=0
    )
    factor_copies = {}

    def send(number, direction, value, source, landing):
        source[...] = value
        where = number * 4 + direction
        copy = pltpu.make_async_remote_copy(
            src_ref=source,
            dst_ref=landing,
            send_sem=send_sem.at[where],
            recv_sem=recv_sem.at[where],
            device_id=targets[direction],
            device_id_type=MESH,
        )
        copy.start()
        pending.append(copy)
        return copy

    def towards_first(value, last):
        value = jnp.where(last, value, 0.0)
        return value + roll(value, -4) + roll(value, -8)

    def towards_last(value):
        return jnp.where(width == 1, value, jnp.where(width == 2, roll(value, 4), roll(value, 8)))

    def contract(table, source, first, count):
        total = None
        for k in range(table.shape[0]):
            term = table[k][None] * source[first : first + count, k : k + 1, :]
            total = term if total is None else total + term
        return total

    def give_back(lv):
        n, lanes = lv.n, lv.lanes
        back = contract(lv.TIT, lv.G, 0, 4)
        for f in range(2):
            for j in range(n):
                lv.Y[j, :, f * lanes : (f + 1) * lanes] = lv.IL[j : j + 1, :] * back[f]
        lv.RZ[...] = dot3(back[2:4].reshape(2 * n, lanes), lv.RIT, lv.RITl).reshape(2, n, lanes)
        first, second = split(lv.Y[...].reshape(n * n, 2 * lanes))
        x_back = (dot(first, lv.PPT[...]) + dot(second, lv.PPT[...])).reshape(n, n, lanes)
        return x_back, lambda j: lv.FM * lv.RZ[0, j : j + 1, :] + lv.LM * lv.RZ[1, j : j + 1, :]

    def apply_level(lv, slot_of, number, consume, meanwhile=None, near=None, defer=False, lead=False):
        n, lanes = lv.n, lv.lanes
        high, low = split(lv.V[...].reshape(n * n, lanes))
        lv.U[...] = (dot(high, lv.PP[...]) + dot(low, lv.PP[...])).reshape(n, n, 2 * lanes)
        z0 = lv.V[:, 0, :]
        z1 = jnp.zeros_like(z0)
        for p in lv.last_range:
            z1 = jnp.where(lv.last == p, lv.V[:, p, :], z1)
        turned = dot3(jnp.concatenate([z0, z1], axis=0), lv.RI, lv.RIl)
        for f in range(2):
            total = None
            for j in range(n):
                term = lv.IL[j : j + 1, :] * lv.U[j, :, f * lanes : (f + 1) * lanes]
                total = term if total is None else total + term
            lv.H[f] = total
        lv.Q[0:2] = contract(lv.TI, lv.H, 0, 2)
        copies = []
        start = lambda d, value: copies.append(
            send(number, d, value, lv.SB.at[slot_of, d], lv.RB.at[slot_of, d])
        )
        if near is None:
            start(0, lv.Q[0])
            start(1, lv.Q[1])
        lv.H[2:4] = turned.reshape(2, n, lanes)
        lv.Q[2:4] = contract(lv.TI, lv.H, 2, 2)
        if near is None:
            start(2, lv.Q[2])
            start(3, towards_first(lv.Q[3], lv.at_last))
        if lead:
            return copies
        if meanwhile is not None:
            meanwhile()
        y0 = lv.V[0]
        y1 = jnp.zeros_like(y0)
        for p in lv.last_range:
            y1 = jnp.where(lv.last == p, lv.V[p], y1)
        turned = dot3(jnp.concatenate([y0, y1], axis=0), lv.RI, lv.RIl)
        lv.H[4:6] = turned.reshape(2, n, lanes)
        lv.Q[4:6] = contract(lv.TI, lv.H, 4, 2)
        lv.G[4] = lv.pair[...] * (lv.Q[4] - jnp.where(lv.row > 0, roll(lv.Q[5], 1), 0.0))
        lv.G[5] = lv.pair[...] * (lv.Q[5] - jnp.where(lv.row < 3, roll(lv.Q[4], -1), 0.0))
        back = contract(lv.TIT, lv.G, 4, 2).reshape(2 * n, lanes)
        back = dot3(back, lv.RIT, lv.RITl)
        y_back = [back[:n], back[n:]]
        lv.OUT[...] = (
            dot(high, lv.RS[...]) + dot(low, lv.RS[...]) + dot(high, lv.RSl[...])
        ).reshape(n, n, lanes)
        size = 4 if n == 16 else 8
        for a in range(0, n, size):
            block = slice(a, a + size)
            along_j, along_k = None, None
            for j in range(n):
                term = lv.TT[block, j : j + 1, :] * lv.V[j][None]
                along_j = term if along_j is None else along_j + term
            for k in range(n):
                term = lv.T[k][None] * lv.V[block, k : k + 1, :]
                along_k = term if along_k is None else along_k + term
            lv.OUT[block] = lv.WWW[block] * (
                lv.OUT[block] + lv.f[1] * along_j + lv.f[2] * along_k + lv.cm * lv.V[block]
            )
        lv.OUT[0] = lv.OUT[0] + y_back[0]
        for p in lv.last_range:
            lv.OUT[p] = lv.OUT[p] + jnp.where(lv.last == p, y_back[1], 0.0)
        if defer:
            lv.deferred, near = copies, [0.0] * 4
        else:
            for copy in copies:
                copy.wait_recv()
        pair = lv.pair[...]
        landed = lambda d: lv.RB[slot_of, d]
        if near is None:
            x_low, x_high, z_low, z_high = landed(1), landed(0), landed(3), towards_last(landed(2))
        else:
            x_low, x_high, z_low, z_high = near() if callable(near) else near
        lv.G[0] = pair * (lv.Q[0] - x_low)
        lv.G[1] = pair * (lv.Q[1] - x_high)
        lv.G[2] = pair * (lv.Q[2] - jnp.where(lv.at_first, z_low, roll(lv.Q[3], 4)))
        lv.G[3] = pair * (lv.Q[3] - jnp.where(lv.at_last, z_high, roll(lv.Q[2], -4)))
        x_back, z_back = give_back(lv)
        for j in range(n):
            consume(j, lv.OUT[j] + x_back[j] + z_back(j))

    centre = 0.5 * (cheb_high + cheb_low)
    radius = 0.5 * (cheb_high - cheb_low)
    rho_first = radius / centre
    rho_next = 1.0 / (2.0 * centre / radius - rho_first)
    keep_d = 1.0 + rho_next * rho_first
    take_e = 2.0 * rho_next / radius

    def first_step(lv):
        lv.V[...] = lv.DINV[...] * lv.R[...] * (1.0 / centre)

    def end_pre(lv):
        def consume(j, applied):
            lv.V[j] = keep_d * lv.V[j] + take_e * lv.DINV[j] * (lv.R[j] - applied)

        return consume

    def remainder(lv):
        def consume(j, applied):
            lv.OUT[j] = lv.R[j] - applied

        return consume

    def begin_post(lv):
        def consume(j, applied):
            rest = lv.R[j] - applied
            lv.R[j] = rest
            lv.X[j] = lv.V[j]
            lv.V[j] = lv.DINV[j] * rest * (1.0 / centre)

        return consume

    def end_post(lv):
        def consume(j, applied):
            lv.V[j] = lv.X[j] + keep_d * lv.V[j] + take_e * lv.DINV[j] * (lv.R[j] - applied)

        return consume

    def after_first_send():
        setup_return(fine, 0)
        setup_volume(fine, 0)

    def after_third_send():
        factor_copies.update(gather_start(0, own_factors, REACH - 1))
        setup_volume(middle, 1)
        setup_coarse()

    first_step(fine)
    apply_level(fine, 0, 0, end_pre(fine), after_first_send)
    apply_level(fine, 1, 1, remainder(fine), after_second_send, defer=True)

    lanes_down = dot3(fine.OUT[...].reshape(256, 256), RP, RPl).reshape(16, 16, 128)
    total = None
    for j in range(16):
        term = TPT[:, j : j + 1, :] * lanes_down[j][None]
        total = term if total is None else total + term
    A8[...] = total
    middle.R[...] = contract(TP, A8, 0, 8)

    def on_rows(high, low, values):
        first, second = split(values)
        return dot(high[...], first) + dot(high[...], second) + dot(low[...], first)

    for copy in fine.deferred:
        copy.wait_recv()
    z_low = jnp.where(fine.at_first, fine.RB[1, 3], 0.0)
    z_high = jnp.where(fine.at_last, towards_last(fine.RB[1, 2]), 0.0)
    near_faces = [fine.pair[...] * value for value in (fine.RB[1, 1], fine.RB[1, 0], z_low, z_high)]
    near_faces = on_rows(lift_refs[2], lift_refs[3], jnp.concatenate(near_faces, axis=1))[:8]
    near_faces = jnp.concatenate([near_faces[:, f * 256 : (f + 1) * 256] for f in range(4)], axis=0)
    middle.G[0:4] = dot3(near_faces, lift_refs[4], lift_refs[5]).reshape(4, 8, 128)
    x_back, z_back = give_back(middle)
    for j in range(8):
        middle.R[j] = middle.R[j] + x_back[j] + z_back(j)
    first_step(middle)
    apply_level(middle, 0, 2, end_pre(middle), after_third_send)
    apply_level(middle, 1, 3, remainder(middle), defer=True)

    parts = []
    for a in range(2):
        total = None
        for j in range(8):
            term = PT1[a, j : j + 1, :] * middle.OUT[j]
            total = term if total is None else total + term
        for b in range(2):
            parts.append(jnp.sum(PT1[b] * total, axis=0, keepdims=True))
    coarse_r = dot3(jnp.concatenate(parts + [jnp.zeros((4, 128), jnp.float32)], axis=0), RP1, RP1l)

    def placed(value):
        total = value
        for g in range(1, 4):
            total = jnp.where(grp == g, roll(value, 32 * g), total)
        return total

    def unplaced(value):
        total = value
        for g in range(1, 4):
            total = jnp.where(grp == g, roll(value, -32 * g), total)
        return jnp.where(lane1 < 32, total, 0.0)

    points = cheb_nodes(7)
    line2 = rows_iota(8, 128)
    along_lane, along_row = jnp.zeros((1, 128), jnp.float32), jnp.zeros((8, 128), jnp.float32)
    for b in range(8):
        along_lane = jnp.where((lane1 >> 4) == b, float(points[b]), along_lane)
        along_row = jnp.where(line2 == b, float(points[b]), along_row)
    lane_ends = [0.5 - 0.5 * along_lane, 0.5 + 0.5 * along_lane]
    row_ends = [0.5 - 0.5 * along_row, 0.5 + 0.5 * along_row]

    def row_sums(face):
        weighted = middle.pair[...] * middle.Q[face]
        return [jnp.sum(row_ends[end] * weighted, axis=0, keepdims=True) for end in range(2)]

    def group_sums(rows):
        total = jnp.concatenate(rows, axis=0)
        for shift in (16, 32, 64):
            total = total + roll(total, shift)
        return total

    def two_groups(low, high):
        return jnp.where(lane1 < 16, low, jnp.where(lane1 < 32, high, 0.0))

    x_rows = [lane_ends[j] * row_sums(f)[k] for f in range(2) for j in range(2) for k in range(2)]
    x_sums = group_sums(x_rows)
    z_rows = [lane_ends[i] * row_sums(2 + k)[j] for i in range(2) for j in range(2) for k in range(2)]
    z_sums = group_sums(z_rows)
    x_given = two_groups(x_sums[:4], x_sums[4:])
    z_given = two_groups(z_sums[:4], z_sums[4:])
    own_r = placed(jnp.concatenate([coarse_r[:4], x_given, z_given, jnp.zeros((4, 128), jnp.float32)], axis=0))
    r_copies = gather_start(1, own_r, REACH)

    fs = gather_end(0, own_factors, REACH - 1, factor_copies)
    f0, f1, f2, f3 = [fs[:, c : c + 1, :] for c in range(4)]
    low_i = ((lane1 >> 4) & 1) == 0
    low_j = line2 < 2
    low_k = (line2 & 1) == 0
    row2, layer2 = lane1 & 3, (lane1 >> 2) & 3
    width2, before2 = jnp.zeros((1, 128), jnp.int32), jnp.zeros((1, 128), jnp.int32)
    for g in range(4):
        width2 = jnp.where(group1 == g, widths_ref[g], width2)
        before2 = jnp.where(group1 == (g + 1) % 4, widths_ref[g], before2)
    s00, s01 = float(coarse["scaled"][0, 0, 0]), float(coarse["scaled"][0, 0, 1])
    w0 = float(coarse["quad_w"][0, 0])
    www = w0**3
    pair2 = float(coarse["pair"][0, 0])
    centre_coeff = www * (s00 * (f0 + f1 + f2) + mass_weight * f3) + 3.0 * pair2
    live2 = jnp.where((layer2 < width2) & (line2 < 4), 1.0, 0.0)[None]
    dinv2 = live2 / (centre_coeff + 1.0 - live2)
    f0, f1, f2 = [(www * s01) * entry for entry in (f0, f1, f2)]

    def sideways(value, shift):
        return roll(value.reshape(-1, 128), shift).reshape(value.shape)

    def next_layer(value):
        across = jnp.where(
            width2 == 1, sideways(value, -32), jnp.where(width2 == 2, sideways(value, -28), sideways(value, -24))
        )
        return jnp.where(layer2 < width2 - 1, sideways(value, -4), across)

    def last_layer(value):
        across = jnp.where(
            before2 == 1, sideways(value, 32), jnp.where(before2 == 2, sideways(value, 28), sideways(value, 24))
        )
        return jnp.where(layer2 > 0, sideways(value, 4), across)

    def other_k(value):
        return jnp.where(low_k, roll(value, -1, 1), roll(value, 1, 1))

    def coarse_apply(value, skip):
        mid = value[1:-1]
        part = slice(skip, COLUMNS - 2 - skip)
        flip_i = jnp.where(low_i, sideways(mid, -16), sideways(mid, 16))
        flip_j = jnp.where(low_j, roll(mid, -2, 1), roll(mid, 2, 1))
        flip_k = other_k(mid)
        near_x = jnp.where(low_i, sideways(value[:-2], -16), sideways(value[2:], 16))
        near_y = jnp.where(
            low_j,
            jnp.where(row2 > 0, sideways(flip_j, 1), 0.0),
            jnp.where(row2 < 3, sideways(flip_j, -1), 0.0),
        )
        near_z = jnp.where(low_k, last_layer(flip_k), next_layer(flip_k))
        return (
            centre_coeff[part] * mid
            + (f0[part] * flip_i + f1[part] * flip_j + f2[part] * flip_k)
            - pair2 * (near_x + near_y + near_z)
        )

    both = gather_end(1, own_r, REACH, r_copies)
    upper, lower = both[:, :8], both[:, 8:]
    given = roll(upper, 4, 1)
    rs = upper[1:-1] + jnp.where(low_i, sideways(given[:-2], -16), sideways(given[2:], 16))
    given = other_k(lower[1:-1])
    rs = rs + jnp.where(
        low_k,
        jnp.where(layer2 == 0, last_layer(given), 0.0),
        jnp.where(layer2 == width2 - 1, next_layer(given), 0.0),
    )
    d = dinv2 * rs * (1.0 / centre)
    xs = keep_d * d[1:-1] + take_e * dinv2[1:-1] * (rs[1:-1] - coarse_apply(d, 1))
    rest = rs[2:-2] - coarse_apply(xs, 2)
    d = dinv2[2:-2] * rest * (1.0 / centre)
    xs = xs[2:-2] + keep_d * d[1:-1] + take_e * dinv2[3:-3] * (rest[1:-1] - coarse_apply(d, 3))
    x = unplaced(xs[1])

    def all_lanes(value, end):
        value = jnp.where(lane1 < 16, roll(value, -16) if end else value, 0.0)
        value = value + roll(value, 16)
        value = value + roll(value, 32)
        return value + roll(value, 64)

    def x_trace(column, end):
        face = all_lanes(unplaced(column), end)
        total = 0.0
        for k in range(2):
            line = lane_ends[0] * face[k : k + 1, :] + lane_ends[1] * face[2 + k : 3 + k, :]
            total = total + row_ends[k] * line
        return total

    def z_trace(column, k):
        column = unplaced(column)
        face = lane_ends[0] * all_lanes(column, 0) + lane_ends[1] * all_lanes(column, 1)
        return row_ends[0] * face[k : k + 1, :] + row_ends[1] * face[2 + k : 3 + k, :]

    turned = other_k(xs[1:2])
    correction_traces = [
        x_trace(xs[0], 1),
        x_trace(xs[2], 0),
        z_trace(last_layer(turned)[0], 0),
        z_trace(next_layer(turned)[0], 1),
    ]
    for copy in middle.deferred:
        copy.wait_recv()
    before = [middle.RB[1, 1], middle.RB[1, 0], middle.RB[1, 3], towards_last(middle.RB[1, 2])]
    middle_near = [old + new for old, new in zip(before, correction_traces)]

    lifted = dot3(x, RPT1, RPT1l)
    columns = []
    for a in range(2):
        columns.append(PT1[0] * lifted[2 * a : 2 * a + 1, :] + PT1[1] * lifted[2 * a + 1 : 2 * a + 2, :])
    for j in range(8):
        middle.V[j] = middle.V[j] + PT1[0, j : j + 1, :] * columns[0] + PT1[1, j : j + 1, :] * columns[1]
    apply_level(middle, 2, None, begin_post(middle), near=middle_near)
    apply_level(middle, 3, 8, end_post(middle))

    lead = apply_level(middle, 4, 7, None, lead=True)

    C8[...] = contract(TPT, middle.V, 0, 8)
    for j0 in (0, 8):
        total = None
        for a in range(8):
            term = TP[j0 : j0 + 8, a : a + 1, :] * C8[a][None]
            total = term if total is None else total + term
        fine.U[j0 : j0 + 8, :, :128] = total
    lifted = dot3(fine.U[:, :, :128].reshape(256, 128), RPT, RPTl)
    fine.V[...] = fine.V[...] + lifted.reshape(16, 16, 256)

    def fine_near():
        for copy in lead:
            copy.wait_recv()
        faces = [middle.RB[4, 1], middle.RB[4, 0], middle.RB[4, 3], towards_last(middle.RB[4, 2])]
        wide = dot3(jnp.concatenate(faces, axis=0), lift_refs[6], lift_refs[7])
        wide = jnp.concatenate([wide[f * 8 : (f + 1) * 8] for f in range(4)], axis=1)
        wide = on_rows(lift_refs[0], lift_refs[1], jnp.concatenate([wide, jnp.zeros_like(wide)], axis=0))
        before = [fine.RB[1, 1], fine.RB[1, 0], fine.RB[1, 3], towards_last(fine.RB[1, 2])]
        return [old + wide[:, f * 256 : (f + 1) * 256] for f, old in enumerate(before)]

    apply_level(fine, 2, None, begin_post(fine), near=fine_near)
    apply_level(fine, 3, 10, end_post(fine))

    XIN[...] = jnp.transpose(fine.V[...].reshape(256, 256))
    for i in range(16):
        for t in range(3):
            out_ref[0, t, :, i * 256 : (i + 1) * 256] = XIN[i * SLOTS + t * 4 : i * SLOTS + t * 4 + 4, :]
    for copy in pending:
        copy.wait_send()


def scratch(given):
    f32, b16 = jnp.float32, jnp.bfloat16
    shapes = []
    for n in (16, 8):
        lanes = n * SLOTS
        shapes += [((n, n, lanes), f32)] * 4
        shapes += [((lanes, lanes), b16)] * 6 + [((lanes, 2 * lanes), b16), ((2 * lanes, lanes), b16)]
        shapes += [((n, lanes), f32)] + [((n, n, lanes), f32)] * 6
        shapes += [((6, n, lanes), f32)] * 3 + [((2, n, lanes), f32)]
        shapes += [((n, n, 2 * lanes), f32)] * 2 + [((5, 4, n, lanes), f32)] * 2
    shapes += [((16, 8, 128), f32), ((8, 16, 128), f32), ((2, 8, 128), f32)]
    shapes += [((256, 128), b16)] * 2 + [((128, 256), b16)] * 2 + [((128, 128), b16)] * 4
    shapes += [((8, 16, 128), f32)] * 2 + [((8, 128), f32), ((len(AROUND), 8, 128), f32)]
    shapes += [((16, 128), f32), ((len(AROUND), 16, 128), f32)]
    shapes += [((16, 256), f32), ((256, 256), f32)]
    semaphores = [pltpu.SemaphoreType.DMA((44,))] * 2 + [pltpu.SemaphoreType.DMA((16,))]
    semaphores += [pltpu.SemaphoreType.DMA((2 * len(AROUND),))] * 2
    landings = [pltpu.SMEM(x.shape, x.dtype) for x in given[:3]] + [pltpu.VMEM(x.shape, x.dtype) for x in given[3:]]
    return landings + [pltpu.VMEM(shape, dtype) for shape, dtype in shapes] + semaphores


def shards(residual, orders, factors, widths):
    lifts, c0, c1, pair0, pair1, taus, coarse = constants()
    given = [
        widths,
        jnp.transpose(orders, (2, 0, 1)),
        jnp.transpose(factors, (0, 2, 1, 3)),
        jnp.asarray(c0),
        jnp.asarray(c1),
        jnp.asarray(pair0),
        jnp.asarray(pair1),
        jnp.transpose(residual, (0, 2, 1, 3)),
    ] + [jnp.asarray(table) for table in lifts]
    out = pl.pallas_call(
        functools.partial(kernel, taus, coarse),
        out_shape=jax.ShapeDtypeStruct((1, 3, 4, 4096), jnp.float32),
        in_specs=[pl.BlockSpec(memory_space=pltpu.HBM)] * 16,
        out_specs=pl.BlockSpec(memory_space=pltpu.VMEM),
        scratch_shapes=scratch(given),
        compiler_params=pltpu.CompilerParams(
            collective_id=0, has_side_effects=True, vmem_limit_bytes=62 * 1024 * 1024
        ),
    )(*given)
    return jnp.transpose(out, (0, 2, 1, 3))


def solution(mesh):
    return jax.shard_map(
        shards,
        mesh=mesh,
        in_specs=(
            P("dom", None, "grp", None),
            P("dom", None, "grp"),
            P("dom", None, "grp", None),
            P(),
        ),
        out_specs=P("dom", None, "grp", None),
        check_vma=False,
    )
```

```python
import functools

import jax
import jax.numpy as jnp
import ml_dtypes
import numpy as np
from jax import lax
from jax.experimental import pallas as pl
from jax.experimental.pallas import tpu as pltpu
from jax.sharding import PartitionSpec as P

MESH = pl.DeviceIdType.MESH
SLOTS = 16
REACH = 5
COLUMNS = 2 * REACH + 1
AROUND = sorted(
    [
        (dx, dg)
        for dx in range(-REACH, REACH + 1)
        for dg in (0, 1, -1, 2)
        if (dx, dg) != (0, 0) and abs(dg) <= REACH - abs(dx)
    ],
    key=lambda place: -(abs(place[0]) + 3 * abs(place[1])),
)
mass_weight = 0.5
penalty = 0.5
cheb_high = 4.0
cheb_low = 0.15


def cheb_nodes(degree):
    return -np.cos(np.pi * np.arange(degree + 1) / degree)


def bary_weights(npoints):
    weights = (-1.0) ** np.arange(npoints)
    weights[0] = 0.5 * weights[0]
    weights[-1] = 0.5 * weights[-1]
    return weights


def lagrange_table(source, target):
    weights = bary_weights(source.shape[0])
    spacing = target[:, None] - source[None, :]
    coincide = np.abs(spacing) < 1e-12
    fractions = weights[None, :] / np.where(coincide, 1.0, spacing)
    lookup = fractions / fractions.sum(axis=1, keepdims=True)
    return np.where(coincide.any(axis=1, keepdims=True), np.where(coincide, 1.0, 0.0), lookup)


def quad_weights(degree):
    weights = np.full(degree + 1, np.pi / degree)
    weights[0] = 0.5 * weights[0]
    weights[-1] = 0.5 * weights[-1]
    return weights


def derivative(degree):
    points = cheb_nodes(degree)
    weights = bary_weights(degree + 1)
    spacing = points[:, None] - points[None, :] + np.eye(degree + 1)
    lookup = weights[None, :] / weights[:, None] / spacing
    lookup = lookup * (1.0 - np.eye(degree + 1))
    return lookup - np.eye(degree + 1) * lookup.sum(axis=1)[:, None]


def level_degree(degree, level_index):
    return [degree, degree // 2, 1][level_index]


def split3(table):
    high = table.astype(ml_dtypes.bfloat16)
    rest = table - high.astype(np.float64)
    middle = rest.astype(ml_dtypes.bfloat16)
    low = (rest - middle.astype(np.float64)).astype(ml_dtypes.bfloat16)
    return high, middle, low


def packed(tables):
    rows = np.concatenate([entry.reshape(9, -1) for entry in tables], axis=1).T
    return np.concatenate(list(split3(rows)) + [np.zeros((rows.shape[0], 5), ml_dtypes.bfloat16)], axis=1)


def order_tables(level_index):
    points = [16, 8, 2][level_index]
    common = cheb_nodes(points - 1)
    common_w = quad_weights(points - 1)
    names = ("scaled", "stiff_diag", "quad_w", "interpolate", "face_diag", "living", "prolong")
    table = {name: [] for name in names}
    for degree in range(7, 16):
        local = level_degree(degree, level_index)
        quad = quad_weights(local)
        deriv = derivative(local)
        stiff = deriv.T @ (quad[:, None] * deriv)
        scaled = np.zeros((points, points))
        scaled[: local + 1, : local + 1] = stiff / quad[:, None]
        padded = lambda vector: np.concatenate([vector, np.zeros(points - local - 1)])
        interp = np.zeros((points, points))
        interp[:, : local + 1] = lagrange_table(cheb_nodes(local), common)
        table["scaled"].append(scaled)
        table["stiff_diag"].append(padded(np.diagonal(stiff)))
        table["quad_w"].append(padded(quad))
        table["interpolate"].append(interp)
        table["face_diag"].append((common_w[:, None] * interp**2).sum(axis=0))
        table["living"].append(padded(np.ones(local + 1)))
        if level_index < 2:
            coarse = level_degree(degree, level_index + 1)
            lift = np.zeros((points, [16, 8, 2][level_index + 1]))
            lift[: local + 1, : coarse + 1] = lagrange_table(cheb_nodes(coarse), cheb_nodes(local))
            table["prolong"].append(lift)
    table = {name: np.stack(table[name]) for name in names if table[name]}
    tau = penalty * (points - 1) ** 2
    table["pair"] = tau * np.outer(common_w, common_w)
    table["tau"] = tau
    return table


def flip(table):
    return np.swapaxes(table, 1, 2)


def constants():
    fine, middle, coarse = [order_tables(level_index) for level_index in range(3)]
    vectors = ("quad_w", "face_diag", "living", "stiff_diag")
    matrices = lambda t: [flip(t["scaled"]), t["scaled"], flip(t["interpolate"]), t["interpolate"]]
    c0 = packed(matrices(fine) + [fine[name] for name in vectors])
    c1 = packed(
        matrices(middle)
        + [middle[name] for name in vectors]
        + [fine["prolong"], flip(fine["prolong"]), flip(middle["prolong"])]
    )
    pairs = [np.repeat(t["pair"], SLOTS, axis=1).astype(np.float32) for t in (fine, middle)]
    lift = lagrange_table(cheb_nodes(7), cheb_nodes(15))
    wide = np.kron(lift, np.eye(SLOTS))
    blank = lambda table, rows, cols: np.pad(table, ((0, rows - table.shape[0]), (0, cols - table.shape[1])))
    lifts = []
    for table in (blank(lift, 16, 16), blank(lift.T, 16, 16), wide, wide.T):
        high = table.astype(ml_dtypes.bfloat16)
        lifts += [high, (table - high.astype(np.float64)).astype(ml_dtypes.bfloat16)]
    return lifts, c0, c1, pairs[0], pairs[1], (fine["tau"], middle["tau"]), coarse


def split(values):
    high = values.astype(jnp.bfloat16)
    return high, (values - high.astype(jnp.float32)).astype(jnp.bfloat16)


def dot(left, right):
    return jnp.dot(left, right, preferred_element_type=jnp.float32)


def dot3(values, high, low):
    first, second = split(values)
    return dot(first, high[...]) + dot(second, high[...]) + dot(first, low[...])


def roll(values, shift, axis=-1):
    axis = axis % values.ndim
    return pltpu.roll(values, shift % values.shape[axis], axis)


def lanes_iota(lanes):
    return lax.broadcasted_iota(jnp.int32, (1, lanes), 1)


def rows_iota(rows, lanes):
    return lax.broadcasted_iota(jnp.int32, (rows, lanes), 0)


class Level:
    pass


def resolve(table, place):
    own = lax.broadcasted_iota(jnp.int32, table.shape[1:], 0) == place
    return jnp.sum(jnp.where(own[None], table[...], 0.0), axis=1)


def spread(keep, rows, count, target, low=None):
    keep[: rows.shape[0], : rows.shape[1]] = rows
    lanes = rows.shape[1]
    same = rows_iota(SLOTS, lanes) == (lanes_iota(lanes) & (SLOTS - 1))
    for p in range(count):
        block = jnp.where(same, keep[p : p + 1, :lanes], 0.0)
        high = block.astype(jnp.bfloat16)
        target[p * SLOTS : (p + 1) * SLOTS, :] = high
        if low is not None:
            low[p * SLOTS : (p + 1) * SLOTS, :] = (block - high.astype(jnp.float32)).astype(jnp.bfloat16)


def kernel(taus, coarse, *refs):
    names = iter(refs)
    take = lambda count: [next(names) for _ in range(count)]
    given = take(16)
    (out_ref,) = take(1)
    widths_ref, orders_ref, factors_ref, c0_ref, c1_ref, pair0_ref, pair1_ref, res_ref = take(8)
    lift_refs = take(8)
    levels = []
    for index in range(2):
        lv = Level()
        lv.n = [16, 8][index]
        lv.lanes = lv.n * SLOTS
        (lv.T, lv.TT, lv.TI, lv.TIT) = take(4)
        (lv.RS, lv.RSl, lv.RI, lv.RIl, lv.RIT, lv.RITl, lv.PP, lv.PPT) = take(8)
        (lv.IL, lv.DINV, lv.WWW, lv.R, lv.X, lv.V, lv.OUT) = take(7)
        (lv.H, lv.Q, lv.G, lv.RZ, lv.U, lv.Y, lv.SB, lv.RB) = take(8)
        lv.pair = [pair0_ref, pair1_ref][index]
        levels.append(lv)
    TP, TPT, PT1, RP, RPl, RPT, RPTl, RP1, RP1l, RPT1, RPT1l, A8, C8, SBF, RBF, SBR, RBR, KEEP, XIN = take(19)
    send_sem, recv_sem, load_sem, wide_send, wide_recv = take(5)
    landings = [widths_ref, orders_ref, factors_ref, c0_ref, c1_ref, pair0_ref, pair1_ref, res_ref] + lift_refs
    loads = [pltpu.make_async_copy(*pair, load_sem.at[i]) for i, pair in enumerate(zip(given, landings))]
    for load in loads:
        load.start()

    dom, grp = lax.axis_index("dom"), lax.axis_index("grp")
    n_dom, n_grp = lax.axis_size("dom"), lax.axis_size("grp")
    targets = [
        {"dom": lax.rem(dom + n_dom - 1, n_dom)},
        {"dom": lax.rem(dom + 1, n_dom)},
        {"grp": lax.rem(grp + n_grp - 1, n_grp)},
        {"grp": lax.rem(grp + 1, n_grp)},
    ]
    barrier = pltpu.get_barrier_semaphore()
    around = [
        {"dom": lax.rem(dom + n_dom + dx, n_dom), "grp": lax.rem(grp + n_grp + dg, n_grp)} for dx, dg in AROUND
    ]
    for target in around:
        pl.semaphore_signal(barrier, inc=1, device_id=target, device_id_type=MESH)

    lane = lanes_iota(16 * SLOTS)
    slot = lane & (SLOTS - 1)
    layer = slot >> 2
    row = slot & 3
    for load in loads[:3]:
        load.wait()
    width = jnp.int32(0)
    for g in range(4):
        width = jnp.where(grp == g, widths_ref[g], width)
    order = jnp.full(lane.shape, 7, jnp.int32)
    factor = [jnp.full(lane.shape, 1.0, jnp.float32) for _ in range(4)]
    for r in range(4):
        for t in range(3):
            here = slot == t * 4 + r
            order = jnp.where(here, orders_ref[t, 0, r], order)
            for c in range(4):
                factor[c] = jnp.where(here, factors_ref[0, t, r, c], factor[c])
    alive = layer < width
    mask = jnp.where(alive, 1.0, 0.0)
    at_first = layer == 0
    at_last = layer == width - 1
    line = rows_iota(32, 16 * SLOTS)
    line = jnp.where(line < 9, line, jnp.where(line < 18, line - 9, jnp.where(line < 27, line - 18, -1)))
    onehot = jnp.where(line == order - 7, 1.0, 0.0).astype(jnp.bfloat16)

    def tables(lv, index, which):
        refs = (lv.TI, lv.TIT, lv.T, lv.TT)
        source = [c0_ref, c1_ref][index]
        size = lv.n * lv.n
        at = (2, 3, 0, 1)[which] * size
        refs[which][...] = dot(source[at : at + size, :], lv.hot).reshape(lv.n, lv.n, lv.lanes)

    def setup_first(lv, index):
        n, lanes = lv.n, lv.lanes
        lv.place = lane[:, :lanes] >> 4
        lv.last = [order, order >> 1][index][:, :lanes]
        lv.f = [entry[:, :lanes] for entry in factor]
        lv.cm = lv.f[3] * mass_weight
        lv.at_first, lv.at_last = at_first[:, :lanes], at_last[:, :lanes]
        lv.row = row[:, :lanes]
        lv.last_range = [range(7, 16), range(3, 8)][index]
        lv.hot = onehot[:, :lanes]
        tables(lv, index, 0)
        at = 4 * n * n
        vectors = dot([c0_ref, c1_ref][index][at : at + 4 * n, :], lv.hot)
        quad, face, live, stiff = [vectors[i * n : (i + 1) * n] for i in range(4)]
        inter = resolve(lv.TI, lv.place)
        lv.IL[...] = inter
        spread(KEEP, inter, n, lv.RI, lv.RIl)
        points = rows_iota(n, lanes)
        lv.FM = jnp.where(points == 0, 1.0, 0.0)
        lv.LM = jnp.where(points == lv.last, 1.0, 0.0)
        lv.same = rows_iota(SLOTS, lanes) == (lane[:, :lanes] & (SLOTS - 1))
        for p in range(n):
            rows = slice(p * SLOTS, (p + 1) * SLOTS)
            lv.PP[rows, :lanes] = one(lv.same) if p == 0 else jnp.zeros((SLOTS, lanes), jnp.bfloat16)
            lv.PP[rows, lanes:] = one(lv.same & (lv.last == p))
        pick = lambda table: jnp.sum(jnp.where(points == lv.place, table, 0.0), axis=0, keepdims=True)
        w_i, face_i, live_i, stiff_i = pick(quad), pick(face), pick(live) * mask[:, :lanes], pick(stiff)
        ends = lv.FM + lv.LM
        ends_i = pick(ends)
        f0, f1, f2, _ = lv.f
        for j in range(n):
            one_row = lambda table: table[j : j + 1, :]
            w_j, face_j, live_j, stiff_j, ends_j = [one_row(t) for t in (quad, face, live, stiff, ends)]
            www = (w_i * w_j) * quad
            diagonal = (
                (f0 * stiff_i * w_j) * quad
                + (f1 * w_i * stiff_j) * quad
                + (f2 * w_i * w_j) * stiff
                + lv.cm * www
                + taus[index] * ((ends_j * face_i + face_j * ends_i) * face + (face_j * face_i) * ends)
            )
            node_live = (live_j * live_i) * live
            lv.WWW[j] = www
            lv.DINV[j] = node_live / (diagonal + 1.0 - node_live)
            if index == 0:
                lv.X[j] = node_live

    def setup_return(lv, index):
        n, lanes = lv.n, lv.lanes
        tables(lv, index, 1)
        spread(KEEP, resolve(lv.TIT, lv.place), n, lv.RIT, lv.RITl)
        for p in range(n):
            lv.PPT[p * SLOTS : (p + 1) * SLOTS, :] = one(lv.same & (lv.place == 0))
            lv.PPT[lanes + p * SLOTS : lanes + (p + 1) * SLOTS, :] = one(lv.same & (lv.place == lv.last))

    def setup_volume(lv, index):
        tables(lv, index, 2)
        tables(lv, index, 3)
        spread(KEEP, resolve(lv.T, lv.place) * lv.f[0], lv.n, lv.RS, lv.RSl)

    def setup_between():
        at = 4 * 64 + 4 * 8
        TP[...] = dot(c1_ref[at : at + 128, :], middle.hot).reshape(16, 8, 128)
        TPT[...] = dot(c1_ref[at + 128 : at + 256, :], middle.hot).reshape(8, 16, 128)
        spread(KEEP, resolve(TP, middle.place), 16, RP, RPl)

    def setup_coarse():
        at = 4 * 64 + 4 * 8 + 256
        PT1[...] = dot(c1_ref[at : at + 16, :], middle.hot).reshape(2, 8, 128)
        place1 = middle.place
        wide = jnp.concatenate([TPT[...], TPT[...]], axis=2)
        spread(KEEP, resolve(wide, fine.place), 8, RPT, RPTl)
        spread(KEEP, jnp.where(place1 == 0, PT1[0], jnp.where(place1 == 1, PT1[1], 0.0)), 8, RP1, RP1l)
        RPT1[...] = jnp.zeros(RPT1.shape, jnp.bfloat16)
        RPT1l[...] = jnp.zeros(RPT1l.shape, jnp.bfloat16)
        spread(KEEP, resolve(PT1, place1), 2, RPT1, RPT1l)

    def after_second_send():
        for load in loads[8:]:
            load.wait()
        setup_first(middle, 1)
        setup_return(middle, 1)
        setup_between()

    one = lambda cond: jnp.where(cond, 1.0, 0.0).astype(jnp.bfloat16)
    fine, middle = levels
    for load in loads[3:7]:
        load.wait()
    setup_first(fine, 0)

    loads[7].wait()
    for i in range(16):
        for t in range(3):
            XIN[i * SLOTS + t * 4 : i * SLOTS + t * 4 + 4, :] = res_ref[0, t, :, i * 256 : (i + 1) * 256]
        XIN[i * SLOTS + 12 : i * SLOTS + 16, :] = jnp.zeros((4, 256), jnp.float32)
    fine.R[...] = jnp.transpose(XIN[...]).reshape(16, 16, 256) * fine.X[...]

    pl.semaphore_wait(barrier, len(AROUND))
    pending = []
    lane1 = lane[:, :128]
    group1 = lane1 >> 5

    def gather_start(which, value, reach):
        source, landing = [(SBF, RBF), (SBR, RBR)][which]
        source[...] = value
        copies = {}
        for q, (dx, dg) in enumerate(AROUND):
            if abs(dx) + abs(dg) > reach:
                continue
            where = which * len(AROUND) + q
            copies[q] = pltpu.make_async_remote_copy(
                src_ref=source,
                dst_ref=landing.at[q],
                send_sem=wide_send.at[where],
                recv_sem=wide_recv.at[where],
                device_id=around[q],
                device_id_type=MESH,
            )
            copies[q].start()
            pending.append(copies[q])
        return copies

    def gather_end(which, value, reach, copies):
        landing = [RBF, RBR][which]
        for q in copies:
            copies[q].wait_recv()
        columns = []
        for column in range(-reach, reach + 1):
            total = value if column == 0 else None
            for q in copies:
                if -AROUND[q][0] == column:
                    total = landing[q] if total is None else total + landing[q]
            columns.append(total)
        return jnp.stack(columns)

    own_group = group1 == grp
    own_factors = jnp.concatenate(
        [jnp.where(own_group, entry[:, :128], 0.0) for entry in factor] + [jnp.zeros((4, 128), jnp.float32)], axis=0
    )
    factor_copies = {}

    def send(number, direction, value, source, landing):
        source[...] = value
        where = number * 4 + direction
        copy = pltpu.make_async_remote_copy(
            src_ref=source,
            dst_ref=landing,
            send_sem=send_sem.at[where],
            recv_sem=recv_sem.at[where],
            device_id=targets[direction],
            device_id_type=MESH,
        )
        copy.start()
        pending.append(copy)
        return copy

    def towards_first(value, last):
        value = jnp.where(last, value, 0.0)
        return value + roll(value, -4) + roll(value, -8)

    def towards_last(value):
        return jnp.where(width == 1, value, jnp.where(width == 2, roll(value, 4), roll(value, 8)))

    def contract(table, source, first, count):
        total = None
        for k in range(table.shape[0]):
            term = table[k][None] * source[first : first + count, k : k + 1, :]
            total = term if total is None else total + term
        return total

    def give_back(lv):
        n, lanes = lv.n, lv.lanes
        back = contract(lv.TIT, lv.G, 0, 4)
        for f in range(2):
            for j in range(n):
                lv.Y[j, :, f * lanes : (f + 1) * lanes] = lv.IL[j : j + 1, :] * back[f]
        lv.RZ[...] = dot3(back[2:4].reshape(2 * n, lanes), lv.RIT, lv.RITl).reshape(2, n, lanes)
        first, second = split(lv.Y[...].reshape(n * n, 2 * lanes))
        x_back = (dot(first, lv.PPT[...]) + dot(second, lv.PPT[...])).reshape(n, n, lanes)
        return x_back, lambda j: lv.FM * lv.RZ[0, j : j + 1, :] + lv.LM * lv.RZ[1, j : j + 1, :]

    def apply_level(lv, slot_of, number, consume, meanwhile=None, near=None, defer=False, lead=False):
        n, lanes = lv.n, lv.lanes
        flat = lv.V[...].reshape(n * n, lanes)
        high, low = split(flat)
        lv.U[...] = (dot(high, lv.PP[...]) + dot(low, lv.PP[...])).reshape(n, n, 2 * lanes)
        y0, z0 = lv.V[0], lv.V[:, 0, :]
        y1, z1 = jnp.zeros_like(y0), jnp.zeros_like(z0)
        for p in lv.last_range:
            here = lv.last == p
            y1 = jnp.where(here, lv.V[p], y1)
            z1 = jnp.where(here, lv.V[:, p, :], z1)
        turned = dot3(jnp.concatenate([z0, z1, y0, y1], axis=0), lv.RI, lv.RIl)
        lv.H[2:6] = turned.reshape(4, n, lanes)
        for f in range(2):
            total = None
            for j in range(n):
                term = lv.IL[j : j + 1, :] * lv.U[j, :, f * lanes : (f + 1) * lanes]
                total = term if total is None else total + term
            lv.H[f] = total
        lv.Q[...] = contract(lv.TI, lv.H, 0, 6)
        copies = []
        if near is None:
            outgoing = [lv.Q[0], lv.Q[1], lv.Q[2], towards_first(lv.Q[3], lv.at_last)]
            copies = [
                send(number, d, outgoing[d], lv.SB.at[slot_of, d], lv.RB.at[slot_of, d]) for d in range(4)
            ]
        if lead:
            return copies
        if meanwhile is not None:
            meanwhile()
        lv.G[4] = lv.pair[...] * (lv.Q[4] - jnp.where(lv.row > 0, roll(lv.Q[5], 1), 0.0))
        lv.G[5] = lv.pair[...] * (lv.Q[5] - jnp.where(lv.row < 3, roll(lv.Q[4], -1), 0.0))
        back = contract(lv.TIT, lv.G, 4, 2).reshape(2 * n, lanes)
        back = dot3(back, lv.RIT, lv.RITl)
        y_back = [back[:n], back[n:]]
        lv.OUT[...] = (
            dot(high, lv.RS[...]) + dot(low, lv.RS[...]) + dot(high, lv.RSl[...])
        ).reshape(n, n, lanes)
        size = 4 if n == 16 else 8
        for a in range(0, n, size):
            block = slice(a, a + size)
            along_j, along_k = None, None
            for j in range(n):
                term = lv.TT[block, j : j + 1, :] * lv.V[j][None]
                along_j = term if along_j is None else along_j + term
            for k in range(n):
                term = lv.T[k][None] * lv.V[block, k : k + 1, :]
                along_k = term if along_k is None else along_k + term
            lv.OUT[block] = lv.WWW[block] * (
                lv.OUT[block] + lv.f[1] * along_j + lv.f[2] * along_k + lv.cm * lv.V[block]
            )
        lv.OUT[0] = lv.OUT[0] + y_back[0]
        for p in lv.last_range:
            lv.OUT[p] = lv.OUT[p] + jnp.where(lv.last == p, y_back[1], 0.0)
        if defer:
            lv.deferred, near = copies, [0.0] * 4
        else:
            for copy in copies:
                copy.wait_recv()
        pair = lv.pair[...]
        landed = lambda d: lv.RB[slot_of, d]
        if near is None:
            x_low, x_high, z_low, z_high = landed(1), landed(0), landed(3), towards_last(landed(2))
        else:
            x_low, x_high, z_low, z_high = near() if callable(near) else near
        lv.G[0] = pair * (lv.Q[0] - x_low)
        lv.G[1] = pair * (lv.Q[1] - x_high)
        lv.G[2] = pair * (lv.Q[2] - jnp.where(lv.at_first, z_low, roll(lv.Q[3], 4)))
        lv.G[3] = pair * (lv.Q[3] - jnp.where(lv.at_last, z_high, roll(lv.Q[2], -4)))
        x_back, z_back = give_back(lv)
        for j in range(n):
            consume(j, lv.OUT[j] + x_back[j] + z_back(j))

    centre = 0.5 * (cheb_high + cheb_low)
    radius = 0.5 * (cheb_high - cheb_low)
    rho_first = radius / centre
    rho_next = 1.0 / (2.0 * centre / radius - rho_first)
    keep_d = 1.0 + rho_next * rho_first
    take_e = 2.0 * rho_next / radius

    def first_step(lv):
        lv.V[...] = lv.DINV[...] * lv.R[...] * (1.0 / centre)

    def end_pre(lv):
        def consume(j, applied):
            lv.V[j] = keep_d * lv.V[j] + take_e * lv.DINV[j] * (lv.R[j] - applied)

        return consume

    def remainder(lv):
        def consume(j, applied):
            lv.OUT[j] = lv.R[j] - applied

        return consume

    def begin_post(lv):
        def consume(j, applied):
            rest = lv.R[j] - applied
            lv.R[j] = rest
            lv.X[j] = lv.V[j]
            lv.V[j] = lv.DINV[j] * rest * (1.0 / centre)

        return consume

    def end_post(lv):
        def consume(j, applied):
            lv.V[j] = lv.X[j] + keep_d * lv.V[j] + take_e * lv.DINV[j] * (lv.R[j] - applied)

        return consume

    def after_first_send():
        setup_return(fine, 0)
        setup_volume(fine, 0)

    def after_third_send():
        factor_copies.update(gather_start(0, own_factors, REACH - 1))
        setup_volume(middle, 1)
        setup_coarse()

    first_step(fine)
    apply_level(fine, 0, 0, end_pre(fine), after_first_send)
    apply_level(fine, 1, 1, remainder(fine), after_second_send, defer=True)

    lanes_down = dot3(fine.OUT[...].reshape(256, 256), RP, RPl).reshape(16, 16, 128)
    total = None
    for j in range(16):
        term = TPT[:, j : j + 1, :] * lanes_down[j][None]
        total = term if total is None else total + term
    A8[...] = total
    middle.R[...] = contract(TP, A8, 0, 8)

    def on_rows(high, low, values):
        first, second = split(values)
        return dot(high[...], first) + dot(high[...], second) + dot(low[...], first)

    for copy in fine.deferred:
        copy.wait_recv()
    z_low = jnp.where(fine.at_first, fine.RB[1, 3], 0.0)
    z_high = jnp.where(fine.at_last, towards_last(fine.RB[1, 2]), 0.0)
    near_faces = [fine.pair[...] * value for value in (fine.RB[1, 1], fine.RB[1, 0], z_low, z_high)]
    near_faces = on_rows(lift_refs[2], lift_refs[3], jnp.concatenate(near_faces, axis=1))[:8]
    near_faces = jnp.concatenate([near_faces[:, f * 256 : (f + 1) * 256] for f in range(4)], axis=0)
    middle.G[0:4] = dot3(near_faces, lift_refs[4], lift_refs[5]).reshape(4, 8, 128)
    x_back, z_back = give_back(middle)
    for j in range(8):
        middle.R[j] = middle.R[j] + x_back[j] + z_back(j)
    first_step(middle)
    apply_level(middle, 0, 2, end_pre(middle), after_third_send)
    apply_level(middle, 1, 3, remainder(middle), defer=True)

    parts = []
    for a in range(2):
        total = None
        for j in range(8):
            term = PT1[a, j : j + 1, :] * middle.OUT[j]
            total = term if total is None else total + term
        for b in range(2):
            parts.append(jnp.sum(PT1[b] * total, axis=0, keepdims=True))
    coarse_r = dot3(jnp.concatenate(parts + [jnp.zeros((4, 128), jnp.float32)], axis=0), RP1, RP1l)

    def placed(value):
        total = value
        for g in range(1, 4):
            total = jnp.where(grp == g, roll(value, 32 * g), total)
        return total

    def unplaced(value):
        total = value
        for g in range(1, 4):
            total = jnp.where(grp == g, roll(value, -32 * g), total)
        return jnp.where(lane1 < 32, total, 0.0)

    points = cheb_nodes(7)
    line2 = rows_iota(8, 128)
    along_lane, along_row = jnp.zeros((1, 128), jnp.float32), jnp.zeros((8, 128), jnp.float32)
    for b in range(8):
        along_lane = jnp.where((lane1 >> 4) == b, float(points[b]), along_lane)
        along_row = jnp.where(line2 == b, float(points[b]), along_row)
    lane_ends = [0.5 - 0.5 * along_lane, 0.5 + 0.5 * along_lane]
    row_ends = [0.5 - 0.5 * along_row, 0.5 + 0.5 * along_row]

    def row_sums(face):
        weighted = middle.pair[...] * middle.Q[face]
        return [jnp.sum(row_ends[end] * weighted, axis=0, keepdims=True) for end in range(2)]

    def group_sums(rows):
        total = jnp.concatenate(rows, axis=0)
        for shift in (16, 32, 64):
            total = total + roll(total, shift)
        return total

    def two_groups(low, high):
        return jnp.where(lane1 < 16, low, jnp.where(lane1 < 32, high, 0.0))

    x_rows = [lane_ends[j] * row_sums(f)[k] for f in range(2) for j in range(2) for k in range(2)]
    x_sums = group_sums(x_rows)
    z_rows = [lane_ends[i] * row_sums(2 + k)[j] for i in range(2) for j in range(2) for k in range(2)]
    z_sums = group_sums(z_rows)
    x_given = two_groups(x_sums[:4], x_sums[4:])
    z_given = two_groups(z_sums[:4], z_sums[4:])
    own_r = placed(jnp.concatenate([coarse_r[:4], x_given, z_given, jnp.zeros((4, 128), jnp.float32)], axis=0))
    r_copies = gather_start(1, own_r, REACH)

    fs = gather_end(0, own_factors, REACH - 1, factor_copies)
    f0, f1, f2, f3 = [fs[:, c : c + 1, :] for c in range(4)]
    low_i = ((lane1 >> 4) & 1) == 0
    low_j = line2 < 2
    low_k = (line2 & 1) == 0
    row2, layer2 = lane1 & 3, (lane1 >> 2) & 3
    width2, before2 = jnp.zeros((1, 128), jnp.int32), jnp.zeros((1, 128), jnp.int32)
    for g in range(4):
        width2 = jnp.where(group1 == g, widths_ref[g], width2)
        before2 = jnp.where(group1 == (g + 1) % 4, widths_ref[g], before2)
    s00, s01 = float(coarse["scaled"][0, 0, 0]), float(coarse["scaled"][0, 0, 1])
    w0 = float(coarse["quad_w"][0, 0])
    www = w0**3
    pair2 = float(coarse["pair"][0, 0])
    centre_coeff = www * (s00 * (f0 + f1 + f2) + mass_weight * f3) + 3.0 * pair2
    live2 = jnp.where((layer2 < width2) & (line2 < 4), 1.0, 0.0)[None]
    dinv2 = live2 / (centre_coeff + 1.0 - live2)
    f0, f1, f2 = [(www * s01) * entry for entry in (f0, f1, f2)]

    def sideways(value, shift):
        return roll(value.reshape(-1, 128), shift).reshape(value.shape)

    def next_layer(value):
        across = jnp.where(
            width2 == 1, sideways(value, -32), jnp.where(width2 == 2, sideways(value, -28), sideways(value, -24))
        )
        return jnp.where(layer2 < width2 - 1, sideways(value, -4), across)

    def last_layer(value):
        across = jnp.where(
            before2 == 1, sideways(value, 32), jnp.where(before2 == 2, sideways(value, 28), sideways(value, 24))
        )
        return jnp.where(layer2 > 0, sideways(value, 4), across)

    def other_k(value):
        return jnp.where(low_k, roll(value, -1, 1), roll(value, 1, 1))

    def coarse_apply(value, skip):
        mid = value[1:-1]
        part = slice(skip, COLUMNS - 2 - skip)
        flip_i = jnp.where(low_i, sideways(mid, -16), sideways(mid, 16))
        flip_j = jnp.where(low_j, roll(mid, -2, 1), roll(mid, 2, 1))
        flip_k = other_k(mid)
        near_x = jnp.where(low_i, sideways(value[:-2], -16), sideways(value[2:], 16))
        near_y = jnp.where(
            low_j,
            jnp.where(row2 > 0, sideways(flip_j, 1), 0.0),
            jnp.where(row2 < 3, sideways(flip_j, -1), 0.0),
        )
        near_z = jnp.where(low_k, last_layer(flip_k), next_layer(flip_k))
        return (
            centre_coeff[part] * mid
            + (f0[part] * flip_i + f1[part] * flip_j + f2[part] * flip_k)
            - pair2 * (near_x + near_y + near_z)
        )

    both = gather_end(1, own_r, REACH, r_copies)
    upper, lower = both[:, :8], both[:, 8:]
    given = roll(upper, 4, 1)
    rs = upper[1:-1] + jnp.where(low_i, sideways(given[:-2], -16), sideways(given[2:], 16))
    given = other_k(lower[1:-1])
    rs = rs + jnp.where(
        low_k,
        jnp.where(layer2 == 0, last_layer(given), 0.0),
        jnp.where(layer2 == width2 - 1, next_layer(given), 0.0),
    )
    d = dinv2 * rs * (1.0 / centre)
    xs = keep_d * d[1:-1] + take_e * dinv2[1:-1] * (rs[1:-1] - coarse_apply(d, 1))
    rest = rs[2:-2] - coarse_apply(xs, 2)
    d = dinv2[2:-2] * rest * (1.0 / centre)
    xs = xs[2:-2] + keep_d * d[1:-1] + take_e * dinv2[3:-3] * (rest[1:-1] - coarse_apply(d, 3))
    x = unplaced(xs[1])

    def all_lanes(value, end):
        value = jnp.where(lane1 < 16, roll(value, -16) if end else value, 0.0)
        value = value + roll(value, 16)
        value = value + roll(value, 32)
        return value + roll(value, 64)

    def x_trace(column, end):
        face = all_lanes(unplaced(column), end)
        total = 0.0
        for k in range(2):
            line = lane_ends[0] * face[k : k + 1, :] + lane_ends[1] * face[2 + k : 3 + k, :]
            total = total + row_ends[k] * line
        return total

    def z_trace(column, k):
        column = unplaced(column)
        face = lane_ends[0] * all_lanes(column, 0) + lane_ends[1] * all_lanes(column, 1)
        return row_ends[0] * face[k : k + 1, :] + row_ends[1] * face[2 + k : 3 + k, :]

    turned = other_k(xs[1:2])
    correction_traces = [
        x_trace(xs[0], 1),
        x_trace(xs[2], 0),
        z_trace(last_layer(turned)[0], 0),
        z_trace(next_layer(turned)[0], 1),
    ]
    for copy in middle.deferred:
        copy.wait_recv()
    before = [middle.RB[1, 1], middle.RB[1, 0], middle.RB[1, 3], towards_last(middle.RB[1, 2])]
    middle_near = [old + new for old, new in zip(before, correction_traces)]

    lifted = dot3(x, RPT1, RPT1l)
    columns = []
    for a in range(2):
        columns.append(PT1[0] * lifted[2 * a : 2 * a + 1, :] + PT1[1] * lifted[2 * a + 1 : 2 * a + 2, :])
    for j in range(8):
        middle.V[j] = middle.V[j] + PT1[0, j : j + 1, :] * columns[0] + PT1[1, j : j + 1, :] * columns[1]
    apply_level(middle, 2, None, begin_post(middle), near=middle_near)
    apply_level(middle, 3, 8, end_post(middle))

    lead = apply_level(middle, 4, 7, None, lead=True)

    C8[...] = contract(TPT, middle.V, 0, 8)
    for j0 in (0, 8):
        total = None
        for a in range(8):
            term = TP[j0 : j0 + 8, a : a + 1, :] * C8[a][None]
            total = term if total is None else total + term
        fine.U[j0 : j0 + 8, :, :128] = total
    lifted = dot3(fine.U[:, :, :128].reshape(256, 128), RPT, RPTl)
    fine.V[...] = fine.V[...] + lifted.reshape(16, 16, 256)

    def fine_near():
        for copy in lead:
            copy.wait_recv()
        faces = [middle.RB[4, 1], middle.RB[4, 0], middle.RB[4, 3], towards_last(middle.RB[4, 2])]
        wide = dot3(jnp.concatenate(faces, axis=0), lift_refs[6], lift_refs[7])
        wide = jnp.concatenate([wide[f * 8 : (f + 1) * 8] for f in range(4)], axis=1)
        wide = on_rows(lift_refs[0], lift_refs[1], jnp.concatenate([wide, jnp.zeros_like(wide)], axis=0))
        before = [fine.RB[1, 1], fine.RB[1, 0], fine.RB[1, 3], towards_last(fine.RB[1, 2])]
        return [old + wide[:, f * 256 : (f + 1) * 256] for f, old in enumerate(before)]

    apply_level(fine, 2, None, begin_post(fine), near=fine_near)
    apply_level(fine, 3, 10, end_post(fine))

    XIN[...] = jnp.transpose(fine.V[...].reshape(256, 256))
    for i in range(16):
        for t in range(3):
            out_ref[0, t, :, i * 256 : (i + 1) * 256] = XIN[i * SLOTS + t * 4 : i * SLOTS + t * 4 + 4, :]
    for copy in pending:
        copy.wait_send()


def scratch(given):
    f32, b16 = jnp.float32, jnp.bfloat16
    shapes = []
    for n in (16, 8):
        lanes = n * SLOTS
        shapes += [((n, n, lanes), f32)] * 4
        shapes += [((lanes, lanes), b16)] * 6 + [((lanes, 2 * lanes), b16), ((2 * lanes, lanes), b16)]
        shapes += [((n, lanes), f32)] + [((n, n, lanes), f32)] * 6
        shapes += [((6, n, lanes), f32)] * 3 + [((2, n, lanes), f32)]
        shapes += [((n, n, 2 * lanes), f32)] * 2 + [((5, 4, n, lanes), f32)] * 2
    shapes += [((16, 8, 128), f32), ((8, 16, 128), f32), ((2, 8, 128), f32)]
    shapes += [((256, 128), b16)] * 2 + [((128, 256), b16)] * 2 + [((128, 128), b16)] * 4
    shapes += [((8, 16, 128), f32)] * 2 + [((8, 128), f32), ((len(AROUND), 8, 128), f32)]
    shapes += [((16, 128), f32), ((len(AROUND), 16, 128), f32)]
    shapes += [((16, 256), f32), ((256, 256), f32)]
    semaphores = [pltpu.SemaphoreType.DMA((44,))] * 2 + [pltpu.SemaphoreType.DMA((16,))]
    semaphores += [pltpu.SemaphoreType.DMA((2 * len(AROUND),))] * 2
    landings = [pltpu.SMEM(x.shape, x.dtype) for x in given[:3]] + [pltpu.VMEM(x.shape, x.dtype) for x in given[3:]]
    return landings + [pltpu.VMEM(shape, dtype) for shape, dtype in shapes] + semaphores


def shards(residual, orders, factors, widths):
    lifts, c0, c1, pair0, pair1, taus, coarse = constants()
    given = [
        widths,
        jnp.transpose(orders, (2, 0, 1)),
        jnp.transpose(factors, (0, 2, 1, 3)),
        jnp.asarray(c0),
        jnp.asarray(c1),
        jnp.asarray(pair0),
        jnp.asarray(pair1),
        jnp.transpose(residual, (0, 2, 1, 3)),
    ] + [jnp.asarray(table) for table in lifts]
    out = pl.pallas_call(
        functools.partial(kernel, taus, coarse),
        out_shape=jax.ShapeDtypeStruct((1, 3, 4, 4096), jnp.float32),
        in_specs=[pl.BlockSpec(memory_space=pltpu.HBM)] * 16,
        out_specs=pl.BlockSpec(memory_space=pltpu.VMEM),
        scratch_shapes=scratch(given),
        compiler_params=pltpu.CompilerParams(
            collective_id=0, has_side_effects=True, vmem_limit_bytes=62 * 1024 * 1024
        ),
    )(*given)
    return jnp.transpose(out, (0, 2, 1, 3))


def solution(mesh):
    return jax.shard_map(
        shards,
        mesh=mesh,
        in_specs=(
            P("dom", None, "grp", None),
            P("dom", None, "grp"),
            P("dom", None, "grp", None),
            P(),
        ),
        out_specs=P("dom", None, "grp", None),
        check_vma=False,
    )
```
